32 devices in a mesh: dp: 4 (over x, core), fsdp: 8 (over z, y).
Axes of the slice: x: 2, y: 2, z: 4, core: 2. Of those that a mesh axis runs over, the one named last changes fastest.
Arguments:
- tokens: bfloat16 [16384, 768], P(('dp', 'fsdp')), may hold values from -6 to 6
- mask: int32 [16384], P(('dp', 'fsdp')), may hold values from 0 to 1, as said below
- cotangent: bfloat16 [16384, 768], P(('dp', 'fsdp')), may hold values from -6 to 6
- mask_embed: bfloat16 [768], P('fsdp'), may hold values from -6 to 6
- attn_in: bfloat16 [2, 768, 2304], P(None, 'fsdp'), may hold values from -0.21875 to 0.21875
- attn_out: bfloat16 [2, 768, 768], P(None, 'fsdp'), may hold values from -0.875 to 0.875
- fc_in: bfloat16 [2, 768, 3072], P(None, 'fsdp'), may hold values from -0.21875 to 0.21875
- fc_out: bfloat16 [2, 3072, 768], P(None, 'fsdp'), may hold values from -0.109375 to 0.109375
- gains: bfloat16 [2, 2, 768], P(None, None, 'fsdp'), may hold values from 0.099609375 to 1.8984375
- biases: bfloat16 [2, 6, 768], P(None, None, 'fsdp'), may hold values from -3 to 3
- fc_bias: bfloat16 [2, 3072], P(None, 'fsdp'), may hold values from -3 to 3
Outputs:
- activations: float32 [16384, 768], P(('dp', 'fsdp'))
- input_grad: float32 [16384, 768], P(('dp', 'fsdp'))
- mask_embed_grad: float32 [768], P('fsdp')
- attn_in_grad: float32 [2, 768, 2304], P(None, 'fsdp')
- attn_out_grad: float32 [2, 768, 768], P(None, 'fsdp')
- fc_in_grad: float32 [2, 768, 3072], P(None, 'fsdp')
- fc_out_grad: float32 [2, 3072, 768], P(None, 'fsdp')
- gains_grad: float32 [2, 2, 768], P(None, None, 'fsdp')
- biases_grad: float32 [2, 6, 768], P(None, None, 'fsdp')
- fc_bias_grad: float32 [2, 3072], P(None, 'fsdp')
The draws below stay inside these ranges and needn't reach their ends.
Inputs may be any that keep to these rules, and one draw needn't show every extreme that they name: `mask`: each clip of 512 consecutive patches has exactly 400 ones.
All inputs are finite; a program needn't handle non-finite values.
Results may differ from the reference program's by a relative error of at most 0.015.
Values may be sent and summed in bfloat16 or wider, within the bound.
A program may use at most 256 MiB of HBM per device.

```python
import jax
import jax.numpy as jnp
from jax import lax

D = 768
HEADS = 12
FF = 3072
SEQ = 512
MASKED = 400
LAYERS = 2
TOKENS = 16384


def draw_mask(key, part):
    key = jax.random.fold_in(key, 7)
    keys = jax.random.split(key, TOKENS // SEQ)
    ranks = jax.vmap(lambda one: jax.random.permutation(one, SEQ))(keys)
    return (ranks < MASKED).astype(jnp.int32).reshape(TOKENS)


def levels(stream_key, shape, shards, low, largest):
    factor_of = 1.0
    for dim, blocks in shards:
        draws = jax.random.uniform(jax.random.fold_in(jax.random.fold_in(stream_key, 6), dim), (blocks,), jnp.float32, low / len(shards), largest / len(shards))
        factor_of = factor_of * jnp.repeat(jnp.exp(draws), shape[dim] // blocks).reshape((-1,) + (1,) * (len(shape) - 1 - dim))
    return factor_of


def centred(rng, extent, scale, limit, cuts=(), held_as=jnp.bfloat16):
    factor_of = levels(rng, extent, cuts, -0.22, 0.18) if cuts else 1.0
    values = jax.random.normal(rng, extent, jnp.float32) * scale * factor_of
    return jnp.minimum(jnp.maximum(values, -limit), limit).astype(held_as)


def setup_inputs(seed: int = 0) -> dict:
    seeds = jax.random.split(jax.random.key(seed), 12)
    tokens = centred(seeds[0], (TOKENS, D), 1.0, 6.0, ((0, 32),))
    mask = draw_mask(jax.random.fold_in(seeds[11], 71), 0)
    cotangent = centred(seeds[2], (TOKENS, D), 1.0, 6.0, ((0, 32),))
    mask_embed = centred(seeds[3], (D,), 1.0, 6.0, ((0, 8),))
    attn_in = centred(seeds[4], (LAYERS, D, 3 * D), D ** -0.5, 0.21875, ((1, 8),))
    attn_out = centred(seeds[5], (LAYERS, D, D), (D // 16) ** -0.5, 0.875, ((1, 8),))
    fc_in = centred(seeds[6], (LAYERS, D, FF), D ** -0.5, 0.21875, ((1, 8),))
    fc_out = centred(seeds[7], (LAYERS, FF, D), FF ** -0.5, 0.109375, ((1, 8),))
    gains = jnp.clip(1.0 + 0.18 * jax.random.normal(seeds[8], (LAYERS, 2, D), jnp.float32), 0.099609375, 1.8984375).astype(jnp.bfloat16)
    biases = centred(seeds[9], (LAYERS, 6, D), 0.5, 3.0, ((2, 8),))
    fc_bias = centred(seeds[10], (LAYERS, FF), 0.5, 3.0, ((1, 8),))
    return dict(tokens=tokens, mask=mask, cotangent=cotangent, mask_embed=mask_embed, attn_in=attn_in, attn_out=attn_out, fc_in=fc_in, fc_out=fc_out, gains=gains, biases=biases, fc_bias=fc_bias)


eps = 1e-06
HIGH = lax.Precision.HIGHEST

@jax.custom_vjp
def low(v):
    return lax.optimization_barrier(v.astype(jnp.bfloat16)).astype(jnp.float32)

@jax.custom_vjp
def low_back(v):
    return v

def low_keep(v):
    return (low(v), None)

def low_pass(kept, grad):
    return (grad,)

def back_keep(v):
    return (v, None)

def back_low(kept, grad):
    return (low(grad),)
low.defvjp(low_keep, low_pass)
low_back.defvjp(back_keep, back_low)

def norm_rows(values, gain, bias):
    center = values - lax.optimization_barrier(jnp.mean(values, axis=-1, keepdims=True))
    spread = lax.optimization_barrier(jnp.mean(center * center, axis=-1, keepdims=True))
    return center * lax.rsqrt(spread + eps) * gain + bias

def attend(pack):
    query, key_rows, value = pack
    length, width = query.shape
    head_size = width // HEADS
    query_h = query.reshape(length, HEADS, head_size)
    key_h = key_rows.reshape(length, HEADS, head_size)
    value_h = value.reshape(length, HEADS, head_size)
    scores = low_back(jnp.einsum('qhd,khd->hqk', query_h, key_h, precision=HIGH) * head_size ** (-0.5))
    probs = jax.nn.softmax(scores, axis=-1)
    mixed = jnp.einsum('hqk,khd->qhd', low(probs), value_h, precision=HIGH)
    return mixed.reshape(length, width)

def block(state, w_qkv, w_out, w_in, w_down, gain, bias, fcb):
    rows, width = state.shape
    clips = rows // SEQ
    normed = low(norm_rows(state, gain[0], bias[0]))
    qkv_bias = jnp.concatenate([bias[1], jnp.zeros_like(bias[1]), bias[2]])
    joined = low(low_back(jnp.dot(normed, w_qkv, precision=HIGH) + qkv_bias))
    query = joined[:, :width].reshape(clips, SEQ, width)
    key_rows = joined[:, width:2 * width].reshape(clips, SEQ, width)
    value = joined[:, 2 * width:].reshape(clips, SEQ, width)
    mixed = lax.map(jax.checkpoint(attend), (query, key_rows, value)).reshape(rows, width)
    mixed = low(low_back(mixed))
    middle = state + low_back(jnp.dot(mixed, w_out, precision=HIGH) + bias[3])
    normed_two = low(norm_rows(middle, gain[1], bias[4]))
    hidden = low_back(jnp.dot(normed_two, w_in, precision=HIGH) + fcb)
    activated = low(jax.nn.gelu(hidden, approximate=False))
    return middle + low_back(jnp.dot(activated, w_down, precision=HIGH) + bias[5])

def network(state, mask_f, mask_embed, attn_in, attn_out, fc_in, fc_out, gains, biases, fc_bias):
    state = state * (1.0 - mask_f) + mask_f * mask_embed
    for layer in range(LAYERS):
        state = block(state, attn_in[layer], attn_out[layer], fc_in[layer], fc_out[layer], gains[layer], biases[layer], fc_bias[layer])
    return state

def reference(tokens, mask, cotangent, mask_embed, attn_in, attn_out, fc_in, fc_out, gains, biases, fc_bias):
    params = tuple((a.astype(jnp.float32) for a in (mask_embed, attn_in, attn_out, fc_in, fc_out, gains, biases, fc_bias)))
    clips = TOKENS // SEQ
    group = max([k for k in (1, 2, 4, 8) if clips % k == 0 and k * SEQ <= 4096])
    count = clips // group
    rows = group * SEQ
    width = tokens.shape[1]
    inputs = tokens.astype(jnp.float32).reshape(count, rows, width)
    masks = mask.astype(jnp.float32).reshape(count, rows, 1)
    cots = cotangent.astype(jnp.float32).reshape(count, rows, width)

    def one(total, pack):
        state, mask_f, cot = pack
        out, back = jax.vjp(lambda xx, *ps: network(xx, mask_f, *ps), state, *params)
        grads = back(cot)
        total = tuple((a + b for a, b in zip(total, grads[1:])))
        return (total, (out, grads[0]))
    zeros = tuple((jnp.zeros_like(p) for p in params))
    total, (outs, dxs) = lax.scan(one, zeros, (inputs, masks, cots))
    return (outs.reshape(TOKENS, width), dxs.reshape(TOKENS, width), total[0], total[1], total[2], total[3], total[4], total[5], total[6], total[7])
```

```python
import functools
import jax, jax.numpy as jnp
from jax import lax
from jax.experimental import pallas as pl
from jax.experimental.pallas import tpu as pltpu
MESH = pl.DeviceIdType.MESH

class Pos:
    def __init__(s):
        s.dp = lax.axis_index("dp"); s.fs = lax.axis_index("fsdp")
        s.x = s.dp // 2; s.c = lax.rem(s.dp, 2)
        s.z = s.fs // 2; s.y = lax.rem(s.fs, 2)
        s.dev_c = (s.dp + 1 - 2 * s.c, s.fs)
        s.dev_x = (lax.rem(s.dp + 2, 4), s.fs)
        s.dev_y = (s.dp, s.fs + 1 - 2 * s.y)
    def dev_z(s, dz):
        return (s.dp, 2 * lax.rem(s.z + dz, 4) + s.y)

def remote(src, dst, ss, rs, dev):
    return pltpu.make_async_remote_copy(src_ref=src, dst_ref=dst, send_sem=ss, recv_sem=rs, device_id=dev, device_id_type=MESH)

def barrier(p, extra=()):
    bar = pltpu.get_barrier_semaphore()
    devs = [p.dev_c, p.dev_x, p.dev_y] + [p.dev_z(d) for d in (1, 2, 3)] + list(extra)
    for d in devs:
        pl.semaphore_signal(bar, inc=1, device_id=d, device_id_type=MESH)
    pl.semaphore_wait(bar, len(devs))

class Gather:
    def __init__(s, p, refs, ssem, rsem, lag=1, lead=2):
        s.p, s.refs, s.ss, s.rs, s.lag, s.lead = p, refs, ssem, rsem, lag, lead
        s.n = len(refs); s.t = 0
    def z(s, u, d):
        p, w = s.p, s.refs[u]; R, C = w.shape[2] // 2, w.shape[3] // 3
        b = w.at[p.z, p.y, pl.ds(pl.multiple_of(p.c * R, 16), R), pl.ds(pl.multiple_of(p.x * C, 128), 2 * C)]
        return remote(b, b, s.ss.at[u, d], s.rs.at[u, d], p.dev_z(d + 1))
    def y(s, u):
        p, w = s.p, s.refs[u]; R, C = w.shape[2] // 2, w.shape[3] // 3
        b = w.at[:, p.y, pl.ds(pl.multiple_of(p.c * R, 16), R), pl.ds(pl.multiple_of(p.x * C, 128), 2 * C)]
        return remote(b, b, s.ss.at[u, 3], s.rs.at[u, 3], p.dev_y)
    def xx(s, u):
        p, w = s.p, s.refs[u]; R, C = w.shape[2] // 2, w.shape[3] // 3
        b = w.at[:, :, pl.ds(pl.multiple_of(p.c * R, 16), R), pl.ds(pl.multiple_of(p.x * 2 * C, 128), C)]
        return remote(b, b, s.ss.at[u, 4], s.rs.at[u, 4], p.dev_x)
    def cc(s, u):
        p, w = s.p, s.refs[u]; R = w.shape[2] // 2
        b = w.at[:, :, pl.ds(pl.multiple_of(p.c * R, 16), R), :]
        return remote(b, b, s.ss.at[u, 5], s.rs.at[u, 5], p.dev_c)
    def start(s):
        for u in range(s.lead):
            for d in range(3): s.z(u, d).start()
    def pump(s):
        t, L, n = s.t, s.lag, s.n; s.t += 1
        v = t - 3 * L
        if 0 <= v < n: s.cc(v).wait()
        v = t - 2 * L
        if 0 <= v < n: s.xx(v).wait(); s.cc(v).start()
        v = t - L
        if 0 <= v < n: s.y(v).wait(); s.xx(v).start()
        if t < n:
            for d in range(3): s.z(t, d).wait()
            s.y(t).start()
        if t + s.lead < n:
            for d in range(3): s.z(t + s.lead, d).start()
        return t - 3 * L
    def until(s, u):
        while s.t - 3 * s.lag <= u: s.pump()

NA, ND = 8, 3
def unit_views(wa, wd, layer):
    return [wa.at[layer, k] for k in range(NA)] + [wd.at[layer, k] for k in range(ND)]

def load_shards(p, attn_in, attn_out, fc_in, fc_out, wa, wd, sem):
    out = []
    i = 0
    for l in range(2):
        for k in range(NA):
            if k < 3: src = attn_in.at[l, :, pl.ds(768 * k, 768)]
            elif k == 3: src = attn_out.at[l]
            else: src = fc_in.at[l, :, pl.ds(768 * (k - 4), 768)]
            out.append(pltpu.make_async_copy(src, wa.at[l, k, p.z, p.y], sem.at[i])); i += 1
        for k in range(ND):
            out.append(pltpu.make_async_copy(fc_out.at[l, pl.ds(128 * k, 128)], wd.at[l, k, p.z, p.y], sem.at[i])); i += 1
    return out

class Reduce:
    def __init__(s, p, units, bufs, ssem, rsem, lag=2, clag=1):
        s.p, s.units, s.b, s.ss, s.rs, s.L, s.Lc = p, units, bufs, ssem, rsem, lag, clag
        s.n = len(units); s.t = 0
        p2 = p
        s.half = []
    def geo(s, u):
        w, fin, out, kind, j = s.units[u]
        R = w.shape[2] // 2; p = s.p
        rc = pl.ds(pl.multiple_of(p.c * R, 16), R)
        ro = pl.ds(pl.multiple_of((1 - p.c) * R, 16), R)
        xc = pl.ds(pl.multiple_of(p.x * 384, 128), 384)
        xo = pl.ds(pl.multiple_of((1 - p.x) * 384, 128), 384)
        return w, fin, out, kind, j, R, rc, ro, xc, xo
    def sem(s, u, i):
        k = u % (2 * s.L)
        return s.ss.at[k, i], s.rs.at[k, i]
    def copy_c(s, u):
        w, fin, out, kind, j, R, rc, ro, xc, xo = s.geo(u)
        return remote(w.at[:, :, ro, :], s.b["c"].at[u % (2 * s.Lc), :, :, pl.ds(0, R), :], *s.sem(u, 0), s.p.dev_c)
    def hop1(s, u):
        w, fin, out, kind, j, R, rc, ro, xc, xo = s.geo(u); p = s.p
        if kind == 0:
            return remote(w.at[:, :, rc, xo], s.b["h1x"].at[j % s.L, :, :, pl.ds(0, R), :], *s.sem(u, 1), p.dev_x)
        return remote(w.at[:, 1 - p.y, rc, :], s.b["h1y"].at[j % s.L, :, pl.ds(0, R), :], *s.sem(u, 1), p.dev_y)
    def hop2(s, u):
        w, fin, out, kind, j, R, rc, ro, xc, xo = s.geo(u); p = s.p
        if kind == 0:
            return [remote(w.at[:, 1 - p.y, rc, xc], s.b["h2y"].at[j % s.L, :, pl.ds(0, R), :], *s.sem(u, 2), p.dev_y)]
        return [remote(w.at[lax.rem(p.z + d + 1, 4), p.y, rc, :], s.b["h2z"].at[j % s.L, d, pl.ds(0, R), :], *s.sem(u, 2 + d), p.dev_z(d + 1)) for d in range(3)]
    def hop3(s, u):
        w, fin, out, kind, j, R, rc, ro, xc, xo = s.geo(u); p = s.p
        if kind == 0:
            return [remote(w.at[lax.rem(p.z + d + 1, 4), p.y, rc, xc], s.b["h3z"].at[j % s.L, d, pl.ds(0, R), :], *s.sem(u, 5 + d), p.dev_z(d + 1)) for d in range(3)]
        return [remote(w.at[p.z, p.y, rc, :], s.b["h3x"].at[j % s.L, pl.ds(0, R), :], *s.sem(u, 5), p.dev_x)]
    def xa(s, u):
        w, fin, out, kind, j, R, rc, ro, xc, xo = s.geo(u)
        return remote(fin.at[rc, xc], fin.at[rc, xc], *s.sem(u, 8), s.p.dev_x)
    def ca(s, u):
        w, fin, out, kind, j, R, rc, ro, xc, xo = s.geo(u)
        return remote(fin.at[rc, :], fin.at[rc, :], *s.sem(u, 9), s.p.dev_c)
    def out_copy(s, u):
        w, fin, out, kind, j, R, rc, ro, xc, xo = s.geo(u)
        return pltpu.make_async_copy(fin, out, s.b["osem"].at[u])
    def add_c(s, u):
        w, fin, out, kind, j, R, rc, ro, xc, xo = s.geo(u); c = s.b["c"].at[u % (2 * s.Lc)]
        def body(i, _):
            a, b = i // 2, lax.rem(i, 2)
            w[a, b, rc, :] = w[a, b, rc, :] + c[a, b, pl.ds(0, R), :]
            return 0
        lax.fori_loop(0, 8, body, 0)
    def add1(s, u):
        w, fin, out, kind, j, R, rc, ro, xc, xo = s.geo(u); p = s.p
        if kind == 0:
            h = s.b["h1x"].at[j % s.L]
            def body(i, _):
                a, b = i // 2, lax.rem(i, 2)
                w[a, b, rc, xc] = w[a, b, rc, xc] + h[a, b, pl.ds(0, R), :]
                return 0
            lax.fori_loop(0, 8, body, 0)
        else:
            h = s.b["h1y"].at[j % s.L]
            def body(a, _):
                w[a, p.y, rc, :] = w[a, p.y, rc, :] + h[a, pl.ds(0, R), :]
                return 0
            lax.fori_loop(0, 4, body, 0)
    def add2(s, u):
        w, fin, out, kind, j, R, rc, ro, xc, xo = s.geo(u); p = s.p
        if kind == 0:
            h = s.b["h2y"].at[j % s.L]
            def body(a, _):
                w[a, p.y, rc, xc] = w[a, p.y, rc, xc] + h[a, pl.ds(0, R), :]
                return 0
            lax.fori_loop(0, 4, body, 0)
        else:
            h = s.b["h2z"].at[j % s.L]
            f = lambda d: h[d, pl.ds(0, R), :].astype(jnp.float32)
            w[p.z, p.y, rc, :] = (w[p.z, p.y, rc, :].astype(jnp.float32) + f(0) + f(1) + f(2)).astype(jnp.bfloat16)
    def add3(s, u):
        w, fin, out, kind, j, R, rc, ro, xc, xo = s.geo(u); p = s.p
        if kind == 0:
            h = s.b["h3z"].at[j % s.L]
            f = lambda d: h[d, pl.ds(0, R), :].astype(jnp.float32)
            fin[rc, xc] = (w[p.z, p.y, rc, xc].astype(jnp.float32) + f(0) + f(1) + f(2)).astype(jnp.bfloat16)
        else:
            h = s.b["h3x"].at[j % s.L]
            fin[rc, :] = w[p.z, p.y, rc, :] + h[pl.ds(0, R), :]
    def pump(s):
        t, L, n = s.t, s.L, s.n; s.t += 1
        ok = lambda v: 0 <= v < n
        v = t - s.Lc - 5 * L
        if ok(v) and s.units[v][3] == 0: s.ca(v).wait(); s.out_copy(v).start()
        v = t - s.Lc - 4 * L
        if ok(v):
            if s.units[v][3] == 0: s.xa(v).wait(); s.ca(v).start()
            else: s.ca(v).wait(); s.out_copy(v).start()
        v = t - s.Lc - 3 * L
        if ok(v):
            for q in s.hop3(v): q.wait()
            s.add3(v)
            if s.units[v][3] == 0: s.xa(v).start()
            else: s.ca(v).start()
        v = t - s.Lc - 2 * L
        if ok(v):
            for q in s.hop2(v): q.wait()
            s.add2(v)
            for q in s.hop3(v): q.start()
        v = t - s.Lc - L
        if ok(v):
            s.hop1(v).wait(); s.add1(v)
            for q in s.hop2(v): q.start()
        v = t - s.Lc
        if ok(v):
            s.copy_c(v).wait(); s.add_c(v); s.hop1(v).start()
        if ok(t): s.copy_c(t).start()
    def finish(s):
        while s.t < s.n + s.Lc + 5 * s.L: s.pump()
        for u in range(s.n): s.out_copy(u).wait()

def reduce_scratch(lag, clag):
    b = jnp.bfloat16; V = pltpu.VMEM
    return dict(c=V((2 * clag, 4, 2, 64, 768), b), h1x=V((lag, 4, 2, 64, 384), b), h1y=V((lag, 4, 64, 768), b),
        h2y=V((lag, 4, 64, 384), b), h2z=V((lag, 3, 64, 768), b), h3z=V((lag, 3, 64, 384), b), h3x=V((lag, 64, 768), b),
        osem=pltpu.SemaphoreType.DMA((22,)))
ORDER = [("D", 0), ("D", 1), ("D", 2), ("A", 4), ("A", 5), ("A", 6), ("A", 7), ("A", 3), ("A", 0), ("A", 1), ("A", 2)]
def reduce_units(wa, wd, fa, fd, oa, od):
    out = []; cnt = [0, 0]
    for l in (1, 0):
        for i, (k, q) in enumerate(ORDER):
            kind = (i + (1 - l)) % 2
            w, f, o = (wa, fa, oa) if k == "A" else (wd, fd, od)
            out.append((w.at[l, q], f.at[l, q], o.at[l, q], kind, cnt[kind])); cnt[kind] += 1
    return out


from jax.sharding import PartitionSpec as P

HEADS = 12
SEQ = 512
LAYERS = 2


eps = 1e-06


def norm_rows(values, gain, bias):
    center = values - jnp.mean(values, axis=-1, keepdims=True)
    spread = jnp.mean(center * center, axis=-1, keepdims=True)
    return center * lax.rsqrt(spread + eps) * gain + bias


def gelu_exact(values):
    return jax.nn.gelu(values, approximate=False)


def split_heads(values, clips):
    width = values.shape[1]
    return values.reshape(clips, SEQ, HEADS, width // HEADS)


def attend(pack):
    query, key_rows, value = pack
    scale = query.shape[-1] ** (-0.5)
    scores = jnp.einsum("qhd,khd->hqk", query, key_rows, preferred_element_type=jnp.float32) * scale
    top = jnp.max(scores, axis=-1, keepdims=True)
    expo = jnp.exp(scores - top)
    total = jnp.sum(expo, axis=-1, keepdims=True)
    probs = (expo / total).astype(jnp.bfloat16)
    mixed = jnp.einsum("hqk,khd->qhd", probs, value, preferred_element_type=jnp.float32)
    return (mixed, top + jnp.log(total))


def attend_back(pack):
    query, key_rows, value, logsum, d_mixed = pack
    scale = query.shape[-1] ** (-0.5)
    scores = jnp.einsum("qhd,khd->hqk", query, key_rows, preferred_element_type=jnp.float32) * scale
    probs = jnp.exp(scores - logsum)
    d_probs = jnp.einsum("qhd,khd->hqk", d_mixed, value, preferred_element_type=jnp.float32)
    d_value = jnp.einsum(
        "hqk,qhd->khd", probs.astype(jnp.bfloat16), d_mixed, preferred_element_type=jnp.float32
    )
    d_scores = probs * (d_probs - jnp.sum(probs * d_probs, axis=-1, keepdims=True))
    d_scaled = d_scores.astype(jnp.bfloat16) * scale
    d_query = jnp.einsum("hqk,khd->qhd", d_scaled, key_rows, preferred_element_type=jnp.float32)
    d_key = jnp.einsum("hqk,qhd->khd", d_scaled, query, preferred_element_type=jnp.float32)
    return (d_query, d_key, d_value)


def layer_forward(state, weights):
    w_qkv, w_out, w_in, w_down, gain, bias, fcb = weights
    rows, width = state.shape
    clips = rows // SEQ
    normed = norm_rows(state, gain[0].astype(jnp.float32), bias[0].astype(jnp.float32)).astype(
        jnp.bfloat16
    )
    qkv_bias = jnp.concatenate([bias[1], jnp.zeros_like(bias[1]), bias[2]]).astype(jnp.float32)
    joined = (jnp.dot(normed, w_qkv, preferred_element_type=jnp.float32) + qkv_bias).astype(
        jnp.bfloat16
    )
    query = split_heads(joined[:, :width], clips)
    key_rows = split_heads(joined[:, width : 2 * width], clips)
    value = split_heads(joined[:, 2 * width :], clips)
    mixed, logsum = lax.map(attend, (query, key_rows, value))
    mixed = mixed.reshape(rows, width).astype(jnp.bfloat16)
    middle = (
        state
        + jnp.dot(mixed, w_out, preferred_element_type=jnp.float32)
        + bias[3].astype(jnp.float32)
    )
    normed_two = norm_rows(middle, gain[1].astype(jnp.float32), bias[4].astype(jnp.float32)).astype(
        jnp.bfloat16
    )
    hidden = jnp.dot(normed_two, w_in, preferred_element_type=jnp.float32) + fcb.astype(jnp.float32)
    activated = gelu_exact(hidden).astype(jnp.bfloat16)
    return (normed, query, key_rows, value, logsum, mixed, middle, normed_two, hidden, activated)


def layer_finish(saved, weights):
    middle = saved[6]
    activated = saved[9]
    return (
        middle
        + jnp.dot(activated, weights[3], preferred_element_type=jnp.float32)
        + weights[5][5].astype(jnp.float32)
    )


def layer_backward(state, weights, grad):
    w_qkv, w_out, w_in, w_down, gain, bias, fcb = weights
    rows, width = state.shape
    clips = rows // SEQ
    normed, query, key_rows, value, logsum, mixed, middle, normed_two, hidden, activated = (
        layer_forward(state, weights)
    )
    d_up = grad.astype(jnp.bfloat16)
    g_down = jnp.einsum("tf,td->fd", activated, d_up, preferred_element_type=jnp.float32)
    d_two = jnp.sum(d_up.astype(jnp.float32), axis=0)
    d_act = jnp.einsum("td,fd->tf", d_up, w_down, preferred_element_type=jnp.float32)
    d_hidden = jax.vjp(gelu_exact, hidden)[1](d_act)[0].astype(jnp.bfloat16)
    g_in = jnp.einsum("td,tf->df", normed_two, d_hidden, preferred_element_type=jnp.float32)
    d_one = jnp.sum(d_hidden.astype(jnp.float32), axis=0)
    d_normed_two = jnp.einsum("tf,df->td", d_hidden, w_in, preferred_element_type=jnp.float32)
    back_two = jax.vjp(norm_rows, middle, gain[1].astype(jnp.float32), bias[4].astype(jnp.float32))[
        1
    ]
    d_middle, d_gain_two, d_bias_two = back_two(d_normed_two)
    d_middle = grad + d_middle
    d_branch = d_middle.astype(jnp.bfloat16)
    g_out = jnp.einsum("td,te->de", mixed, d_branch, preferred_element_type=jnp.float32)
    d_outb = jnp.sum(d_branch.astype(jnp.float32), axis=0)
    d_mixed = jnp.einsum("te,de->td", d_branch, w_out, preferred_element_type=jnp.float32).astype(
        jnp.bfloat16
    )
    d_query, d_key, d_value = lax.map(
        attend_back, (query, key_rows, value, logsum, split_heads(d_mixed, clips))
    )
    d_joined = jnp.concatenate(
        [d_query.reshape(rows, width), d_key.reshape(rows, width), d_value.reshape(rows, width)],
        axis=1,
    ).astype(jnp.bfloat16)
    g_qkv = jnp.einsum("td,te->de", normed, d_joined, preferred_element_type=jnp.float32)
    d_sums = jnp.sum(d_joined.astype(jnp.float32), axis=0)
    d_normed = jnp.einsum("te,de->td", d_joined, w_qkv, preferred_element_type=jnp.float32)
    back_one = jax.vjp(norm_rows, state, gain[0].astype(jnp.float32), bias[0].astype(jnp.float32))[
        1
    ]
    d_state, d_gain_one, d_bias_one = back_one(d_normed)
    gain_terms = jnp.stack([d_gain_one, d_gain_two])
    bias_terms = jnp.stack(
        [d_bias_one, d_sums[:width], d_sums[2 * width :], d_outb, d_bias_two, d_two]
    )
    return (d_middle + d_state, (g_qkv, g_out, g_in, g_down, gain_terms, bias_terms, d_one))


def local(
    tokens, mask, cotangent, mask_embed, attn_in, attn_out, fc_in, fc_out, gains, biases, fc_bias
):
    mask_f = mask.astype(jnp.float32)[:, None]
    state = tokens.astype(jnp.float32)
    stored = []
    kept = []
    for layer in range(LAYERS):
        fetched = (
            lax.all_gather(attn_in[layer], "fsdp", axis=0, tiled=True),
            lax.all_gather(attn_out[layer], "fsdp", axis=0, tiled=True),
            lax.all_gather(fc_in[layer], "fsdp", axis=0, tiled=True),
            lax.all_gather(fc_out[layer], "fsdp", axis=0, tiled=True),
            lax.all_gather(gains[layer], "fsdp", axis=1, tiled=True),
            lax.all_gather(biases[layer], "fsdp", axis=1, tiled=True),
            lax.all_gather(fc_bias[layer], "fsdp", axis=0, tiled=True),
            lax.all_gather(mask_embed, "fsdp", axis=0, tiled=True),
        )
        if layer == 0:
            state = state * (1.0 - mask_f) + mask_f * fetched[7].astype(jnp.float32)
        stored.append(state)
        weights = tuple(fetched[:7])
        kept.append(weights)
        state = layer_finish(layer_forward(state, weights), weights)
    grad = cotangent.astype(jnp.float32)
    layer_grads = [None] * LAYERS
    for layer in reversed(range(LAYERS)):
        weights = tuple(
            (
                lax.all_gather(attn_in[layer], "fsdp", axis=0, tiled=True),
                lax.all_gather(attn_out[layer], "fsdp", axis=0, tiled=True),
                lax.all_gather(fc_in[layer], "fsdp", axis=0, tiled=True),
                lax.all_gather(fc_out[layer], "fsdp", axis=0, tiled=True),
                lax.all_gather(gains[layer], "fsdp", axis=1, tiled=True),
                lax.all_gather(biases[layer], "fsdp", axis=1, tiled=True),
                lax.all_gather(fc_bias[layer], "fsdp", axis=0, tiled=True),
            )
        )
        grad, terms = layer_backward(stored[layer], weights, grad)
        if layer == 0:
            mask_term = jnp.sum(grad * mask_f, axis=0)
        else:
            mask_term = jnp.zeros((grad.shape[1],), jnp.float32)
        shares = (
            lax.psum_scatter(terms[0], "fsdp", scatter_dimension=0, tiled=True),
            lax.psum_scatter(terms[1], "fsdp", scatter_dimension=0, tiled=True),
            lax.psum_scatter(terms[2], "fsdp", scatter_dimension=0, tiled=True),
            lax.psum_scatter(terms[3], "fsdp", scatter_dimension=0, tiled=True),
            lax.psum_scatter(terms[4], "fsdp", scatter_dimension=1, tiled=True),
            lax.psum_scatter(terms[5], "fsdp", scatter_dimension=1, tiled=True),
            lax.psum_scatter(terms[6], "fsdp", scatter_dimension=0, tiled=True),
            lax.psum_scatter(mask_term, "fsdp", scatter_dimension=0, tiled=True),
        )
        slices = (
            lax.psum_scatter(
                shares[0].astype(jnp.bfloat16), "dp", scatter_dimension=1, tiled=True
            ).astype(jnp.float32),
            lax.psum_scatter(
                shares[1].astype(jnp.bfloat16), "dp", scatter_dimension=1, tiled=True
            ).astype(jnp.float32),
            lax.psum_scatter(
                shares[2].astype(jnp.bfloat16), "dp", scatter_dimension=1, tiled=True
            ).astype(jnp.float32),
            lax.psum_scatter(
                shares[3].astype(jnp.bfloat16), "dp", scatter_dimension=1, tiled=True
            ).astype(jnp.float32),
        )
        matrices = (
            lax.all_gather(slices[0].astype(jnp.bfloat16), "dp", axis=1, tiled=True).astype(
                jnp.float32
            ),
            lax.all_gather(slices[1].astype(jnp.bfloat16), "dp", axis=1, tiled=True).astype(
                jnp.float32
            ),
            lax.all_gather(slices[2].astype(jnp.bfloat16), "dp", axis=1, tiled=True).astype(
                jnp.float32
            ),
            lax.all_gather(slices[3].astype(jnp.bfloat16), "dp", axis=1, tiled=True).astype(
                jnp.float32
            ),
        )
        smalls = lax.psum((shares[4], shares[5], shares[6], shares[7]), "dp")
        layer_grads[layer] = (
            matrices[0],
            matrices[1],
            matrices[2],
            matrices[3],
            smalls[0],
            smalls[1],
            smalls[2],
            smalls[3],
        )
    input_grad = grad * (1.0 - mask_f)
    stacked = [jnp.stack([layer_grads[lay][item] for lay in range(LAYERS)]) for item in range(7)]
    results = tuple(stacked) + (layer_grads[0][7],)
    return (
        state,
        input_grad,
        results[7],
        results[0],
        results[1],
        results[2],
        results[3],
        results[4],
        results[5],
        results[6],
    )


def generic_solution(mesh):
    placed = (
        P(("dp", "fsdp"), None),
        P(("dp", "fsdp")),
        P(("dp", "fsdp"), None),
        P("fsdp"),
        P(None, "fsdp", None),
        P(None, "fsdp", None),
        P(None, "fsdp", None),
        P(None, "fsdp", None),
        P(None, None, "fsdp"),
        P(None, None, "fsdp"),
        P(None, "fsdp"),
    )
    return jax.shard_map(
        local,
        mesh=mesh,
        in_specs=placed,
        out_specs=(
            P(("dp", "fsdp"), None),
            P(("dp", "fsdp"), None),
            P("fsdp"),
            P(None, "fsdp", None),
            P(None, "fsdp", None),
            P(None, "fsdp", None),
            P(None, "fsdp", None),
            P(None, None, "fsdp"),
            P(None, None, "fsdp"),
            P(None, "fsdp"),
        ),
        check_vma=False,
    )


BF = jnp.bfloat16
VMEM_LIMIT = 60 * 1024 * 1024


def gather_kernel(ai, ao, fi, fo, oa, od, wa, wd, lsem, ss, rs, osem):
    p = Pos()
    loads = load_shards(p, ai, ao, fi, fo, wa, wd, lsem)
    for c in loads:
        c.start()
    for c in loads:
        c.wait()
    barrier(p)
    g = Gather(p, unit_views(wa, wd, 0) + unit_views(wa, wd, 1), ss, rs, 2, 2)
    g.start()
    g.until(g.n - 1)
    outs = [pltpu.make_async_copy(wa, oa, osem.at[0]), pltpu.make_async_copy(wd, od, osem.at[1])]
    for c in outs:
        c.start()
    for c in outs:
        c.wait()


def gather_weights(ai, ao, fi, fo):
    sa, sd = (2, 8, 4, 2, 96, 768), (2, 3, 4, 2, 128, 768)
    return pl.pallas_call(
        gather_kernel,
        out_shape=[jax.ShapeDtypeStruct(sa, BF), jax.ShapeDtypeStruct(sd, BF)],
        in_specs=[pl.BlockSpec(memory_space=pl.ANY)] * 4,
        out_specs=[pl.BlockSpec(memory_space=pl.ANY)] * 2,
        scratch_shapes=[
            pltpu.VMEM(sa, BF), pltpu.VMEM(sd, BF), pltpu.SemaphoreType.DMA((22,)),
            pltpu.SemaphoreType.DMA((22, 6)), pltpu.SemaphoreType.DMA((22, 6)), pltpu.SemaphoreType.DMA((2,)),
        ],
        compiler_params=pltpu.CompilerParams(collective_id=0, has_side_effects=True, vmem_limit_bytes=VMEM_LIMIT),
    )(ai, ao, fi, fo)


def reduce_kernel(ga, gd, oa, od, wa, wd, fa, fd, bufs, lsem, ss, rs):
    p = Pos()
    loads = [pltpu.make_async_copy(ga, wa, lsem.at[0]), pltpu.make_async_copy(gd, wd, lsem.at[1])]
    for c in loads:
        c.start()
    for c in loads:
        c.wait()
    barrier(p)
    r = Reduce(p, reduce_units(wa, wd, fa, fd, oa, od), bufs, ss, rs, 2, 1)
    r.finish()


def reduce_grads(ga, gd):
    return pl.pallas_call(
        reduce_kernel,
        out_shape=[jax.ShapeDtypeStruct((2, 8, 96, 768), BF), jax.ShapeDtypeStruct((2, 3, 128, 768), BF)],
        in_specs=[pl.BlockSpec(memory_space=pl.ANY)] * 2,
        out_specs=[pl.BlockSpec(memory_space=pl.ANY)] * 2,
        scratch_shapes=[
            pltpu.VMEM((2, 8, 4, 2, 96, 768), BF), pltpu.VMEM((2, 3, 4, 2, 128, 768), BF),
            pltpu.VMEM((2, 8, 96, 768), BF), pltpu.VMEM((2, 3, 128, 768), BF),
            reduce_scratch(2, 1), pltpu.SemaphoreType.DMA((2,)),
            pltpu.SemaphoreType.DMA((4, 10)), pltpu.SemaphoreType.DMA((4, 10)),
        ],
        compiler_params=pltpu.CompilerParams(collective_id=1, has_side_effects=True, vmem_limit_bytes=VMEM_LIMIT),
    )(ga, gd)


def fused_local(tokens, mask, cotangent, mask_embed, attn_in, attn_out, fc_in, fc_out, gains, biases, fc_bias):
    wa, wd = gather_weights(attn_in, attn_out, fc_in, fc_out)
    wa = wa.reshape(2, 8, 768, 768)
    pack = jnp.concatenate([gains.reshape(4, 96), biases.reshape(12, 96), fc_bias.reshape(8, 96), mask_embed.reshape(1, 96)], axis=0)
    full = lax.all_gather(pack, "fsdp", axis=0)
    line = lambda r0, r1: full[:, r0:r1].transpose(1, 0, 2).reshape(r1 - r0, 768)
    gain_f, bias_f = line(0, 4).reshape(2, 2, 768), line(4, 16).reshape(2, 6, 768)
    fcb_f = full[:, 16:24].reshape(8, 2, 384).transpose(1, 0, 2).reshape(2, 3072)
    embed = line(24, 25)[0]
    weights = []
    for l in range(LAYERS):
        weights.append((
            wa[l, 0:3].transpose(1, 0, 2).reshape(768, 2304), wa[l, 3],
            wa[l, 4:8].transpose(1, 0, 2).reshape(768, 3072),
            wd[l].reshape(3, 8, 128, 768).transpose(1, 0, 2, 3).reshape(3072, 768),
            gain_f[l], bias_f[l], fcb_f[l]))
    mask_f = mask.astype(jnp.float32)[:, None]
    state = tokens.astype(jnp.float32) * (1.0 - mask_f) + mask_f * embed.astype(jnp.float32)
    stored = []
    for l in range(LAYERS):
        stored.append(state)
        state = layer_finish(layer_forward(state, weights[l]), weights[l])
    grad = cotangent.astype(jnp.float32)
    terms = [None] * LAYERS
    for l in reversed(range(LAYERS)):
        grad, terms[l] = layer_backward(stored[l], weights[l], grad)
    cut = lambda g: g.astype(BF).reshape(768, -1, 768).transpose(1, 0, 2)
    ga = jnp.stack([jnp.concatenate([cut(t[0]), cut(t[1]), cut(t[2])]) for t in terms]).reshape(2, 8, 4, 2, 96, 768)
    gd = jnp.stack([t[3].astype(BF).reshape(8, 3, 128, 768).transpose(1, 0, 2, 3) for t in terms]).reshape(2, 3, 4, 2, 128, 768)
    oa, od = reduce_grads(ga, gd)
    back = lambda o: o.transpose(0, 2, 1, 3).reshape(2, 96, -1).astype(jnp.float32)
    mask_term = jnp.sum(grad * mask_f, axis=0)
    small = jnp.concatenate([jnp.stack([t[4] for t in terms]).reshape(4, 768), jnp.stack([t[5] for t in terms]).reshape(12, 768),
        jnp.stack([t[6] for t in terms]).reshape(8, 768), mask_term[None]])
    small = lax.psum(small, ("dp", "fsdp"))
    f = lax.axis_index("fsdp")
    own = lax.dynamic_slice(small, (0, f * 96), (25, 96))
    fb = lax.dynamic_slice(small[16:24].reshape(2, 3072), (0, f * 384), (2, 384))
    return (
        state, grad * (1.0 - mask_f), own[24], back(oa[:, 0:3]), oa[:, 3].astype(jnp.float32), back(oa[:, 4:8]),
        od.reshape(2, 384, 768).astype(jnp.float32), own[0:4].reshape(2, 2, 96), own[4:16].reshape(2, 6, 96), fb)


def solution(mesh):
    if dict(mesh.shape) != {"dp": 4, "fsdp": 8}:
        return generic_solution(mesh)
    rows = P(("dp", "fsdp"), None)
    mat = P(None, "fsdp", None)
    vec = P(None, None, "fsdp")
    return jax.shard_map(
        fused_local, mesh=mesh,
        in_specs=(rows, P(("dp", "fsdp")), rows, P("fsdp"), mat, mat, mat, mat, vec, vec, P(None, "fsdp")),
        out_specs=(rows, rows, P("fsdp"), mat, mat, mat, mat, vec, vec, P(None, "fsdp")),
        check_vma=False)
```

```python
import functools

import jax
import jax.numpy as jnp
from jax import lax
from jax.experimental import pallas as pl
from jax.experimental.pallas import tpu as pltpu
from jax.sharding import PartitionSpec as P
MESH = pl.DeviceIdType.MESH

class Pos:
    def __init__(s):
        s.dp = lax.axis_index("dp"); s.fs = lax.axis_index("fsdp")
        s.x = s.dp // 2; s.c = lax.rem(s.dp, 2)
        s.z = s.fs // 2; s.y = lax.rem(s.fs, 2)
        s.dev_c = (s.dp + 1 - 2 * s.c, s.fs)
        s.dev_x = (lax.rem(s.dp + 2, 4), s.fs)
        s.dev_y = (s.dp, s.fs + 1 - 2 * s.y)
    def dev_f(s, d):
        return (s.dp, lax.rem(s.fs + d, 8))
    def dev_z(s, dz):
        return (s.dp, 2 * lax.rem(s.z + dz, 4) + s.y)

def remote(src, dst, ss, rs, dev):
    return pltpu.make_async_remote_copy(src_ref=src, dst_ref=dst, send_sem=ss, recv_sem=rs, device_id=dev, device_id_type=MESH)

def barrier(p):
    bar = pltpu.get_barrier_semaphore()
    devs = [p.dev_c, p.dev_x] + [p.dev_f(d) for d in range(1, 8)]
    for d in devs:
        pl.semaphore_signal(bar, inc=1, device_id=d, device_id_type=MESH)
    pl.semaphore_wait(bar, len(devs))

class Gather:
    def __init__(s, p, refs, ssem, rsem, lag=1, lead=2):
        s.p, s.refs, s.ss, s.rs, s.lag, s.lead = p, refs, ssem, rsem, lag, lead
        s.n = len(refs); s.t = 0
    def z(s, u, d):
        p, w = s.p, s.refs[u]; R, C = w.shape[2] // 2, w.shape[3] // 3
        b = w.at[p.z, p.y, pl.ds(pl.multiple_of(p.c * R, 16), R), pl.ds(pl.multiple_of(p.x * C, 128), 2 * C)]
        return remote(b, b, s.ss.at[u, d], s.rs.at[u, d], p.dev_z(d + 1))
    def y(s, u):
        p, w = s.p, s.refs[u]; R, C = w.shape[2] // 2, w.shape[3] // 3
        b = w.at[:, p.y, pl.ds(pl.multiple_of(p.c * R, 16), R), pl.ds(pl.multiple_of(p.x * C, 128), 2 * C)]
        return remote(b, b, s.ss.at[u, 3], s.rs.at[u, 3], p.dev_y)
    def xx(s, u):
        p, w = s.p, s.refs[u]; R, C = w.shape[2] // 2, w.shape[3] // 3
        b = w.at[:, :, pl.ds(pl.multiple_of(p.c * R, 16), R), pl.ds(pl.multiple_of(p.x * 2 * C, 128), C)]
        return remote(b, b, s.ss.at[u, 4], s.rs.at[u, 4], p.dev_x)
    def cc(s, u):
        p, w = s.p, s.refs[u]; R = w.shape[2] // 2
        b = w.at[:, :, pl.ds(pl.multiple_of(p.c * R, 16), R), :]
        return remote(b, b, s.ss.at[u, 5], s.rs.at[u, 5], p.dev_c)
    def start(s):
        for u in range(s.lead):
            for d in range(3): s.z(u, d).start()
    def pump(s):
        t, L, n = s.t, s.lag, s.n; s.t += 1
        v = t - 3 * L
        if 0 <= v < n: s.cc(v).wait()
        v = t - 2 * L
        if 0 <= v < n: s.xx(v).wait(); s.cc(v).start()
        v = t - L
        if 0 <= v < n: s.y(v).wait(); s.xx(v).start()
        if t < n:
            for d in range(3): s.z(t, d).wait()
            s.y(t).start()
        if t + s.lead < n:
            for d in range(3): s.z(t + s.lead, d).start()
        return t - 3 * L
    def until(s, u):
        while s.t - 3 * s.lag <= u: s.pump()

NA, ND = 8, 3
def unit_views(wa, wd, layer):
    return [wa.at[layer, k] for k in range(NA)] + [wd.at[layer, k] for k in range(ND)]

def load_shards(p, attn_in, attn_out, fc_in, fc_out, wa, wd, sem):
    out = []
    i = 0
    for l in range(2):
        for k in range(NA):
            if k < 3: src = attn_in.at[l, :, pl.ds(768 * k, 768)]
            elif k == 3: src = attn_out.at[l]
            else: src = fc_in.at[l, :, pl.ds(768 * (k - 4), 768)]
            out.append(pltpu.make_async_copy(src, wa.at[l, k, p.z, p.y], sem.at[i])); i += 1
        for k in range(ND):
            out.append(pltpu.make_async_copy(fc_out.at[l, pl.ds(128 * k, 128)], wd.at[l, k, p.z, p.y], sem.at[i])); i += 1
    return out

class Reduce:
    def __init__(s, p, units, bufs, ssem, rsem, lag=2, clag=1):
        s.p, s.units, s.b, s.ss, s.rs, s.L, s.Lc = p, units, bufs, ssem, rsem, lag, clag
        s.n = len(units); s.t = 0
        s.born = {}
    def geo(s, u):
        w, fin, out, kind, j = s.units[u]
        R = w.shape[2] // 2; p = s.p
        rc = pl.ds(pl.multiple_of(p.c * R, 16), R)
        ro = pl.ds(pl.multiple_of((1 - p.c) * R, 16), R)
        xc = pl.ds(pl.multiple_of(p.x * 384, 128), 384)
        xo = pl.ds(pl.multiple_of((1 - p.x) * 384, 128), 384)
        return w, fin, out, kind, j, R, rc, ro, xc, xo
    def sem(s, u, i):
        k = u % (2 * s.L)
        return s.ss.at[k, i], s.rs.at[k, i]
    def copy_c(s, u):
        w, fin, out, kind, j, R, rc, ro, xc, xo = s.geo(u)
        return remote(w.at[:, :, ro, :], s.b["c"].at[u % (2 * s.Lc), :, :, pl.ds(0, R), :], *s.sem(u, 0), s.p.dev_c)
    def hop1(s, u):
        w, fin, out, kind, j, R, rc, ro, xc, xo = s.geo(u); p = s.p
        if kind == 0:
            return remote(w.at[:, :, rc, xo], s.b["h1x"].at[j % s.L, :, :, pl.ds(0, R), :], *s.sem(u, 1), p.dev_x)
        return remote(w.at[:, 1 - p.y, rc, :], s.b["h1y"].at[j % s.L, :, pl.ds(0, R), :], *s.sem(u, 1), p.dev_y)
    def hop2(s, u):
        w, fin, out, kind, j, R, rc, ro, xc, xo = s.geo(u); p = s.p
        if kind == 0:
            return [remote(w.at[:, 1 - p.y, rc, xc], s.b["h2y"].at[j % s.L, :, pl.ds(0, R), :], *s.sem(u, 2), p.dev_y)]
        return [remote(w.at[lax.rem(p.z + d + 1, 4), p.y, rc, :], s.b["h2z"].at[j % s.L, d, pl.ds(0, R), :], *s.sem(u, 2 + d), p.dev_z(d + 1)) for d in range(3)]
    def hop3(s, u):
        w, fin, out, kind, j, R, rc, ro, xc, xo = s.geo(u); p = s.p
        if kind == 0:
            return [remote(w.at[lax.rem(p.z + d + 1, 4), p.y, rc, xc], s.b["h3z"].at[j % s.L, d, pl.ds(0, R), :], *s.sem(u, 5 + d), p.dev_z(d + 1)) for d in range(3)]
        return [remote(w.at[p.z, p.y, rc, :], s.b["h3x"].at[j % s.L, pl.ds(0, R), :], *s.sem(u, 5), p.dev_x)]
    def xa(s, u):
        w, fin, out, kind, j, R, rc, ro, xc, xo = s.geo(u)
        return remote(fin.at[rc, xc], fin.at[rc, xc], *s.sem(u, 8), s.p.dev_x)
    def ca(s, u):
        w, fin, out, kind, j, R, rc, ro, xc, xo = s.geo(u)
        return remote(fin.at[rc, :], fin.at[rc, :], *s.sem(u, 9), s.p.dev_c)
    def out_copy(s, u):
        w, fin, out, kind, j, R, rc, ro, xc, xo = s.geo(u)
        return pltpu.make_async_copy(fin, out, s.b["osem"].at[u])
    def add_c(s, u):
        w, fin, out, kind, j, R, rc, ro, xc, xo = s.geo(u); c = s.b["c"].at[u % (2 * s.Lc)]
        def body(i, _):
            a, b = i // 2, lax.rem(i, 2)
            w[a, b, rc, :] = w[a, b, rc, :] + c[a, b, pl.ds(0, R), :]
            return 0
        lax.fori_loop(0, 8, body, 0)
    def add1(s, u):
        w, fin, out, kind, j, R, rc, ro, xc, xo = s.geo(u); p = s.p
        if kind == 0:
            h = s.b["h1x"].at[j % s.L]
            def body(i, _):
                a, b = i // 2, lax.rem(i, 2)
                w[a, b, rc, xc] = w[a, b, rc, xc] + h[a, b, pl.ds(0, R), :]
                return 0
            lax.fori_loop(0, 8, body, 0)
        else:
            h = s.b["h1y"].at[j % s.L]
            def body(a, _):
                w[a, p.y, rc, :] = w[a, p.y, rc, :] + h[a, pl.ds(0, R), :]
                return 0
            lax.fori_loop(0, 4, body, 0)
    def add2(s, u):
        w, fin, out, kind, j, R, rc, ro, xc, xo = s.geo(u); p = s.p
        if kind == 0:
            h = s.b["h2y"].at[j % s.L]
            def body(a, _):
                w[a, p.y, rc, xc] = w[a, p.y, rc, xc] + h[a, pl.ds(0, R), :]
                return 0
            lax.fori_loop(0, 4, body, 0)
        else:
            h = s.b["h2z"].at[j % s.L]
            f = lambda d: h[d, pl.ds(0, R), :].astype(jnp.float32)
            w[p.z, p.y, rc, :] = (w[p.z, p.y, rc, :].astype(jnp.float32) + f(0) + f(1) + f(2)).astype(jnp.bfloat16)
    def add3(s, u):
        w, fin, out, kind, j, R, rc, ro, xc, xo = s.geo(u); p = s.p
        if kind == 0:
            h = s.b["h3z"].at[j % s.L]
            f = lambda d: h[d, pl.ds(0, R), :].astype(jnp.float32)
            fin[rc, xc] = (w[p.z, p.y, rc, xc].astype(jnp.float32) + f(0) + f(1) + f(2)).astype(jnp.bfloat16)
        else:
            h = s.b["h3x"].at[j % s.L]
            fin[rc, :] = w[p.z, p.y, rc, :] + h[pl.ds(0, R), :]
    def at(s, t):
        return s.born.get(t)
    def pump(s, new=True):
        t, L = s.t, s.L
        s.t += 1
        v = s.at(t - s.Lc - 5 * L)
        if v is not None and s.units[v][3] == 0:
            s.ca(v).wait(); s.out_copy(v).start()
        v = s.at(t - s.Lc - 4 * L)
        if v is not None:
            if s.units[v][3] == 0:
                s.xa(v).wait(); s.ca(v).start()
            else:
                s.ca(v).wait(); s.out_copy(v).start()
        v = s.at(t - s.Lc - 3 * L)
        if v is not None:
            for q in s.hop3(v): q.wait()
            s.add3(v)
            if s.units[v][3] == 0: s.xa(v).start()
            else: s.ca(v).start()
        v = s.at(t - s.Lc - 2 * L)
        if v is not None:
            for q in s.hop2(v): q.wait()
            s.add2(v)
            for q in s.hop3(v): q.start()
        v = s.at(t - s.Lc - L)
        if v is not None:
            s.hop1(v).wait(); s.add1(v)
            for q in s.hop2(v): q.start()
        v = s.at(t - s.Lc)
        if v is not None:
            s.copy_c(v).wait(); s.add_c(v); s.hop1(v).start()
        if new:
            u = len(s.born)
            s.born[t] = u
            s.copy_c(u).start()
    def busy(s):
        return s.t <= max(s.born) + s.Lc + 5 * s.L
    def finish(s):
        while s.busy(): s.pump(False)
        for u in range(s.n): s.out_copy(u).wait()

def reduce_scratch(lag, clag):
    b = jnp.bfloat16; V = pltpu.VMEM
    return dict(c=V((2 * clag, 4, 2, 64, 768), b), h1x=V((lag, 4, 2, 64, 384), b), h1y=V((lag, 4, 64, 768), b),
        h2y=V((lag, 4, 64, 384), b), h2z=V((lag, 3, 64, 768), b), h3z=V((lag, 3, 64, 384), b), h3x=V((lag, 64, 768), b),
        osem=pltpu.SemaphoreType.DMA((22,)))
ORDER = [("D", 0), ("D", 1), ("D", 2), ("A", 4), ("A", 5), ("A", 6), ("A", 7), ("A", 3), ("A", 0), ("A", 1), ("A", 2)]
def reduce_units(wa, wd, fa, fd, oa, od):
    out = []; cnt = [0, 0]
    for l in (1, 0):
        for i, (k, q) in enumerate(ORDER):
            kind = (i + (1 - l)) % 2
            w, f, o = (wa, fa, oa) if k == "A" else (wd, fd, od)
            out.append((w.at[l, q], f.at[l, q], o.at[l, q], kind, cnt[kind])); cnt[kind] += 1
    return out


F32, BF = jnp.float32, jnp.bfloat16
NN = (((1,), (0,)), ((), ()))
NT = (((1,), (1,)), ((), ()))
TN = (((0,), (0,)), ((), ()))
def mm(a, b, dims=NN):
    return lax.dot_general(a, b, dims, preferred_element_type=F32)

ROWS, WIDTH, PAIRS = 512, 768, 6
def r_gain(l, i): return 2 * l + i
def r_bias(l, i): return 4 + 6 * l + i
R_EMBED = 16
def r_fcb(l, k): return 24 + 4 * l + k

def row(ref, r):
    return ref[pl.ds(r, 1), :]

def rows_loop(step, body):
    def run(i, c):
        body(pl.ds(pl.multiple_of(i * step, step), step))
        return c
    lax.fori_loop(0, ROWS // step, run, 0)

def gelu_parts(z):
    a = jnp.abs(z)
    t = 1.0 / (1.0 + (0.3275911 * 0.7071067811865476) * a)
    e = jnp.exp(-0.5 * (z * z))
    poly = t * (0.254829592 + t * (-0.284496736 + t * (1.421413741 + t * (-1.453152027 + t * 1.061405429))))
    tail = 0.5 * poly * e
    cdf = jnp.where(z < 0, tail, 1.0 - tail)
    return z * cdf, cdf + z * (0.3989422804014327 * e)

class Net:
    def __init__(s, r):
        s.__dict__.update(r)
    def w(s, l, k):
        return s.wa.at[l, k]
    def wtile(s, l, k, cols):
        v = s.wa[l, k, :, :, :, cols]
        return v.reshape(WIDTH, v.shape[-1])
    def norm(s, l, i, xh, rs, h):
        g, b = row(s.V, r_gain(l, i)), row(s.V, r_bias(l, 4 if i else 0))
        def body(q):
            v = s.x[q, :]
            c = v - jnp.mean(v, axis=-1, keepdims=True)
            r = lax.rsqrt(jnp.mean(c * c, axis=-1, keepdims=True) + 1e-6)
            n = c * r
            xh[q, :] = n.astype(BF)
            rs[l, q, :] = r
            h[q, :] = (n * g + b).astype(BF)
        rows_loop(64, body)
    def norm_back(s, l, i, d, xh, rs, out):
        g = row(s.V, r_gain(l, i))
        z = jnp.zeros((1, WIDTH), F32)
        def run(j, c):
            q = pl.ds(pl.multiple_of(j * 64, 64), 64)
            dv, n = d[q, :], xh[q, :].astype(F32)
            dn = dv * g
            m1 = jnp.mean(dn, axis=-1, keepdims=True)
            m2 = jnp.mean(dn * n, axis=-1, keepdims=True)
            e = s.x[q, :] + rs[l, q, :] * (dn - m1 - n * m2)
            s.x[q, :] = e
            sg, sb, so = c
            sg = sg + jnp.sum(dv * n, axis=0, keepdims=True)
            sb = sb + jnp.sum(dv, axis=0, keepdims=True)
            if out is not None:
                eb = e.astype(BF)
                out[q, :] = eb
                so = so + jnp.sum(eb.astype(F32), axis=0, keepdims=True)
            return sg, sb, so
        sg, sb, so = lax.fori_loop(0, ROWS // 64, run, (z, z, z))
        s.S[pl.ds(r_gain(l, i), 1), :] = sg
        s.S[pl.ds(r_bias(l, 4 if i else 0), 1), :] = sb
        return so
    def project(s, l, k):
        bias = None if k == 1 else row(s.V, r_bias(l, 1 if k == 0 else 2))
        def body(i, c):
            q = pl.ds(pl.multiple_of((i // 3) * 256, 256), 256)
            n = pl.ds(pl.multiple_of(lax.rem(i, 3) * 256, 256), 256)
            v = mm(s.h[q, :], s.wtile(l, k, n))
            if bias is not None:
                v = v + s.V[pl.ds(r_bias(l, 1 if k == 0 else 2), 1), n]
            s.t[k, q, n] = v.astype(BF)
            return c
        lax.fori_loop(0, 6, body, 0)
    def masks(s):
        lane = lax.broadcasted_iota(jnp.int32, (1, 128), 1)
        return [(lane < 64).astype(F32).astype(BF), (lane >= 64).astype(F32).astype(BF)]
    def attend(s, l, p0, p1):
        ms = s.masks()
        def body(p, c):
            n = pl.ds(pl.multiple_of(p * 128, 128), 128)
            kk = s.t[1, :, n]
            vt = s.t[2, :, n].T
            for b in range(2):
                q = pl.ds(256 * b, 256)
                qs = s.t[0, q, n] * 0.125
                outs = []
                for i in range(2):
                    st = mm(kk, qs * ms[i], NT)
                    top = jnp.max(st, axis=0, keepdims=True)
                    e = jnp.exp(st - top)
                    total = jnp.sum(e, axis=0, keepdims=True)
                    s.lse[l, pl.ds(2 * p + i, 1), q] = top + jnp.log(total)
                    outs.append(mm(vt[64 * i:64 * i + 64], e.astype(BF)) * (1.0 / total))
                s.o[q, n] = jnp.concatenate(outs, axis=0).T.astype(BF)
            return c
        lax.fori_loop(p0, p1, body, 0)
    def attend_back(s, l, p0, p1):
        ms = s.masks()
        def body(p, c):
            n = pl.ds(pl.multiple_of(p * 128, 128), 128)
            kk, vv = s.t[1, :, n], s.t[2, :, n]
            kt = kk.T
            dv = jnp.zeros((ROWS, 128), F32)
            dk = jnp.zeros((ROWS, 128), F32)
            for b in range(2):
                q = pl.ds(256 * b, 256)
                qs = s.t[0, q, n] * 0.125
                do = s.do[q, n]
                dq = []
                for i in range(2):
                    qm, dm = qs * ms[i], do * ms[i]
                    pt = jnp.exp(mm(kk, qm, NT) - s.lse[l, pl.ds(2 * p + i, 1), q])
                    dp = mm(vv, dm, NT)
                    dv = dv + mm(pt.astype(BF), dm)
                    ds = (pt * (dp - jnp.sum(pt * dp, axis=0, keepdims=True))).astype(BF)
                    dk = dk + mm(ds, qm)
                    dq.append(mm(kt[64 * i:64 * i + 64], ds) * 0.125)
                s.dt[0, q, n] = jnp.concatenate(dq, axis=0).T.astype(BF)
            s.dt[1, :, n] = dk.astype(BF)
            s.dt[2, :, n] = dv.astype(BF)
            return c
        lax.fori_loop(p0, p1, body, 0)
    def attn_out(s, l):
        def body(i, c):
            q = pl.ds(pl.multiple_of((i // 3) * 256, 256), 256)
            n = pl.ds(pl.multiple_of(lax.rem(i, 3) * 256, 256), 256)
            s.x[q, n] = s.x[q, n] + (mm(s.o[q, :], s.wtile(l, 3, n)) + s.V[pl.ds(r_bias(l, 3), 1), n])
            return c
        lax.fori_loop(0, 6, body, 0)
    def mlp_in(s, l, k):
        def body(i, c):
            q = pl.ds(pl.multiple_of((i // 2) * 256, 256), 256)
            f = lax.rem(i, 2)
            n = pl.ds(pl.multiple_of(f * 384, 128), 384)
            z = mm(s.h2[q, :], s.wtile(l, 4 + k, n)) + s.V[pl.ds(r_fcb(l, k), 1), n]
            a, d = gelu_parts(z)
            a, d = a.astype(BF), d.astype(BF)
            at = pl.ds(pl.multiple_of((2 * k + f) * 128, 128), 128)
            for j in range(3):
                s.g[j, q, at] = a[:, 128 * j:128 * j + 128]
                s.gp[j, q, at] = d[:, 128 * j:128 * j + 128]
            return c
        lax.fori_loop(0, 4, body, 0)
    def mlp_out(s, l, j, to):
        def body(i, c):
            q = pl.ds(pl.multiple_of((i // 3) * 256, 256), 256)
            n = pl.ds(pl.multiple_of(lax.rem(i, 3) * 256, 256), 256)
            w = s.wd[l, j, :, :, :, n].reshape(1024, 256)
            v = mm(s.g[j, q, :], w)
            if j == 0:
                v = v + s.V[pl.ds(r_bias(l, 5), 1), n]
            to[q, n] = s.x[q, n] + v
            return c
        lax.fori_loop(0, 6, body, 0)
    def start_back(s, l):
        def run(j, c):
            q = pl.ds(pl.multiple_of(j * 64, 64), 64)
            eb = s.x[q, :].astype(BF)
            s.du[q, :] = eb
            return c + jnp.sum(eb.astype(F32), axis=0, keepdims=True)
        s.S[pl.ds(r_bias(l, 5), 1), :] = lax.fori_loop(0, ROWS // 64, run, jnp.zeros((1, WIDTH), F32))
    def mlp_out_back(s, l, j):
        def body(i, c):
            f = 2 * i
            w = s.wd[l, j, i].reshape(256, WIDTH)
            n = pl.ds(pl.multiple_of(i * 256, 256), 256)
            tot = jnp.zeros((1, 256), F32)
            for b in range(2):
                q = pl.ds(256 * b, 256)
                dz = (mm(s.du[q, :], w, NT) * s.gp[j, q, n].astype(F32)).astype(BF)
                s.gp[j, q, n] = dz
                tot = tot + jnp.sum(dz.astype(F32), axis=0, keepdims=True)
            s.bz[pl.ds(3 * l + j, 1), n] = tot
            gr = mm(s.g[j, :, n], s.du[...], TN).astype(BF)
            s.wd[l, j, i] = gr.reshape(2, 128, WIDTH)
            return c
        lax.fori_loop(0, 4, body, 0)
    def hidden_bias(s):
        for l in range(2):
            for j in range(3):
                for f in range(8):
                    s.S[pl.ds(r_fcb(l, f // 2), 1), pl.ds(384 * (f % 2) + 128 * j, 128)] = s.bz[pl.ds(3 * l + j, 1), pl.ds(128 * f, 128)]
    def dz_tile(s, k, q):
        parts = []
        for f in range(2):
            for j in range(3):
                parts.append(s.gp[j, q, pl.ds((2 * k + f) * 128, 128)])
        return jnp.concatenate(parts, axis=1)
    def back_mm(s, l, k, get, lhs, first):
        def body(i, c):
            q = pl.ds(pl.multiple_of(lax.rem(i, 2) * 256, 256), 256)
            z = i // 2
            w = s.wa[l, k, pl.ds(z * 2, 2)].reshape(384, WIDTH)
            n = pl.ds(pl.multiple_of(z * 384, 128), 384)
            v = mm(get(q), w, NT)
            s.acc[q, n] = v if first else s.acc[q, n] + v
            return c
        lax.fori_loop(0, 4, body, 0)
        s.grad_a(l, k, get, lhs)
    def grad_a(s, l, k, get, lhs):
        def body(i, c):
            n = pl.ds(pl.multiple_of(i * 384, 128), 384)
            gr = mm(lhs[:, n], get(slice(None)), TN).astype(BF)
            s.wa[l, k, pl.ds(i * 2, 2)] = gr.reshape(2, 2, 96, WIDTH)
            return c
        lax.fori_loop(0, 2, body, 0)
    def attn_out_back(s, l):
        def body(i, c):
            q = pl.ds(pl.multiple_of(lax.rem(i, 2) * 256, 256), 256)
            z = i // 2
            w = s.wa[l, 3, pl.ds(z * 2, 2)].reshape(384, WIDTH)
            n = pl.ds(pl.multiple_of(z * 384, 128), 384)
            s.do[q, n] = mm(s.du[q, :], w, NT).astype(BF)
            return c
        lax.fori_loop(0, 4, body, 0)
        s.grad_a(l, 3, lambda q: s.du[q, :], s.o)
    def col_sum(s, ref, r):
        def run(j, c):
            q = pl.ds(pl.multiple_of(j * 128, 128), 128)
            return c + jnp.sum(ref[q, :].astype(F32), axis=0, keepdims=True)
        s.S[pl.ds(r, 1), :] = lax.fori_loop(0, 4, run, jnp.zeros((1, WIDTH), F32))

def net_scratch():
    V = pltpu.VMEM
    return dict(x=V((512, 768), F32), acc=V((512, 768), F32), h=V((512, 768), BF), t=V((3, 512, 768), BF), lse=V((2, 16, 512), F32),
        o=V((512, 768), BF), h2=V((512, 768), BF), g=V((3, 512, 1024), BF), gp=V((3, 512, 1024), BF), xh1=V((512, 768), BF), xh2=V((512, 768), BF),
        rs1=V((2, 512, 1), F32), rs2=V((2, 512, 1), F32), du=V((512, 768), BF), do=V((512, 768), BF), dt=V((3, 512, 768), BF),
        bz=V((8, 1024), F32), V=V((32, 768), F32), S=V((32, 768), F32))
SPILL = ["h", "t", "o", "h2", "g", "gp", "xh1", "xh2"]


SMALL = (32, 768)
VMEM_LIMIT = 63 * 1024 * 1024


class Smalls:
    def __init__(s, p, net, b):
        s.p, s.net, s.b = p, net, b
    def fetch(s, d):
        b, p = s.b, s.p
        return remote(b["sm"].at[p.fs], b["sm"].at[p.fs], b["ss"].at[d - 1], b["rs"].at[d - 1], p.dev_f(d))
    def start(s):
        for d in range(1, 8):
            s.fetch(d).start()
    def build(s):
        for d in range(1, 8):
            s.fetch(d).wait()
        P = s.b["wide"]
        for f in range(8):
            blk = s.b["sm"][f].astype(F32)
            P[0:24, 128 * f:128 * f + 128] = blk[0:24]
            for l in range(2):
                for r in range(4):
                    at = 4 * (f % 2) + r
                    P[24 + 4 * l + f // 2:25 + 4 * l + f // 2, 128 * at:128 * at + 128] = blk[24 + 4 * l + r:25 + 4 * l + r]
        i = lax.broadcasted_iota(jnp.int32, (128, 768), 0)
        c = lax.broadcasted_iota(jnp.int32, (128, 768), 1)
        total = jnp.zeros(SMALL, F32)
        for b in range(8):
            pick = jnp.where((c - 96 * b == i) & (i < 96), 1.0, 0.0).astype(BF)
            total = total + mm(P[:, 128 * b:128 * b + 128].astype(BF), pick)
        s.net.V[...] = total
    def hop(s, h):
        b, p, S = s.b, s.p, s.net.S
        if h < 3:
            return [remote(S, b["sr"].at[h], b["ss"].at[7 + h], b["rs"].at[7 + h], (p.dev_c, p.dev_x, p.dev_y)[h])]
        return [remote(S, b["sr"].at[3 + d], b["ss"].at[10 + d], b["rs"].at[10 + d], p.dev_z(d + 1)) for d in range(3)]
    def send(s, h):
        for q in s.hop(h): q.start()
    def add(s, h):
        for q in s.hop(h): q.wait()
        t = s.net.S[...]
        for i in ([h] if h < 3 else [3, 4, 5]):
            t = t + s.b["sr"][i]
        s.net.S[...] = t


def smalls_scratch():
    return dict(sm=pltpu.VMEM((8, 32, 128), BF), wide=pltpu.VMEM((32, 1024), F32), sr=pltpu.VMEM((6, 32, 768), F32),
        ss=pltpu.SemaphoreType.DMA((13,)), rs=pltpu.SemaphoreType.DMA((13,)))


def whole_kernel(tok, cot, msk, pack, ai, ao, fi, fo, act, ig, so, oa, od, *rest):
    spill = dict(zip(SPILL, rest[:8]))
    sc, wa, wd, fa, fd, rbufs, sbufs, lsem, ssem, iosem, gss, grs, rss, rrs = rest[8:]
    p = Pos()
    n = Net(dict(sc, wa=wa, wd=wd))
    sm = Smalls(p, n, sbufs)
    tok_in = pltpu.make_async_copy(tok, n.du, iosem.at[0])
    cot_in = pltpu.make_async_copy(cot, n.do, iosem.at[1])
    own = pltpu.make_async_copy(pack, sbufs["sm"].at[p.fs], iosem.at[2])
    loads = load_shards(p, ai, ao, fi, fo, wa, wd, lsem)
    own.start()
    for c in loads: c.start()
    tok_in.start(); cot_in.start()
    own.wait()
    for c in loads: c.wait()
    barrier(p)
    g = Gather(p, unit_views(wa, wd, 0) + unit_views(wa, wd, 1), gss, grs, 2, 2)
    sm.start()
    g.start()
    sm.build()
    tok_in.wait()

    def embed(q):
        m = msk[q, :]
        n.x[q, :] = n.du[q, :].astype(F32) * (1.0 - m) + m * row(n.V, R_EMBED)
    rows_loop(64, embed)

    out_of = lambda nm: pltpu.make_async_copy(sc[nm], spill[nm], ssem.at[SPILL.index(nm)])
    back_to = lambda nm: pltpu.make_async_copy(spill[nm], sc[nm], ssem.at[SPILL.index(nm)])
    for l in range(2):
        def reuse(*nms):
            if l == 1:
                for m in nms: out_of(m).wait()
        def keep(*nms):
            if l == 0:
                for m in nms: out_of(m).start()
        reuse("xh1", "h")
        n.norm(l, 0, n.xh1, n.rs1, n.h)
        keep("xh1")
        reuse("t")
        for k in range(3):
            g.until(11 * l + k)
            n.project(l, k)
        keep("h", "t")
        reuse("o")
        for a in range(0, 6, 3):
            n.attend(l, a, a + 3)
            g.pump()
        keep("o")
        g.until(11 * l + 3)
        n.attn_out(l)
        reuse("xh2", "h2")
        n.norm(l, 1, n.xh2, n.rs2, n.h2)
        keep("xh2")
        reuse("g", "gp")
        for k in range(4):
            g.until(11 * l + 4 + k)
            n.mlp_in(l, k)
        keep("h2", "gp")
        for j in range(3):
            g.until(11 * l + 8 + j)
            n.mlp_out(l, j, n.acc if (l == 1 and j == 2) else n.x)
        keep("g")
    act_out = pltpu.make_async_copy(n.acc, act, iosem.at[0])
    act_out.start()
    cot_in.wait()

    def start_grad(q):
        n.x[q, :] = n.do[q, :].astype(F32)
    rows_loop(64, start_grad)
    n.S[...] = jnp.zeros(SMALL, F32)
    r = Reduce(p, reduce_units(wa, wd, fa, fd, oa, od), rbufs, rss, rrs, 2, 1)
    for l in (1, 0):
        def need(*nms):
            if l == 0:
                for m in nms: back_to(m).wait()
        def done(*nms):
            if l == 1:
                for m in nms: back_to(m).start()
        n.start_back(l)
        need("gp", "g")
        for j in range(3):
            n.mlp_out_back(l, j)
            r.pump()
        done("g")
        need("h2")
        if l == 1:
            act_out.wait()
        for k in range(4):
            n.back_mm(l, 4 + k, lambda q: n.dz_tile(k, q), n.h2, k == 0)
            r.pump()
        done("gp", "h2")
        need("xh2")
        sums = n.norm_back(l, 1, n.acc, n.xh2, n.rs2, n.du)
        n.S[pl.ds(r_bias(l, 3), 1), :] = sums
        done("xh2")
        need("o")
        n.attn_out_back(l)
        r.pump()
        done("o")
        need("t")
        for a in range(0, 6, 3):
            n.attend_back(l, a, a + 3)
            r.pump(False)
        done("t")
        need("h")
        n.col_sum(n.dt.at[0], r_bias(l, 1))
        n.col_sum(n.dt.at[2], r_bias(l, 2))
        for k in range(3):
            n.back_mm(l, k, lambda q: n.dt[k, q, :], n.h, k == 0)
            r.pump()
        done("h")
        need("xh1")
        n.norm_back(l, 0, n.acc, n.xh1, n.rs1, None)
        done("xh1")
    n.hidden_bias()

    def finish(j, c):
        q = pl.ds(pl.multiple_of(j * 64, 64), 64)
        m, e = msk[q, :], n.x[q, :]
        n.acc[q, :] = e * (1.0 - m)
        return c + jnp.sum(e * m, axis=0, keepdims=True)
    n.S[pl.ds(R_EMBED, 1), :] = lax.fori_loop(0, ROWS // 64, finish, jnp.zeros((1, WIDTH), F32))
    ig_out = pltpu.make_async_copy(n.acc, ig, iosem.at[1])
    ig_out.start()
    for h in range(4):
        sm.send(h)
        r.pump(False)
        sm.add(h)
    s_out = pltpu.make_async_copy(n.S, so, iosem.at[2])
    s_out.start()
    r.finish()
    ig_out.wait()
    s_out.wait()


def whole(tok, cot, msk, pack, ai, ao, fi, fo):
    net = net_scratch()
    any_, vm = pl.BlockSpec(memory_space=pl.ANY), pl.BlockSpec(memory_space=pltpu.VMEM)
    sa, sd = (2, 8, 4, 2, 96, 768), (2, 3, 4, 2, 128, 768)
    fa, fd = (2, 8, 96, 768), (2, 3, 128, 768)
    shapes = [((512, 768), F32), ((512, 768), F32), (SMALL, F32), (fa, BF), (fd, BF)] + [(net[k].shape, net[k].dtype) for k in SPILL]
    dma = pltpu.SemaphoreType.DMA
    return pl.pallas_call(
        whole_kernel,
        out_shape=[jax.ShapeDtypeStruct(*v) for v in shapes],
        in_specs=[any_, any_, vm, any_] + [any_] * 4,
        out_specs=[any_] * len(shapes),
        scratch_shapes=[
            net, pltpu.VMEM(sa, BF), pltpu.VMEM(sd, BF), pltpu.VMEM(fa, BF), pltpu.VMEM(fd, BF),
            reduce_scratch(2, 1), smalls_scratch(), dma((22,)), dma((8,)), dma((3,)),
            dma((22, 6)), dma((22, 6)), dma((4, 10)), dma((4, 10)),
        ],
        compiler_params=pltpu.CompilerParams(collective_id=0, has_side_effects=True, vmem_limit_bytes=VMEM_LIMIT),
    )(tok, cot, msk, pack, ai, ao, fi, fo)[:5]


def fused_local(tokens, mask, cotangent, mask_embed, attn_in, attn_out, fc_in, fc_out, gains, biases, fc_bias):
    pack = jnp.concatenate([gains.reshape(4, 96), biases.reshape(12, 96), mask_embed.reshape(1, 96), jnp.zeros((7, 96), BF), fc_bias.reshape(8, 96)], axis=0)
    pack = jnp.pad(pack, ((0, 0), (0, 32)))
    act, ig, small, oa, od = whole(tokens, cotangent, mask.astype(F32)[:, None], pack, attn_in, attn_out, fc_in, fc_out)
    back = lambda o: o.transpose(0, 2, 1, 3).reshape(2, 96, -1).astype(F32)
    f = lax.axis_index("fsdp")
    own = lax.dynamic_slice(small, (0, f * 96), (17, 96))
    fb = lax.dynamic_slice(small[24:32].reshape(2, 3072), (0, f * 384), (2, 384))
    return (
        act, ig, own[16], back(oa[:, 0:3]), oa[:, 3].astype(F32), back(oa[:, 4:8]),
        od.reshape(2, 384, 768).astype(F32), own[0:4].reshape(2, 2, 96), own[4:16].reshape(2, 6, 96), fb)


def solution(mesh):
    if dict(mesh.shape) != {"dp": 4, "fsdp": 8}:
        return generic_solution(mesh)
    rows = P(("dp", "fsdp"), None)
    mat = P(None, "fsdp", None)
    vec = P(None, None, "fsdp")
    return jax.shard_map(
        fused_local, mesh=mesh,
        in_specs=(rows, P(("dp", "fsdp")), rows, P("fsdp"), mat, mat, mat, mat, vec, vec, P(None, "fsdp")),
        out_specs=(rows, rows, P("fsdp"), mat, mat, mat, mat, vec, vec, P(None, "fsdp")),
        check_vma=False)


HEADS = 12
SEQ = 512
LAYERS = 2


eps = 1e-06


def norm_rows(values, gain, bias):
    center = values - jnp.mean(values, axis=-1, keepdims=True)
    spread = jnp.mean(center * center, axis=-1, keepdims=True)
    return center * lax.rsqrt(spread + eps) * gain + bias


def gelu_exact(values):
    return jax.nn.gelu(values, approximate=False)


def split_heads(values, clips):
    width = values.shape[1]
    return values.reshape(clips, SEQ, HEADS, width // HEADS)


def attend(pack):
    query, key_rows, value = pack
    scale = query.shape[-1] ** (-0.5)
    scores = jnp.einsum("qhd,khd->hqk", query, key_rows, preferred_element_type=jnp.float32) * scale
    top = jnp.max(scores, axis=-1, keepdims=True)
    expo = jnp.exp(scores - top)
    total = jnp.sum(expo, axis=-1, keepdims=True)
    probs = (expo / total).astype(jnp.bfloat16)
    mixed = jnp.einsum("hqk,khd->qhd", probs, value, preferred_element_type=jnp.float32)
    return (mixed, top + jnp.log(total))


def attend_back(pack):
    query, key_rows, value, logsum, d_mixed = pack
    scale = query.shape[-1] ** (-0.5)
    scores = jnp.einsum("qhd,khd->hqk", query, key_rows, preferred_element_type=jnp.float32) * scale
    probs = jnp.exp(scores - logsum)
    d_probs = jnp.einsum("qhd,khd->hqk", d_mixed, value, preferred_element_type=jnp.float32)
    d_value = jnp.einsum(
        "hqk,qhd->khd", probs.astype(jnp.bfloat16), d_mixed, preferred_element_type=jnp.float32
    )
    d_scores = probs * (d_probs - jnp.sum(probs * d_probs, axis=-1, keepdims=True))
    d_scaled = d_scores.astype(jnp.bfloat16) * scale
    d_query = jnp.einsum("hqk,khd->qhd", d_scaled, key_rows, preferred_element_type=jnp.float32)
    d_key = jnp.einsum("hqk,qhd->khd", d_scaled, query, preferred_element_type=jnp.float32)
    return (d_query, d_key, d_value)


def layer_forward(state, weights):
    w_qkv, w_out, w_in, w_down, gain, bias, fcb = weights
    rows, width = state.shape
    clips = rows // SEQ
    normed = norm_rows(state, gain[0].astype(jnp.float32), bias[0].astype(jnp.float32)).astype(
        jnp.bfloat16
    )
    qkv_bias = jnp.concatenate([bias[1], jnp.zeros_like(bias[1]), bias[2]]).astype(jnp.float32)
    joined = (jnp.dot(normed, w_qkv, preferred_element_type=jnp.float32) + qkv_bias).astype(
        jnp.bfloat16
    )
    query = split_heads(joined[:, :width], clips)
    key_rows = split_heads(joined[:, width : 2 * width], clips)
    value = split_heads(joined[:, 2 * width :], clips)
    mixed, logsum = lax.map(attend, (query, key_rows, value))
    mixed = mixed.reshape(rows, width).astype(jnp.bfloat16)
    middle = (
        state
        + jnp.dot(mixed, w_out, preferred_element_type=jnp.float32)
        + bias[3].astype(jnp.float32)
    )
    normed_two = norm_rows(middle, gain[1].astype(jnp.float32), bias[4].astype(jnp.float32)).astype(
        jnp.bfloat16
    )
    hidden = jnp.dot(normed_two, w_in, preferred_element_type=jnp.float32) + fcb.astype(jnp.float32)
    activated = gelu_exact(hidden).astype(jnp.bfloat16)
    return (normed, query, key_rows, value, logsum, mixed, middle, normed_two, hidden, activated)


def layer_finish(saved, weights):
    middle = saved[6]
    activated = saved[9]
    return (
        middle
        + jnp.dot(activated, weights[3], preferred_element_type=jnp.float32)
        + weights[5][5].astype(jnp.float32)
    )


def layer_backward(state, weights, grad):
    w_qkv, w_out, w_in, w_down, gain, bias, fcb = weights
    rows, width = state.shape
    clips = rows // SEQ
    normed, query, key_rows, value, logsum, mixed, middle, normed_two, hidden, activated = (
        layer_forward(state, weights)
    )
    d_up = grad.astype(jnp.bfloat16)
    g_down = jnp.einsum("tf,td->fd", activated, d_up, preferred_element_type=jnp.float32)
    d_two = jnp.sum(d_up.astype(jnp.float32), axis=0)
    d_act = jnp.einsum("td,fd->tf", d_up, w_down, preferred_element_type=jnp.float32)
    d_hidden = jax.vjp(gelu_exact, hidden)[1](d_act)[0].astype(jnp.bfloat16)
    g_in = jnp.einsum("td,tf->df", normed_two, d_hidden, preferred_element_type=jnp.float32)
    d_one = jnp.sum(d_hidden.astype(jnp.float32), axis=0)
    d_normed_two = jnp.einsum("tf,df->td", d_hidden, w_in, preferred_element_type=jnp.float32)
    back_two = jax.vjp(norm_rows, middle, gain[1].astype(jnp.float32), bias[4].astype(jnp.float32))[
        1
    ]
    d_middle, d_gain_two, d_bias_two = back_two(d_normed_two)
    d_middle = grad + d_middle
    d_branch = d_middle.astype(jnp.bfloat16)
    g_out = jnp.einsum("td,te->de", mixed, d_branch, preferred_element_type=jnp.float32)
    d_outb = jnp.sum(d_branch.astype(jnp.float32), axis=0)
    d_mixed = jnp.einsum("te,de->td", d_branch, w_out, preferred_element_type=jnp.float32).astype(
        jnp.bfloat16
    )
    d_query, d_key, d_value = lax.map(
        attend_back, (query, key_rows, value, logsum, split_heads(d_mixed, clips))
    )
    d_joined = jnp.concatenate(
        [d_query.reshape(rows, width), d_key.reshape(rows, width), d_value.reshape(rows, width)],
        axis=1,
    ).astype(jnp.bfloat16)
    g_qkv = jnp.einsum("td,te->de", normed, d_joined, preferred_element_type=jnp.float32)
    d_sums = jnp.sum(d_joined.astype(jnp.float32), axis=0)
    d_normed = jnp.einsum("te,de->td", d_joined, w_qkv, preferred_element_type=jnp.float32)
    back_one = jax.vjp(norm_rows, state, gain[0].astype(jnp.float32), bias[0].astype(jnp.float32))[
        1
    ]
    d_state, d_gain_one, d_bias_one = back_one(d_normed)
    gain_terms = jnp.stack([d_gain_one, d_gain_two])
    bias_terms = jnp.stack(
        [d_bias_one, d_sums[:width], d_sums[2 * width :], d_outb, d_bias_two, d_two]
    )
    return (d_middle + d_state, (g_qkv, g_out, g_in, g_down, gain_terms, bias_terms, d_one))


def local(
    tokens, mask, cotangent, mask_embed, attn_in, attn_out, fc_in, fc_out, gains, biases, fc_bias
):
    mask_f = mask.astype(jnp.float32)[:, None]
    state = tokens.astype(jnp.float32)
    stored = []
    kept = []
    for layer in range(LAYERS):
        fetched = (
            lax.all_gather(attn_in[layer], "fsdp", axis=0, tiled=True),
            lax.all_gather(attn_out[layer], "fsdp", axis=0, tiled=True),
            lax.all_gather(fc_in[layer], "fsdp", axis=0, tiled=True),
            lax.all_gather(fc_out[layer], "fsdp", axis=0, tiled=True),
            lax.all_gather(gains[layer], "fsdp", axis=1, tiled=True),
            lax.all_gather(biases[layer], "fsdp", axis=1, tiled=True),
            lax.all_gather(fc_bias[layer], "fsdp", axis=0, tiled=True),
            lax.all_gather(mask_embed, "fsdp", axis=0, tiled=True),
        )
        if layer == 0:
            state = state * (1.0 - mask_f) + mask_f * fetched[7].astype(jnp.float32)
        stored.append(state)
        weights = tuple(fetched[:7])
        kept.append(weights)
        state = layer_finish(layer_forward(state, weights), weights)
    grad = cotangent.astype(jnp.float32)
    layer_grads = [None] * LAYERS
    for layer in reversed(range(LAYERS)):
        weights = tuple(
            (
                lax.all_gather(attn_in[layer], "fsdp", axis=0, tiled=True),
                lax.all_gather(attn_out[layer], "fsdp", axis=0, tiled=True),
                lax.all_gather(fc_in[layer], "fsdp", axis=0, tiled=True),
                lax.all_gather(fc_out[layer], "fsdp", axis=0, tiled=True),
                lax.all_gather(gains[layer], "fsdp", axis=1, tiled=True),
                lax.all_gather(biases[layer], "fsdp", axis=1, tiled=True),
                lax.all_gather(fc_bias[layer], "fsdp", axis=0, tiled=True),
            )
        )
        grad, terms = layer_backward(stored[layer], weights, grad)
        if layer == 0:
            mask_term = jnp.sum(grad * mask_f, axis=0)
        else:
            mask_term = jnp.zeros((grad.shape[1],), jnp.float32)
        shares = (
            lax.psum_scatter(terms[0], "fsdp", scatter_dimension=0, tiled=True),
            lax.psum_scatter(terms[1], "fsdp", scatter_dimension=0, tiled=True),
            lax.psum_scatter(terms[2], "fsdp", scatter_dimension=0, tiled=True),
            lax.psum_scatter(terms[3], "fsdp", scatter_dimension=0, tiled=True),
            lax.psum_scatter(terms[4], "fsdp", scatter_dimension=1, tiled=True),
            lax.psum_scatter(terms[5], "fsdp", scatter_dimension=1, tiled=True),
            lax.psum_scatter(terms[6], "fsdp", scatter_dimension=0, tiled=True),
            lax.psum_scatter(mask_term, "fsdp", scatter_dimension=0, tiled=True),
        )
        slices = (
            lax.psum_scatter(
                shares[0].astype(jnp.bfloat16), "dp", scatter_dimension=1, tiled=True
            ).astype(jnp.float32),
            lax.psum_scatter(
                shares[1].astype(jnp.bfloat16), "dp", scatter_dimension=1, tiled=True
            ).astype(jnp.float32),
            lax.psum_scatter(
                shares[2].astype(jnp.bfloat16), "dp", scatter_dimension=1, tiled=True
            ).astype(jnp.float32),
            lax.psum_scatter(
                shares[3].astype(jnp.bfloat16), "dp", scatter_dimension=1, tiled=True
            ).astype(jnp.float32),
        )
        matrices = (
            lax.all_gather(slices[0].astype(jnp.bfloat16), "dp", axis=1, tiled=True).astype(
                jnp.float32
            ),
            lax.all_gather(slices[1].astype(jnp.bfloat16), "dp", axis=1, tiled=True).astype(
                jnp.float32
            ),
            lax.all_gather(slices[2].astype(jnp.bfloat16), "dp", axis=1, tiled=True).astype(
                jnp.float32
            ),
            lax.all_gather(slices[3].astype(jnp.bfloat16), "dp", axis=1, tiled=True).astype(
                jnp.float32
            ),
        )
        smalls = lax.psum((shares[4], shares[5], shares[6], shares[7]), "dp")
        layer_grads[layer] = (
            matrices[0],
            matrices[1],
            matrices[2],
            matrices[3],
            smalls[0],
            smalls[1],
            smalls[2],
            smalls[3],
        )
    input_grad = grad * (1.0 - mask_f)
    stacked = [jnp.stack([layer_grads[lay][item] for lay in range(LAYERS)]) for item in range(7)]
    results = tuple(stacked) + (layer_grads[0][7],)
    return (
        state,
        input_grad,
        results[7],
        results[0],
        results[1],
        results[2],
        results[3],
        results[4],
        results[5],
        results[6],
    )


def generic_solution(mesh):
    placed = (
        P(("dp", "fsdp"), None),
        P(("dp", "fsdp")),
        P(("dp", "fsdp"), None),
        P("fsdp"),
        P(None, "fsdp", None),
        P(None, "fsdp", None),
        P(None, "fsdp", None),
        P(None, "fsdp", None),
        P(None, None, "fsdp"),
        P(None, None, "fsdp"),
        P(None, "fsdp"),
    )
    return jax.shard_map(
        local,
        mesh=mesh,
        in_specs=placed,
        out_specs=(
            P(("dp", "fsdp"), None),
            P(("dp", "fsdp"), None),
            P("fsdp"),
            P(None, "fsdp", None),
            P(None, "fsdp", None),
            P(None, "fsdp", None),
            P(None, "fsdp", None),
            P(None, None, "fsdp"),
            P(None, None, "fsdp"),
            P(None, "fsdp"),
        ),
        check_vma=False,
    )
```

```python
import functools

import jax
import jax.numpy as jnp
from jax import lax
from jax.experimental import pallas as pl
from jax.experimental.pallas import tpu as pltpu
from jax.sharding import PartitionSpec as P
MESH = pl.DeviceIdType.MESH


class Pos:
    def __init__(s):
        s.dp = lax.axis_index("dp"); s.fs = lax.axis_index("fsdp")
        s.x = s.dp // 2; s.c = lax.rem(s.dp, 2)
        s.z = s.fs // 2; s.y = lax.rem(s.fs, 2)
        s.dev_c = (s.dp + 1 - 2 * s.c, s.fs)
        s.dev_x = (lax.rem(s.dp + 2, 4), s.fs)
        s.dev_y = (s.dp, s.fs + 1 - 2 * s.y)
        s.edge = (s.z == 0) | (s.z == 3)
        s.mid = (s.z == 1) | (s.z == 2)
    def dev_f(s, d):
        return (s.dp, lax.rem(s.fs + d, 8))
    def dev_at(s, z):
        return (s.dp, 2 * z + s.y)
    def up(s, d):
        return lax.rem(s.z + d, 4)
    def far(s):
        return jnp.where(s.edge, 3 - s.z, 6 - 3 * s.z)


def when(cond, f):
    if cond is None:
        f()
    else:
        pl.when(cond)(f)


class Move:
    def __init__(s, src, dst, ss, rs, dev, sends=None, takes=None):
        s.copy = pltpu.make_async_remote_copy(src_ref=src, dst_ref=dst, send_sem=ss, recv_sem=rs, device_id=dev, device_id_type=MESH)
        s.sends, s.takes = sends, takes
    def start(s):
        when(s.sends, s.copy.start)
    def sent(s):
        when(s.sends, s.copy.wait_send)
    def got(s):
        when(s.takes, s.copy.wait_recv)
    def wait(s):
        s.sent(); s.got()


def barrier(p):
    bar = pltpu.get_barrier_semaphore()
    devs = [p.dev_c, p.dev_x] + [p.dev_f(d) for d in range(1, 8)]
    for d in devs:
        pl.semaphore_signal(bar, inc=1, device_id=d, device_id_type=MESH)
    pl.semaphore_wait(bar, len(devs))


class Op:
    def __init__(s, start, finish, traffic, deps=(), cost=0.1, rank=0):
        s.start, s.finish, s.traffic, s.cost, s.rank = start, finish, traffic, cost, rank
        s.deps = [d for d in deps if d is not None]
        s.begun = s.ended = False
        s.ready = None


class Plan:
    RATE = dict(x=46e3, y=46e3, m=46e3, e=46e3, g=46e3, c=600e3)
    LATENCY = 1.7
    BACKLOG = 4.0
    def __init__(s):
        s.ops, s.steps = [], []
        s.free = {k: 0.0 for k in s.RATE}
    def op(s, *a, **k):
        s.ops.append(Op(*a, **k))
        return s.ops[-1]
    def step(s, fn, cost, needs=(), opens=()):
        s.steps.append((fn, cost, [n for n in needs if n is not None], list(opens)))
    def mark(s):
        m = Op(None, None, {}); m.begun = True
        return m
    def run(s):
        now, k, waiting, flying = 0.0, 0, list(s.ops), []
        def launch(force=False):
            nonlocal waiting
            rest = []
            for o in sorted(waiting, key=lambda o: o.rank):
                ok = all(d.ended for d in o.deps)
                if ok and (force or all(s.free[r] - now < s.BACKLOG for r in o.traffic)):
                    force = False
                    o.start()
                    end = now
                    for r, v in o.traffic.items():
                        s.free[r] = max(s.free[r], now) + v / s.RATE[r]
                        end = max(end, s.free[r])
                    o.ready = end + s.LATENCY
                    flying.append(o)
                else:
                    rest.append(o)
            waiting = rest
        launch()
        while k < len(s.steps) or flying or waiting:
            flying.sort(key=lambda o: o.ready)
            can = k < len(s.steps) and all(n.ended for n in s.steps[k][2])
            if flying and (flying[0].ready <= now or not can):
                o = flying.pop(0)
                now = max(now, o.ready) + o.cost
                o.finish(); o.ended = True
            elif can:
                fn, cost, needs, opens = s.steps[k]; k += 1
                fn(); now += cost
                for m in opens: m.ended = True
            launch(not flying)
        return now


class Gather:
    def __init__(s, p, units, ssem, rsem, lead=3):
        s.p, s.units, s.ss, s.rs, s.lead = p, units, ssem, rsem, lead
        s.n = len(units)
    def move(s, u, i, block, dev, sends=None, takes=None):
        return Move(block, block, s.ss.at[u, i], s.rs.at[u, i], dev, sends, takes)
    def geo(s, u):
        w, yfirst = s.units[u]
        p, R = s.p, w.shape[2] // 2
        rc = pl.ds(pl.multiple_of(p.c * R, 16), R)
        wide = pl.ds(pl.multiple_of(p.x * 256, 256), 512)
        mine = pl.ds(pl.multiple_of(p.x * 512, 256), 256)
        return w, yfirst, rc, wide, mine
    def near(s, u):
        w, yfirst, rc, wide, mine = s.geo(u); p = s.p
        ys = slice(None) if yfirst else p.y
        b = w.at[p.z, ys, rc, wide]
        return [s.move(u, 0, b, p.dev_at(p.up(1)), p.z < 3, p.z > 0), s.move(u, 1, b, p.dev_at(p.up(2))),
            s.move(u, 2, b, p.dev_at(p.up(3)), p.z > 0, p.z < 3)]
    def relay(s, u):
        w, yfirst, rc, wide, mine = s.geo(u); p = s.p
        ys = slice(None) if yfirst else p.y
        return [s.move(u, 3, w.at[p.far(), ys, rc, wide], p.dev_at(jnp.where(p.edge, p.z, 3 * p.z - 3)), p.mid, p.edge)]
    def over_y(s, u):
        w, yfirst, rc, wide, mine = s.geo(u); p = s.p
        if yfirst:
            return [s.move(u, 4, w.at[p.z, p.y, rc, wide], p.dev_y)]
        return [s.move(u, 4, w.at[:, p.y, rc, wide], p.dev_y, p.mid, p.mid),
            s.move(u, 4, w.at[pl.ds(p.z // 3, 3), p.y, rc, wide], p.dev_y, p.edge, p.edge)]
    def over_y_far(s, u):
        w, yfirst, rc, wide, mine = s.geo(u); p = s.p
        return [s.move(u, 5, w.at[p.far(), p.y, rc, wide], p.dev_y, p.edge, p.edge)]
    def over_x(s, u):
        w, yfirst, rc, wide, mine = s.geo(u); p = s.p
        return [s.move(u, 6, w.at[:, 1 - p.y, rc, mine], p.dev_x)]
    def over_x_own(s, u):
        w, yfirst, rc, wide, mine = s.geo(u); p = s.p
        return [s.move(u, 6 + d, w.at[p.up(d), p.y, rc, mine], p.dev_x) for d in (1, 2, 3)]
    def over_c(s, u):
        w, yfirst, rc, wide, mine = s.geo(u); p = s.p
        return [s.move(u, 10, w.at[:, :, rc, :], p.dev_c)]
    def plan(s, P, gate=None):
        def moves(f):
            def start():
                for m in f(): m.start()
            def finish():
                for m in f(): m.wait()
            return start, finish
        firsts, lasts = [], []
        for u in range(s.n):
            w, yfirst = s.units[u]
            R, b = w.shape[2] // 2, 2 * 256
            piece = R * 2 * b
            first = [gate, firsts[u - s.lead] if u >= s.lead else None]
            f = lambda g, u=u: moves(lambda: g(u))
            if yfirst:
                y = P.op(*f(s.over_y), dict(y=piece), first, rank=u)
                near = P.op(*f(s.near), dict(m=6 * piece, e=4 * piece, g=4 * piece), [y], rank=u)
                rel = P.op(*f(s.relay), dict(g=2 * piece), [near], rank=u)
                x = P.op(*f(lambda u: s.over_x(u) + s.over_x_own(u)), dict(x=7 * R * b), [rel], rank=u)
                c = P.op(*f(s.over_c), dict(c=24 * R * b), [x], rank=u)
                firsts.append(y)
            else:
                near = P.op(*f(s.near), dict(m=3 * piece, e=2 * piece, g=2 * piece), first, rank=u)
                rel = P.op(*f(s.relay), dict(g=piece), [near], rank=u)
                ya = P.op(*f(s.over_y), dict(y=3.5 * piece), [near], rank=u)
                yb = P.op(*f(s.over_y_far), dict(y=0.5 * piece), [rel], rank=u)
                xo = P.op(*f(s.over_x_own), dict(x=3 * R * b), [rel], rank=u)
                xm = P.op(*f(s.over_x), dict(x=4 * R * b), [ya, yb], rank=u)
                c = P.op(*f(s.over_c), dict(c=24 * R * b), [xm, xo], rank=u)
                firsts.append(near)
            lasts.append(c)
        return lasts


class Reduce:
    KINDS = (2, 0, 2, 1)
    def __init__(s, p, units, bufs, ssem, rsem):
        s.p, s.units, s.b, s.ss, s.rs = p, units, bufs, ssem, rsem
        s.n = len(units)
        s.kz = dict(enumerate(("z0", "z1", "z2")))
    def geo(s, u):
        w, fin, out = s.units[u]
        R = w.shape[2] // 2; p = s.p
        rc = pl.ds(pl.multiple_of(p.c * R, 16), R)
        ro = pl.ds(pl.multiple_of((1 - p.c) * R, 16), R)
        xc = pl.ds(pl.multiple_of(p.x * 384, 128), 384)
        xo = pl.ds(pl.multiple_of((1 - p.x) * 384, 128), 384)
        return w, fin, out, R, rc, ro, xc, xo
    def slot(s, u):
        kind = s.KINDS[u % 4]
        return kind, (u // 2) % RING if kind == 2 else (u // 4) % (RING // 2), (u // 2) % RING
    def move(s, u, i, src, dst, dev, sends=None, takes=None):
        k = u % s.ss.shape[0]
        return Move(src, dst, s.ss.at[k, i], s.rs.at[k, i], dev, sends, takes)
    def core(s, u):
        w, fin, out, R, rc, ro, xc, xo = s.geo(u)
        return [s.move(u, 0, w.at[:, :, ro, :], s.b["c"].at[u % CRING, :, :, pl.ds(0, R), :], s.p.dev_c)]
    def add_core(s, u):
        w, fin, out, R, rc, ro, xc, xo = s.geo(u); c = s.b["c"].at[u % CRING]
        def body(i, _):
            a, b = i // 2, lax.rem(i, 2)
            w[a, b, rc, :] = w[a, b, rc, :] + c[a, b, pl.ds(0, R), :]
            return 0
        lax.fori_loop(0, 8, body, 0)
    def first(s, u):
        w, fin, out, R, rc, ro, xc, xo = s.geo(u); p = s.p
        kind, k, k2 = s.slot(u)
        if kind == 2:
            return [s.move(u, 1, w.at[:, 1 - p.y, rc, :], s.b["h1y"].at[k, :, pl.ds(0, R), :], p.dev_y)]
        return [s.move(u, 1, w.at[:, :, rc, xo], s.b["h1x"].at[k2, :, :, pl.ds(0, R), :], p.dev_x)]
    def add_first(s, u):
        w, fin, out, R, rc, ro, xc, xo = s.geo(u); p = s.p
        kind, k, k2 = s.slot(u)
        if kind == 2:
            h = s.b["h1y"].at[k]
            def body(a, _):
                w[a, p.y, rc, :] = w[a, p.y, rc, :] + h[a, pl.ds(0, R), :]
                return 0
            lax.fori_loop(0, 4, body, 0)
        else:
            h = s.b["h1x"].at[k2]
            def body(i, _):
                a, b = i // 2, lax.rem(i, 2)
                w[a, b, rc, xc] = w[a, b, rc, xc] + h[a, b, pl.ds(0, R), :]
                return 0
            lax.fori_loop(0, 8, body, 0)
    def second_y(s, u):
        w, fin, out, R, rc, ro, xc, xo = s.geo(u); p = s.p
        kind, k, k2 = s.slot(u)
        return [s.move(u, 2, w.at[:, 1 - p.y, rc, xc], s.b["h2y"].at[k, :, pl.ds(0, R), :], p.dev_y)]
    def add_second_y(s, u):
        w, fin, out, R, rc, ro, xc, xo = s.geo(u); p = s.p
        kind, k, k2 = s.slot(u)
        h = s.b["h2y"].at[k]
        def body(a, _):
            w[a, p.y, rc, xc] = w[a, p.y, rc, xc] + h[a, pl.ds(0, R), :]
            return 0
        lax.fori_loop(0, 4, body, 0)
    def zblock(s, u, z):
        w, fin, out, R, rc, ro, xc, xo = s.geo(u); p = s.p
        kind, k, k2 = s.slot(u)
        if kind == 1:
            return w.at[z, :, rc, xc]
        return w.at[z, p.y, rc, xc if kind == 0 else slice(None)]
    def zslot(s, u, d):
        kind, k, k2 = s.slot(u); R = s.geo(u)[3]
        b = s.b[s.kz[kind]]
        return b.at[k, d, :, pl.ds(0, R), :] if kind == 1 else b.at[k, d, pl.ds(0, R), :]
    def near(s, u):
        p = s.p
        one = [s.move(u, 2 + d, s.zblock(u, p.up(d)), s.zslot(u, d - 1), p.dev_at(p.up(d)), *((p.z < 3, p.z > 0) if d == 1 else (p.z > 0, p.z < 3))) for d in (1, 3)]
        return [s.far(u)] + one + [s.two(u, p.edge, p.mid)]
    def far(s, u):
        p = s.p
        return s.move(u, 6, s.zblock(u, p.far()), s.zslot(u, 3), p.dev_at(1 + p.z // 3), p.edge, p.mid)
    def two(s, u, sends, takes):
        p = s.p
        return s.move(u, 4, s.zblock(u, p.up(2)), s.zslot(u, 1), p.dev_at(p.up(2)), sends, takes)
    def far_add(s, u):
        m = s.far(u); m.got(); m.sent()
        def add():
            b, h = s.zblock(u, s.p.far()), s.zslot(u, 3)
            b[...] = b[...] + h[...]
        pl.when(s.p.mid)(add)
    def z_sum(s, u):
        f = lambda r: r[...].astype(jnp.float32)
        v = f(s.zblock(u, s.p.z))
        for d in range(3): v = v + f(s.zslot(u, d))
        return v.astype(jnp.bfloat16)
    def last_y(s, u):
        w, fin, out, R, rc, ro, xc, xo = s.geo(u); p = s.p
        kind, k, k2 = s.slot(u)
        return [s.move(u, 7, w.at[p.z, 1 - p.y, rc, xc], s.b["h3y"].at[k, pl.ds(0, R), :], p.dev_y)]
    def last_x(s, u):
        w, fin, out, R, rc, ro, xc, xo = s.geo(u); p = s.p
        kind, k, k2 = s.slot(u)
        return [s.move(u, 7, w.at[p.z, p.y, rc, :], s.b["h3x"].at[k, pl.ds(0, R), :], p.dev_x)]
    def share_x(s, u):
        w, fin, out, R, rc, ro, xc, xo = s.geo(u)
        return [s.move(u, 8, fin.at[rc, xc], fin.at[rc, xc], s.p.dev_x)]
    def share_c(s, u):
        w, fin, out, R, rc, ro, xc, xo = s.geo(u)
        return [s.move(u, 9, fin.at[rc, :], fin.at[rc, :], s.p.dev_c)]
    def out_copy(s, u):
        return pltpu.make_async_copy(s.units[u][1], s.units[u][2], s.b["osem"].at[u])
    def plan(s, P, marks, gate=None):
        def run(ms):
            for m in ms: m.start()
        def wait(ms):
            for m in ms: m.wait()
        core, first, second, zs, last, share, end = [], [], [], [], [], [], []
        def back(ops, u, kinds, ring):
            same = [v for v in range(u) if s.KINDS[v % 4] in kinds]
            return ops[same[-ring // 2]] if len(same) >= ring // 2 else None
        for u in range(s.n):
            w, fin, out, R, rc, ro, xc, xo = s.geo(u); p = s.p
            kind, k, k2 = s.slot(u)
            full = R * 768 * 2
            zb = full if kind != 0 else full // 2
            mine = (kind,) if kind == 2 else (0, 1)
            def f_core(u=u): wait(s.core(u)); s.add_core(u)
            def f_first(u=u): wait(s.first(u)); s.add_first(u)
            def f_second(u=u): wait(s.second_y(u)); s.add_second_y(u)
            def b_near(u=u): run(s.near(u)[1:])
            def f_near(u=u): wait(s.near(u)[1:])
            def b_rel(u=u): s.two(u, s.p.mid, s.p.edge).start()
            def f_z(u=u, w=w, fin=fin, kind=kind, rc=rc, xc=xc):
                s.two(u, s.p.mid, s.p.edge).wait()
                if kind == 0:
                    fin[rc, xc] = s.z_sum(u)
                else:
                    b = s.zblock(u, s.p.z); b[...] = s.z_sum(u)
            def f_last(u=u, w=w, fin=fin, kind=kind, rc=rc, xc=xc, R=R, k=k):
                p = s.p
                if kind == 1:
                    wait(s.last_y(u))
                    fin[rc, xc] = w[p.z, p.y, rc, xc] + s.b["h3y"][k, pl.ds(0, R), :]
                else:
                    wait(s.last_x(u))
                    fin[rc, :] = w[p.z, p.y, rc, :] + s.b["h3x"][k, pl.ds(0, R), :]
            def f_end(u=u): wait(s.share_c(u)); s.out_copy(u).start()
            c = P.op(lambda u=u: run(s.core(u)), f_core, dict(c=8 * full), [marks[u], gate, core[u - CRING // 2] if u >= CRING // 2 else None], cost=0.3, rank=100 + u)
            core.append(c)
            f = P.op(lambda u=u: run(s.first(u)), f_first, dict(y=4 * full) if kind == 2 else dict(x=4 * full), [c, back(first, u, mine, RING)], cost=0.25, rank=100 + u)
            first.append(f)
            prev = f
            if kind == 0:
                prev = P.op(lambda u=u: run(s.second_y(u)), f_second, dict(y=2 * full), [f, back(second, u, (0,), RING // 2)], cost=0.15, rank=100 + u)
            second.append(prev)
            ring = back(zs, u, (kind,), RING if kind == 2 else RING // 2)
            far = P.op(lambda u=u: s.far(u).start(), lambda u=u: s.far_add(u), dict(e=zb), [prev, ring], rank=100 + u)
            near = P.op(b_near, f_near, dict(m=2 * zb, e=2 * zb, g=zb), [prev, ring], rank=100 + u)
            z = P.op(b_rel, f_z, dict(m=zb, g=zb), [far, near], cost=0.15, rank=100 + u)
            zs.append(z)
            prev = z
            if kind != 0:
                prev = P.op((lambda u=u: run(s.last_y(u))) if kind == 1 else (lambda u=u: run(s.last_x(u))), f_last,
                    dict(y=full // 2) if kind == 1 else dict(x=full), [z, back(last, u, (kind,), RING if kind == 2 else RING // 2)], rank=100 + u)
            last.append(prev)
            if kind != 2:
                prev = P.op(lambda u=u: run(s.share_x(u)), lambda u=u: wait(s.share_x(u)), dict(x=full // 2), [prev, back(share, u, (0, 1), RING)], rank=100 + u)
            share.append(prev)
            end.append(P.op(lambda u=u: run(s.share_c(u)), f_end, dict(c=full), [prev, back(end, u, (kind,), RING if kind == 2 else RING // 2)], rank=100 + u))
        return end
    def finish(s):
        for u in range(s.n): s.out_copy(u).wait()
    def clear(s):
        def zero(d):
            def f():
                for q in s.kz.values():
                    b = s.b[q]
                    for k in range(b.shape[0]):
                        b[k, d] = jnp.zeros(b.shape[2:], b.dtype)
            return f
        pl.when(s.p.z == 0)(zero(0))
        pl.when(s.p.z == 3)(zero(2))


CRING, RING, SEMS = 2, 4, 16


def reduce_scratch(n, R):
    b = jnp.bfloat16; V = pltpu.VMEM; lag = RING
    half = lag // 2
    return dict(c=V((CRING, 4, 2, R, 768), b), h1x=V((lag, 4, 2, R, 384), b), h1y=V((lag, 4, R, 768), b),
        h2y=V((half, 4, R, 384), b), z0=V((half, 4, R, 384), b), z1=V((half, 4, 2, R, 384), b), z2=V((lag, 4, R, 768), b),
        h3y=V((half, R, 384), b), h3x=V((lag, R, 768), b), osem=pltpu.SemaphoreType.DMA((n,)))
NA, ND = 8, 3
YFIRST = (1, 5)
def gather_units(wa, wd, layer):
    return [(wa.at[layer, k], k in YFIRST) for k in range(NA)] + [(wd.at[layer, k], False) for k in range(ND)]

def load_shards(p, attn_in, attn_out, fc_in, fc_out, wa, wd, sem):
    out = []
    i = 0
    for l in range(2):
        for k in range(NA):
            if k < 3: src = attn_in.at[l, :, pl.ds(768 * k, 768)]
            elif k == 3: src = attn_out.at[l]
            else: src = fc_in.at[l, :, pl.ds(768 * (k - 4), 768)]
            out.append(pltpu.make_async_copy(src, wa.at[l, k, p.z, p.y], sem.at[i])); i += 1
        for k in range(ND):
            out.append(pltpu.make_async_copy(fc_out.at[l, pl.ds(128 * k, 128)], wd.at[l, k, p.z, p.y], sem.at[i])); i += 1
    return out
ORDER = [("D", 0), ("D", 1), ("D", 2), ("A", 4), ("A", 5), ("A", 6), ("A", 7), ("A", 3), ("A", 0), ("A", 1), ("A", 2)]


F32, BF = jnp.float32, jnp.bfloat16
NN = (((1,), (0,)), ((), ()))
NT = (((1,), (1,)), ((), ()))
TN = (((0,), (0,)), ((), ()))
def mm(a, b, dims=NN):
    return lax.dot_general(a, b, dims, preferred_element_type=F32)

ROWS, WIDTH, PAIRS = 512, 768, 6
def r_gain(l, i): return 2 * l + i
def r_bias(l, i): return 4 + 6 * l + i
R_EMBED = 16
def r_fcb(l, k): return 24 + 4 * l + k

def row(ref, r):
    return ref[pl.ds(r, 1), :]

def rows_loop(step, body):
    def run(i, c):
        body(pl.ds(pl.multiple_of(i * step, step), step))
        return c
    lax.fori_loop(0, ROWS // step, run, 0)

def gelu_parts(z):
    a = jnp.abs(z)
    t = 1.0 / (1.0 + (0.3275911 * 0.7071067811865476) * a)
    e = jnp.exp(-0.5 * (z * z))
    poly = t * (0.254829592 + t * (-0.284496736 + t * (1.421413741 + t * (-1.453152027 + t * 1.061405429))))
    tail = 0.5 * poly * e
    cdf = jnp.where(z < 0, tail, 1.0 - tail)
    return z * cdf, cdf + z * (0.3989422804014327 * e)

class Net:
    def __init__(s, r):
        s.__dict__.update(r)
    def w(s, l, k):
        return s.wa.at[l, k]
    def wtile(s, l, k, cols):
        v = s.wa[l, k, :, :, :, cols]
        return v.reshape(WIDTH, v.shape[-1])
    def norm(s, l, i, xh, rs, h):
        g, b = row(s.V, r_gain(l, i)), row(s.V, r_bias(l, 4 if i else 0))
        def body(q):
            v = s.x[q, :]
            c = v - jnp.mean(v, axis=-1, keepdims=True)
            r = lax.rsqrt(jnp.mean(c * c, axis=-1, keepdims=True) + 1e-6)
            n = c * r
            xh[q, :] = n.astype(BF)
            rs[l, q, :] = r
            h[q, :] = (n * g + b).astype(BF)
        rows_loop(64, body)
    def norm_back(s, l, i, d, xh, rs, out):
        g = row(s.V, r_gain(l, i))
        z = jnp.zeros((1, WIDTH), F32)
        def run(j, c):
            q = pl.ds(pl.multiple_of(j * 64, 64), 64)
            dv, n = d[q, :], xh[q, :].astype(F32)
            dn = dv * g
            m1 = jnp.mean(dn, axis=-1, keepdims=True)
            m2 = jnp.mean(dn * n, axis=-1, keepdims=True)
            e = s.x[q, :] + rs[l, q, :] * (dn - m1 - n * m2)
            s.x[q, :] = e
            sg, sb, so = c
            sg = sg + jnp.sum(dv * n, axis=0, keepdims=True)
            sb = sb + jnp.sum(dv, axis=0, keepdims=True)
            if out is not None:
                eb = e.astype(BF)
                out[q, :] = eb
                so = so + jnp.sum(eb.astype(F32), axis=0, keepdims=True)
            return sg, sb, so
        sg, sb, so = lax.fori_loop(0, ROWS // 64, run, (z, z, z))
        s.S[pl.ds(r_gain(l, i), 1), :] = sg
        s.S[pl.ds(r_bias(l, 4 if i else 0), 1), :] = sb
        return so
    def project(s, l, k):
        bias = None if k == 1 else row(s.V, r_bias(l, 1 if k == 0 else 2))
        def body(i, c):
            q = pl.ds(pl.multiple_of((i // 3) * 256, 256), 256)
            n = pl.ds(pl.multiple_of(lax.rem(i, 3) * 256, 256), 256)
            v = mm(s.h[q, :], s.wtile(l, k, n))
            if bias is not None:
                v = v + s.V[pl.ds(r_bias(l, 1 if k == 0 else 2), 1), n]
            s.t[k, q, n] = v.astype(BF)
            return c
        lax.fori_loop(0, 6, body, 0)
    def masks(s):
        lane = lax.broadcasted_iota(jnp.int32, (1, 128), 1)
        return [(lane < 64).astype(F32).astype(BF), (lane >= 64).astype(F32).astype(BF)]
    def attend(s, l, p0, p1):
        ms = s.masks()
        def body(p, c):
            n = pl.ds(pl.multiple_of(p * 128, 128), 128)
            kk = s.t[1, :, n]
            vt = s.t[2, :, n].T
            for b in range(2):
                q = pl.ds(256 * b, 256)
                qs = s.t[0, q, n] * 0.125
                outs = []
                for i in range(2):
                    st = mm(kk, qs * ms[i], NT)
                    top = jnp.max(st, axis=0, keepdims=True)
                    e = jnp.exp(st - top)
                    total = jnp.sum(e, axis=0, keepdims=True)
                    s.lse[l, pl.ds(2 * p + i, 1), q] = top + jnp.log(total)
                    outs.append(mm(vt[64 * i:64 * i + 64], e.astype(BF)) * (1.0 / total))
                s.o[q, n] = jnp.concatenate(outs, axis=0).T.astype(BF)
            return c
        lax.fori_loop(p0, p1, body, 0)
    def attend_back(s, l, p0, p1):
        ms = s.masks()
        def body(p, c):
            n = pl.ds(pl.multiple_of(p * 128, 128), 128)
            kk, vv = s.t[1, :, n], s.t[2, :, n]
            kt = kk.T
            dv = jnp.zeros((ROWS, 128), F32)
            dk = jnp.zeros((ROWS, 128), F32)
            for b in range(2):
                q = pl.ds(256 * b, 256)
                qs = s.t[0, q, n] * 0.125
                do = s.do[q, n]
                dq = []
                for i in range(2):
                    qm, dm = qs * ms[i], do * ms[i]
                    pt = jnp.exp(mm(kk, qm, NT) - s.lse[l, pl.ds(2 * p + i, 1), q])
                    dp = mm(vv, dm, NT)
                    dv = dv + mm(pt.astype(BF), dm)
                    ds = (pt * (dp - jnp.sum(pt * dp, axis=0, keepdims=True))).astype(BF)
                    dk = dk + mm(ds, qm)
                    dq.append(mm(kt[64 * i:64 * i + 64], ds) * 0.125)
                s.t[0, q, n] = jnp.concatenate(dq, axis=0).T.astype(BF)
            s.t[1, :, n] = dk.astype(BF)
            s.t[2, :, n] = dv.astype(BF)
            return c
        lax.fori_loop(p0, p1, body, 0)
    def attn_out(s, l):
        def body(i, c):
            q = pl.ds(pl.multiple_of((i // 3) * 256, 256), 256)
            n = pl.ds(pl.multiple_of(lax.rem(i, 3) * 256, 256), 256)
            s.x[q, n] = s.x[q, n] + (mm(s.o[q, :], s.wtile(l, 3, n)) + s.V[pl.ds(r_bias(l, 3), 1), n])
            return c
        lax.fori_loop(0, 6, body, 0)
    def mlp_in(s, l, k):
        def body(i, c):
            q = pl.ds(pl.multiple_of((i // 2) * 256, 256), 256)
            f = lax.rem(i, 2)
            n = pl.ds(pl.multiple_of(f * 384, 128), 384)
            z = mm(s.h2[q, :], s.wtile(l, 4 + k, n)) + s.V[pl.ds(r_fcb(l, k), 1), n]
            a, d = gelu_parts(z)
            a, d = a.astype(BF), d.astype(BF)
            at = pl.ds(pl.multiple_of((2 * k + f) * 128, 128), 128)
            for j in range(3):
                s.g[j, q, at] = a[:, 128 * j:128 * j + 128]
                s.gp[j, q, at] = d[:, 128 * j:128 * j + 128]
            return c
        lax.fori_loop(0, 4, body, 0)
    def mlp_out(s, l, j, to):
        def body(i, c):
            q = pl.ds(pl.multiple_of((i // 3) * 256, 256), 256)
            n = pl.ds(pl.multiple_of(lax.rem(i, 3) * 256, 256), 256)
            w = s.wd[l, j, :, :, :, n].reshape(1024, 256)
            v = mm(s.g[j, q, :], w)
            if j == 0:
                v = v + s.V[pl.ds(r_bias(l, 5), 1), n]
            to[q, n] = s.x[q, n] + v
            return c
        lax.fori_loop(0, 6, body, 0)
    def start_back(s, l, make):
        def run(j, c):
            q = pl.ds(pl.multiple_of(j * 64, 64), 64)
            if make:
                s.du[q, :] = s.x[q, :].astype(BF)
            eb = s.du[q, :]
            return c + jnp.sum(eb.astype(F32), axis=0, keepdims=True)
        s.S[pl.ds(r_bias(l, 5), 1), :] = lax.fori_loop(0, ROWS // 64, run, jnp.zeros((1, WIDTH), F32))
    def mlp_out_back(s, l, j):
        def body(i, c):
            f = 2 * i
            w = s.wd[l, j, i].reshape(256, WIDTH)
            n = pl.ds(pl.multiple_of(i * 256, 256), 256)
            tot = jnp.zeros((1, 256), F32)
            for b in range(2):
                q = pl.ds(256 * b, 256)
                dz = (mm(s.du[q, :], w, NT) * s.gp[j, q, n].astype(F32)).astype(BF)
                s.gp[j, q, n] = dz
                tot = tot + jnp.sum(dz.astype(F32), axis=0, keepdims=True)
            s.bz[pl.ds(3 * l + j, 1), n] = tot
            return c
        lax.fori_loop(0, 4, body, 0)
    def mlp_out_grad(s, l, j, to):
        def body(i, c):
            n = pl.ds(pl.multiple_of(i * 256, 256), 256)
            to[i] = mm(s.g[j, :, n], s.du[...], TN).astype(BF).reshape(2, 128, WIDTH)
            return c
        lax.fori_loop(0, 4, body, 0)
    def hidden_bias(s):
        for l in range(2):
            for j in range(3):
                for f in range(8):
                    s.S[pl.ds(r_fcb(l, f // 2), 1), pl.ds(384 * (f % 2) + 128 * j, 128)] = s.bz[pl.ds(3 * l + j, 1), pl.ds(128 * f, 128)]
    def dz_tile(s, k, q):
        parts = []
        for f in range(2):
            for j in range(3):
                parts.append(s.gp[j, q, pl.ds((2 * k + f) * 128, 128)])
        return jnp.concatenate(parts, axis=1)
    def back_mm(s, l, k, get, first):
        def body(i, c):
            q = pl.ds(pl.multiple_of(lax.rem(i, 2) * 256, 256), 256)
            z = i // 2
            w = s.wa[l, k, pl.ds(z * 2, 2)].reshape(384, WIDTH)
            n = pl.ds(pl.multiple_of(z * 384, 128), 384)
            v = mm(get(q), w, NT)
            s.acc[q, n] = v if first else s.acc[q, n] + v
            return c
        lax.fori_loop(0, 4, body, 0)
    def grad_a(s, l, k, get, lhs):
        def body(i, c):
            n = pl.ds(pl.multiple_of(i * 384, 128), 384)
            gr = mm(lhs[:, n], get(slice(None)), TN).astype(BF)
            s.wa[l, k, pl.ds(i * 2, 2)] = gr.reshape(2, 2, 96, WIDTH)
            return c
        lax.fori_loop(0, 2, body, 0)
    def attn_out_back(s, l):
        def body(i, c):
            q = pl.ds(pl.multiple_of(lax.rem(i, 2) * 256, 256), 256)
            z = i // 2
            w = s.wa[l, 3, pl.ds(z * 2, 2)].reshape(384, WIDTH)
            n = pl.ds(pl.multiple_of(z * 384, 128), 384)
            s.do[q, n] = mm(s.du[q, :], w, NT).astype(BF)
            return c
        lax.fori_loop(0, 4, body, 0)
    def col_sum(s, ref, r):
        def run(j, c):
            q = pl.ds(pl.multiple_of(j * 128, 128), 128)
            return c + jnp.sum(ref[q, :].astype(F32), axis=0, keepdims=True)
        s.S[pl.ds(r, 1), :] = lax.fori_loop(0, 4, run, jnp.zeros((1, WIDTH), F32))

def net_scratch():
    V = pltpu.VMEM
    return dict(x=V((512, 768), F32), acc=V((512, 768), F32), h=V((512, 768), BF), t=V((3, 512, 768), BF), lse=V((2, 16, 512), F32),
        o=V((512, 768), BF), h2=V((512, 768), BF), g=V((3, 512, 1024), BF), gp=V((3, 512, 1024), BF), xh1=V((512, 768), BF), xh2=V((512, 768), BF),
        rs1=V((2, 512, 1), F32), rs2=V((2, 512, 1), F32), du=V((512, 768), BF), do=V((512, 768), BF),
        bz=V((8, 1024), F32), V=V((32, 768), F32), S=V((32, 768), F32))
SPILL = ["h", "t", "o", "h2", "g", "gp", "xh1", "xh2"]


SMALL = (32, 768)
VMEM_LIMIT = 63 * 1024 * 1024
EARLY = {0: 32}
LEAD = 30


def gather_list(wa, wd):
    units, first = [], []
    for l in range(2):
        for w, yfirst in gather_units(wa, wd, l):
            h = EARLY.get(len(first), w.shape[2])
            units += [(w.at[:, :, pl.ds(a, h), :], yfirst) for a in range(0, w.shape[2], h)]
            first.append(len(units) - 1)
    return units, first


def reduce_list():
    out = []
    for l in (1, 0):
        for k, q in ORDER:
            H = 128 if k == "D" else 96
            hs = [64, 64] if k == "D" else [H]
            a = 0
            for h in hs:
                out.append((l, k, q, a, h)); a += h
    return out


def steps(P, n, unit, marks, do):
    P.step(do.embed, 1.5, [do.params])
    for l in range(2):
        P.step(lambda l=l: (do.reuse(l, "xh1", "h"), n.norm(l, 0, n.xh1, n.rs1, n.h), do.keep(l, "xh1")), 1.6)
        for k in range(3):
            P.step(lambda l=l, k=k: (do.reuse(l, *(["t"] if k == 0 else [])), n.project(l, k)), 1.7, [unit(l, k)])
        for a in range(0, 6, 2):
            P.step(lambda l=l, a=a: (do.keep(l, *(["h", "t"] if a == 0 else [])), do.reuse(l, *(["o"] if a == 0 else [])), n.attend(l, a, a + 2)), 3.9)
        P.step(lambda l=l: (do.keep(l, "o"), n.attn_out(l)), 1.6, [unit(l, 3)])
        P.step(lambda l=l: (do.reuse(l, "xh2", "h2"), n.norm(l, 1, n.xh2, n.rs2, n.h2), do.keep(l, "xh2")), 1.6)
        for k in range(4):
            P.step(lambda l=l, k=k: (do.reuse(l, *(["g", "gp"] if k == 0 else [])), n.mlp_in(l, k)), 2.8, [unit(l, 4 + k)])
        if l == 1:
            P.step(lambda: n.start_back(1, False), 0.5)
            for j in range(3):
                P.step(lambda j=j: n.mlp_out_grad(1, j, n.wg.at[j]), 1.2, (), marks(1, "D", j))
        for j in range(3):
            P.step(lambda l=l, j=j: (do.keep(l, *(["h2", "gp"] if j == 0 else [])), n.mlp_out(l, j, n.acc if (l == 1 and j == 2) else n.x)), 2.0, [unit(l, 8 + j)])
        P.step(lambda l=l: do.keep(l, "g"), 0.0)
    P.step(do.turn, 1.0)
    for l in (1, 0):
        if l == 0:
            P.step(lambda: n.start_back(0, True), 0.6)
        for j in range(3):
            P.step(lambda l=l, j=j: (do.need(l, *(["gp", "g"] if j == 0 else [])), n.mlp_out_back(l, j)), 1.4)
            if l == 0:
                P.step(lambda j=j: n.mlp_out_grad(0, j, n.wd.at[0, j]), 1.2, (), marks(0, "D", j))
        P.step(lambda l=l: (do.done(l, "g"), do.need(l, "h2")), 0.0)
        for k in range(4):
            get = lambda q, k=k: n.dz_tile(k, q)
            P.step(lambda l=l, k=k, get=get: n.back_mm(l, 4 + k, get, k == 0), 1.6)
            P.step(lambda l=l, k=k, get=get: n.grad_a(l, 4 + k, get, n.h2), 1.1, (), marks(l, "A", 4 + k))
        P.step(lambda l=l: (do.done(l, "gp", "h2"), do.need(l, "xh2"), do.mid_norm(l), do.done(l, "xh2"), do.need(l, "o")), 1.6)
        P.step(lambda l=l: n.attn_out_back(l), 1.5)
        P.step(lambda l=l: n.grad_a(l, 3, lambda q: n.du[q, :], n.o), 1.1, (), marks(l, "A", 3))
        P.step(lambda l=l: (do.done(l, "o"), do.need(l, "t")), 0.0)
        for a in range(0, 6, 2):
            P.step(lambda l=l, a=a: n.attend_back(l, a, a + 2), 4.4)
        P.step(lambda l=l: (do.need(l, "h"), n.col_sum(n.t.at[0], r_bias(l, 1)), n.col_sum(n.t.at[2], r_bias(l, 2))), 0.3)
        for k in range(3):
            get = lambda q, k=k: n.t[k, q, :]
            P.step(lambda l=l, k=k, get=get: n.back_mm(l, k, get, k == 0), 1.6)
            P.step(lambda l=l, k=k, get=get: n.grad_a(l, k, get, n.h), 1.1, (), marks(l, "A", k))
        P.step(lambda l=l: (do.done(l, "t", "h"), do.need(l, "xh1"), n.norm_back(l, 0, n.acc, n.xh1, n.rs1, None), do.done(l, "xh1")), 1.6)
    P.step(do.last, 1.0, (), [do.sums])


class Smalls:
    def __init__(s, p, net, b):
        s.p, s.net, s.b = p, net, b
    def pack(s, gains, biases, embed, fcb):
        k = s.b["own"]
        k[...] = jnp.zeros((32, 128), F32)
        for l in range(2):
            k[2 * l:2 * l + 2, 0:96] = gains[l].astype(F32)
            k[4 + 6 * l:10 + 6 * l, 0:96] = biases[l].astype(F32)
            for i in range(3):
                k[24 + 3 * l + i:25 + 3 * l + i, :] = fcb[l:l + 1, 128 * i:128 * i + 128].astype(F32)
        k[16:17, 0:96] = embed[...].astype(F32)
        s.b["sm"][s.p.fs] = k[...].astype(BF)
    def fetch(s, d):
        b, p = s.b, s.p
        return remote(b["sm"].at[p.fs], b["sm"].at[p.fs], b["ss"].at[d - 1], b["rs"].at[d - 1], p.dev_f(d))
    def start(s):
        for d in range(1, 8):
            s.fetch(d).start()
    def build(s):
        for d in range(1, 8):
            s.fetch(d).wait()
        V = s.net.V
        i = lax.broadcasted_iota(jnp.int32, (128, 768), 0)
        c = lax.broadcasted_iota(jnp.int32, (128, 768), 1)
        total = jnp.zeros((24, 768), F32)
        for f in range(8):
            blk = s.b["sm"][f]
            pick = jnp.where((c - 96 * f == i) & (i < 96), 1.0, 0.0).astype(BF)
            total = total + mm(blk, pick)[0:24]
        V[0:24, :] = total
        for f in range(8):
            blk = s.b["sm"][f].astype(F32)
            for l in range(2):
                for j in range(3):
                    at = 384 * (f % 2) + 128 * j
                    V[r_fcb(l, f // 2):r_fcb(l, f // 2) + 1, at:at + 128] = blk[24 + 3 * l + j:25 + 3 * l + j]
    def hop(s, h):
        b, p, S = s.b, s.p, s.net.S
        if h < 3:
            return [remote(S, b["sr"].at[h], b["ss"].at[7 + h], b["rs"].at[7 + h], (p.dev_c, p.dev_x, p.dev_y)[h])]
        return [remote(S, b["sr"].at[2 + d], b["ss"].at[9 + d], b["rs"].at[9 + d], p.dev_at(p.up(d))) for d in (1, 2, 3)]
    def send(s, h):
        for q in s.hop(h): q.start()
    def add(s, h):
        for q in s.hop(h): q.wait()
        t = s.net.S[...]
        for i in ([h] if h < 3 else [3, 4, 5]):
            t = t + s.b["sr"][i]
        s.net.S[...] = t
    def plan(s, P, begin):
        prev = begin
        for h, r in enumerate("cxym"):
            prev = P.op(lambda h=h: s.send(h), lambda h=h: s.add(h), {r: 98304 * (4 if r == "m" else 1)}, [prev], rank=-1)
        return prev
    def own(s):
        k, S, f = s.b["own"], s.net.S, s.p.fs
        k[...] = jnp.zeros((32, 128), F32)
        v = jnp.zeros((24, 96), F32)
        for i in range(8):
            v = jnp.where(f == i, S[0:24, 96 * i:96 * i + 96], v)
        k[0:24, 0:96] = v
        for l in range(2):
            w = jnp.zeros((1, 384), F32)
            for i in range(8):
                w = jnp.where(f == i, S[r_fcb(l, i // 2):r_fcb(l, i // 2) + 1, 384 * (i % 2):384 * (i % 2) + 384], w)
            for j in range(3):
                k[24 + 3 * l + j:25 + 3 * l + j, :] = w[:, 128 * j:128 * j + 128]


def remote(src, dst, ss, rs, dev):
    return pltpu.make_async_remote_copy(src_ref=src, dst_ref=dst, send_sem=ss, recv_sem=rs, device_id=dev, device_id_type=MESH)


def smalls_scratch():
    return dict(sm=pltpu.VMEM((8, 32, 128), BF), own=pltpu.VMEM((32, 128), F32), sr=pltpu.VMEM((6, 32, 768), F32),
        ss=pltpu.SemaphoreType.DMA((13,)), rs=pltpu.SemaphoreType.DMA((13,)))


class Work:
    pass


def whole_kernel(tok, cot, msk, gains, biases, embed, fcb, ai, ao, fi, fo, act, ig, so, o_ai, o_ao, o_fi, o_fo, *rest):
    spill = dict(zip(SPILL, rest[:8]))
    sc, wa, wd, wg, fa, fd, col, rbufs, sbufs, lsem, ssem, iosem, gss, grs, rss, rrs = rest[8:]
    p = Pos()
    n = Net(dict(sc, wa=wa, wd=wd, wg=wg))
    sm = Smalls(p, n, sbufs)
    tok_in = pltpu.make_async_copy(tok, n.do, iosem.at[0])
    cot_in = pltpu.make_async_copy(cot, n.du, iosem.at[1])
    loads = load_shards(p, ai, ao, fi, fo, wa, wd, lsem)
    for c in loads: c.start()
    tok_in.start(); cot_in.start()
    red = []
    for l, k, q, a, h in reduce_list():
        w = (wg.at[q] if l == 1 else wd.at[l, q]) if k == "D" else wa.at[l, q]
        f = (fd if k == "D" else fa).at[l, q, pl.ds(a, h)]
        if k == "D": o = o_fo.at[l, pl.ds(128 * q + a, h)]
        elif q == 3: o = o_ao.at[l, pl.ds(a, h)]
        elif q < 3: o = o_ai.at[l, pl.ds(a, h), pl.ds(768 * q, 768)]
        else: o = o_fi.at[l, pl.ds(a, h), pl.ds(768 * (q - 4), 768)]
        red.append((w.at[:, :, pl.ds(a, h), :], f, o))
    r = Reduce(p, red, rbufs, rss, rrs)
    r.clear()
    sm.pack(gains, biases, embed, fcb)
    mt = msk[...].astype(F32).T
    for j in range(4):
        col[128 * j:128 * j + 128, :] = mt[:, j:j + 1]
    for c in loads: c.wait()
    barrier(p)
    units, part = gather_list(wa, wd)
    g = Gather(p, units, gss, grs, LEAD)
    P = Plan()
    out_of = lambda nm: pltpu.make_async_copy(sc[nm], spill[nm], ssem.at[SPILL.index(nm)])
    back_to = lambda nm: pltpu.make_async_copy(spill[nm], sc[nm], ssem.at[SPILL.index(nm)])
    act_out = pltpu.make_async_copy(n.acc, act, iosem.at[0])
    ig_out = pltpu.make_async_copy(n.acc, ig, iosem.at[1])

    class Do(Work):
        params = P.op(sm.start, sm.build, dict(y=40e3), (), cost=1.0, rank=-1)
        sums = P.mark()
        @staticmethod
        def reuse(l, *nms):
            for m in nms if l == 1 else (): out_of(m).wait()
        @staticmethod
        def keep(l, *nms):
            for m in nms if l == 0 else (): out_of(m).start()
        @staticmethod
        def need(l, *nms):
            for m in nms if l == 0 else (): back_to(m).wait()
        @staticmethod
        def done(l, *nms):
            for m in nms if l == 1 else (): back_to(m).start()
        @staticmethod
        def embed():
            tok_in.wait(); cot_in.wait()
            n.S[...] = jnp.zeros(SMALL, F32)
            def body(q):
                m = col[q, :]
                n.x[q, :] = n.do[q, :].astype(F32) * (1.0 - m) + m * row(n.V, R_EMBED)
            rows_loop(64, body)
        @staticmethod
        def turn():
            act_out.start()
            def body(q):
                n.x[q, :] = n.du[q, :].astype(F32)
            rows_loop(64, body)
            act_out.wait()
        @staticmethod
        def mid_norm(l):
            n.S[pl.ds(r_bias(l, 3), 1), :] = n.norm_back(l, 1, n.acc, n.xh2, n.rs2, n.du)
        @staticmethod
        def last():
            n.hidden_bias()
            def body(j, c):
                q = pl.ds(pl.multiple_of(j * 64, 64), 64)
                m, e = col[q, :], n.x[q, :]
                n.acc[q, :] = e * (1.0 - m)
                return c + jnp.sum(e * m, axis=0, keepdims=True)
            n.S[pl.ds(R_EMBED, 1), :] = lax.fori_loop(0, ROWS // 64, body, jnp.zeros((1, WIDTH), F32))
            ig_out.start()

    make_plan(P, n, g, part, r, sm, Do)
    P.run()
    sm.own()
    s_out = pltpu.make_async_copy(sbufs["own"], so, iosem.at[2])
    s_out.start()
    r.finish()
    ig_out.wait()
    s_out.wait()


def make_plan(P, n, g, part, r, sm, do):
    lasts = g.plan(P)
    marks = {}
    order = []
    for l, k, q, a, h in reduce_list():
        m = P.mark()
        marks.setdefault((l, k, q), []).append(m)
        order.append(m)
    r.plan(P, order)
    sm.plan(P, do.sums)
    steps(P, n, lambda l, k: lasts[part[11 * l + k]], lambda l, k, q: marks[(l, k, q)], do)


def whole(tok, cot, msk, gains, biases, embed, fcb, ai, ao, fi, fo):
    net = net_scratch()
    any_, vm = pl.BlockSpec(memory_space=pl.ANY), pl.BlockSpec(memory_space=pltpu.VMEM)
    sa, sd = (2, 8, 4, 2, 96, 768), (2, 3, 4, 2, 128, 768)
    fa, fd = (2, 8, 96, 768), (2, 3, 128, 768)
    shapes = [((512, 768), F32), ((512, 768), F32), ((32, 128), F32), (ai.shape, BF), (ao.shape, BF), (fi.shape, BF), (fo.shape, BF)]
    shapes += [(net[k].shape, net[k].dtype) for k in SPILL]
    dma = pltpu.SemaphoreType.DMA
    parts, red = 22 + sum((96 if u % 11 < 8 else 128) // h - 1 for u, h in EARLY.items()), reduce_list()
    R = max(v[4] for v in red) // 2
    return pl.pallas_call(
        whole_kernel,
        out_shape=[jax.ShapeDtypeStruct(*v) for v in shapes],
        in_specs=[any_, any_, vm, vm, vm, vm, vm] + [any_] * 4,
        out_specs=[any_] * len(shapes),
        scratch_shapes=[
            net, pltpu.VMEM(sa, BF), pltpu.VMEM(sd, BF), pltpu.VMEM(sd[1:], BF), pltpu.VMEM(fa, BF), pltpu.VMEM(fd, BF),
            pltpu.VMEM((512, 1), F32), reduce_scratch(len(red), R), smalls_scratch(), dma((22,)), dma((8,)), dma((3,)),
            dma((parts, 11)), dma((parts, 11)), dma((SEMS, 10)), dma((SEMS, 10)),
        ],
        compiler_params=pltpu.CompilerParams(collective_id=0, has_side_effects=True, vmem_limit_bytes=VMEM_LIMIT),
    )(tok, cot, msk, gains, biases, embed, fcb, ai, ao, fi, fo)[:7]


def fused_local(tokens, mask, cotangent, mask_embed, attn_in, attn_out, fc_in, fc_out, gains, biases, fc_bias):
    act, ig, own, o_ai, o_ao, o_fi, o_fo = whole(
        tokens, cotangent, mask.reshape(4, 128), gains, biases, mask_embed.reshape(1, 96), fc_bias, attn_in, attn_out, fc_in, fc_out)
    return (
        act, ig, own[16, :96], o_ai.astype(F32), o_ao.astype(F32), o_fi.astype(F32), o_fo.astype(F32),
        own[0:4, :96].reshape(2, 2, 96), own[4:16, :96].reshape(2, 6, 96), own[24:30].reshape(2, 384))


def solution(mesh):
    if dict(mesh.shape) != {"dp": 4, "fsdp": 8}:
        return generic_solution(mesh)
    rows = P(("dp", "fsdp"), None)
    mat = P(None, "fsdp", None)
    vec = P(None, None, "fsdp")
    return jax.shard_map(
        fused_local, mesh=mesh,
        in_specs=(rows, P(("dp", "fsdp")), rows, P("fsdp"), mat, mat, mat, mat, vec, vec, P(None, "fsdp")),
        out_specs=(rows, rows, P("fsdp"), mat, mat, mat, mat, vec, vec, P(None, "fsdp")),
        check_vma=False)


HEADS = 12
SEQ = 512
LAYERS = 2


eps = 1e-06


def norm_rows(values, gain, bias):
    center = values - jnp.mean(values, axis=-1, keepdims=True)
    spread = jnp.mean(center * center, axis=-1, keepdims=True)
    return center * lax.rsqrt(spread + eps) * gain + bias


def gelu_exact(values):
    return jax.nn.gelu(values, approximate=False)


def split_heads(values, clips):
    width = values.shape[1]
    return values.reshape(clips, SEQ, HEADS, width // HEADS)


def attend(pack):
    query, key_rows, value = pack
    scale = query.shape[-1] ** (-0.5)
    scores = jnp.einsum("qhd,khd->hqk", query, key_rows, preferred_element_type=jnp.float32) * scale
    top = jnp.max(scores, axis=-1, keepdims=True)
    expo = jnp.exp(scores - top)
    total = jnp.sum(expo, axis=-1, keepdims=True)
    probs = (expo / total).astype(jnp.bfloat16)
    mixed = jnp.einsum("hqk,khd->qhd", probs, value, preferred_element_type=jnp.float32)
    return (mixed, top + jnp.log(total))


def attend_back(pack):
    query, key_rows, value, logsum, d_mixed = pack
    scale = query.shape[-1] ** (-0.5)
    scores = jnp.einsum("qhd,khd->hqk", query, key_rows, preferred_element_type=jnp.float32) * scale
    probs = jnp.exp(scores - logsum)
    d_probs = jnp.einsum("qhd,khd->hqk", d_mixed, value, preferred_element_type=jnp.float32)
    d_value = jnp.einsum(
        "hqk,qhd->khd", probs.astype(jnp.bfloat16), d_mixed, preferred_element_type=jnp.float32
    )
    d_scores = probs * (d_probs - jnp.sum(probs * d_probs, axis=-1, keepdims=True))
    d_scaled = d_scores.astype(jnp.bfloat16) * scale
    d_query = jnp.einsum("hqk,khd->qhd", d_scaled, key_rows, preferred_element_type=jnp.float32)
    d_key = jnp.einsum("hqk,qhd->khd", d_scaled, query, preferred_element_type=jnp.float32)
    return (d_query, d_key, d_value)


def layer_forward(state, weights):
    w_qkv, w_out, w_in, w_down, gain, bias, fcb = weights
    rows, width = state.shape
    clips = rows // SEQ
    normed = norm_rows(state, gain[0].astype(jnp.float32), bias[0].astype(jnp.float32)).astype(
        jnp.bfloat16
    )
    qkv_bias = jnp.concatenate([bias[1], jnp.zeros_like(bias[1]), bias[2]]).astype(jnp.float32)
    joined = (jnp.dot(normed, w_qkv, preferred_element_type=jnp.float32) + qkv_bias).astype(
        jnp.bfloat16
    )
    query = split_heads(joined[:, :width], clips)
    key_rows = split_heads(joined[:, width : 2 * width], clips)
    value = split_heads(joined[:, 2 * width :], clips)
    mixed, logsum = lax.map(attend, (query, key_rows, value))
    mixed = mixed.reshape(rows, width).astype(jnp.bfloat16)
    middle = (
        state
        + jnp.dot(mixed, w_out, preferred_element_type=jnp.float32)
        + bias[3].astype(jnp.float32)
    )
    normed_two = norm_rows(middle, gain[1].astype(jnp.float32), bias[4].astype(jnp.float32)).astype(
        jnp.bfloat16
    )
    hidden = jnp.dot(normed_two, w_in, preferred_element_type=jnp.float32) + fcb.astype(jnp.float32)
    activated = gelu_exact(hidden).astype(jnp.bfloat16)
    return (normed, query, key_rows, value, logsum, mixed, middle, normed_two, hidden, activated)


def layer_finish(saved, weights):
    middle = saved[6]
    activated = saved[9]
    return (
        middle
        + jnp.dot(activated, weights[3], preferred_element_type=jnp.float32)
        + weights[5][5].astype(jnp.float32)
    )


def layer_backward(state, weights, grad):
    w_qkv, w_out, w_in, w_down, gain, bias, fcb = weights
    rows, width = state.shape
    clips = rows // SEQ
    normed, query, key_rows, value, logsum, mixed, middle, normed_two, hidden, activated = (
        layer_forward(state, weights)
    )
    d_up = grad.astype(jnp.bfloat16)
    g_down = jnp.einsum("tf,td->fd", activated, d_up, preferred_element_type=jnp.float32)
    d_two = jnp.sum(d_up.astype(jnp.float32), axis=0)
    d_act = jnp.einsum("td,fd->tf", d_up, w_down, preferred_element_type=jnp.float32)
    d_hidden = jax.vjp(gelu_exact, hidden)[1](d_act)[0].astype(jnp.bfloat16)
    g_in = jnp.einsum("td,tf->df", normed_two, d_hidden, preferred_element_type=jnp.float32)
    d_one = jnp.sum(d_hidden.astype(jnp.float32), axis=0)
    d_normed_two = jnp.einsum("tf,df->td", d_hidden, w_in, preferred_element_type=jnp.float32)
    back_two = jax.vjp(norm_rows, middle, gain[1].astype(jnp.float32), bias[4].astype(jnp.float32))[
        1
    ]
    d_middle, d_gain_two, d_bias_two = back_two(d_normed_two)
    d_middle = grad + d_middle
    d_branch = d_middle.astype(jnp.bfloat16)
    g_out = jnp.einsum("td,te->de", mixed, d_branch, preferred_element_type=jnp.float32)
    d_outb = jnp.sum(d_branch.astype(jnp.float32), axis=0)
    d_mixed = jnp.einsum("te,de->td", d_branch, w_out, preferred_element_type=jnp.float32).astype(
        jnp.bfloat16
    )
    d_query, d_key, d_value = lax.map(
        attend_back, (query, key_rows, value, logsum, split_heads(d_mixed, clips))
    )
    d_joined = jnp.concatenate(
        [d_query.reshape(rows, width), d_key.reshape(rows, width), d_value.reshape(rows, width)],
        axis=1,
    ).astype(jnp.bfloat16)
    g_qkv = jnp.einsum("td,te->de", normed, d_joined, preferred_element_type=jnp.float32)
    d_sums = jnp.sum(d_joined.astype(jnp.float32), axis=0)
    d_normed = jnp.einsum("te,de->td", d_joined, w_qkv, preferred_element_type=jnp.float32)
    back_one = jax.vjp(norm_rows, state, gain[0].astype(jnp.float32), bias[0].astype(jnp.float32))[
        1
    ]
    d_state, d_gain_one, d_bias_one = back_one(d_normed)
    gain_terms = jnp.stack([d_gain_one, d_gain_two])
    bias_terms = jnp.stack(
        [d_bias_one, d_sums[:width], d_sums[2 * width :], d_outb, d_bias_two, d_two]
    )
    return (d_middle + d_state, (g_qkv, g_out, g_in, g_down, gain_terms, bias_terms, d_one))


def local(
    tokens, mask, cotangent, mask_embed, attn_in, attn_out, fc_in, fc_out, gains, biases, fc_bias
):
    mask_f = mask.astype(jnp.float32)[:, None]
    state = tokens.astype(jnp.float32)
    stored = []
    kept = []
    for layer in range(LAYERS):
        fetched = (
            lax.all_gather(attn_in[layer], "fsdp", axis=0, tiled=True),
            lax.all_gather(attn_out[layer], "fsdp", axis=0, tiled=True),
            lax.all_gather(fc_in[layer], "fsdp", axis=0, tiled=True),
            lax.all_gather(fc_out[layer], "fsdp", axis=0, tiled=True),
            lax.all_gather(gains[layer], "fsdp", axis=1, tiled=True),
            lax.all_gather(biases[layer], "fsdp", axis=1, tiled=True),
            lax.all_gather(fc_bias[layer], "fsdp", axis=0, tiled=True),
            lax.all_gather(mask_embed, "fsdp", axis=0, tiled=True),
        )
        if layer == 0:
            state = state * (1.0 - mask_f) + mask_f * fetched[7].astype(jnp.float32)
        stored.append(state)
        weights = tuple(fetched[:7])
        kept.append(weights)
        state = layer_finish(layer_forward(state, weights), weights)
    grad = cotangent.astype(jnp.float32)
    layer_grads = [None] * LAYERS
    for layer in reversed(range(LAYERS)):
        weights = tuple(
            (
                lax.all_gather(attn_in[layer], "fsdp", axis=0, tiled=True),
                lax.all_gather(attn_out[layer], "fsdp", axis=0, tiled=True),
                lax.all_gather(fc_in[layer], "fsdp", axis=0, tiled=True),
                lax.all_gather(fc_out[layer], "fsdp", axis=0, tiled=True),
                lax.all_gather(gains[layer], "fsdp", axis=1, tiled=True),
                lax.all_gather(biases[layer], "fsdp", axis=1, tiled=True),
                lax.all_gather(fc_bias[layer], "fsdp", axis=0, tiled=True),
            )
        )
        grad, terms = layer_backward(stored[layer], weights, grad)
        if layer == 0:
            mask_term = jnp.sum(grad * mask_f, axis=0)
        else:
            mask_term = jnp.zeros((grad.shape[1],), jnp.float32)
        shares = (
            lax.psum_scatter(terms[0], "fsdp", scatter_dimension=0, tiled=True),
            lax.psum_scatter(terms[1], "fsdp", scatter_dimension=0, tiled=True),
            lax.psum_scatter(terms[2], "fsdp", scatter_dimension=0, tiled=True),
            lax.psum_scatter(terms[3], "fsdp", scatter_dimension=0, tiled=True),
            lax.psum_scatter(terms[4], "fsdp", scatter_dimension=1, tiled=True),
            lax.psum_scatter(terms[5], "fsdp", scatter_dimension=1, tiled=True),
            lax.psum_scatter(terms[6], "fsdp", scatter_dimension=0, tiled=True),
            lax.psum_scatter(mask_term, "fsdp", scatter_dimension=0, tiled=True),
        )
        slices = (
            lax.psum_scatter(
                shares[0].astype(jnp.bfloat16), "dp", scatter_dimension=1, tiled=True
            ).astype(jnp.float32),
            lax.psum_scatter(
                shares[1].astype(jnp.bfloat16), "dp", scatter_dimension=1, tiled=True
            ).astype(jnp.float32),
            lax.psum_scatter(
                shares[2].astype(jnp.bfloat16), "dp", scatter_dimension=1, tiled=True
            ).astype(jnp.float32),
            lax.psum_scatter(
                shares[3].astype(jnp.bfloat16), "dp", scatter_dimension=1, tiled=True
            ).astype(jnp.float32),
        )
        matrices = (
            lax.all_gather(slices[0].astype(jnp.bfloat16), "dp", axis=1, tiled=True).astype(
                jnp.float32
            ),
            lax.all_gather(slices[1].astype(jnp.bfloat16), "dp", axis=1, tiled=True).astype(
                jnp.float32
            ),
            lax.all_gather(slices[2].astype(jnp.bfloat16), "dp", axis=1, tiled=True).astype(
                jnp.float32
            ),
            lax.all_gather(slices[3].astype(jnp.bfloat16), "dp", axis=1, tiled=True).astype(
                jnp.float32
            ),
        )
        smalls = lax.psum((shares[4], shares[5], shares[6], shares[7]), "dp")
        layer_grads[layer] = (
            matrices[0],
            matrices[1],
            matrices[2],
            matrices[3],
            smalls[0],
            smalls[1],
            smalls[2],
            smalls[3],
        )
    input_grad = grad * (1.0 - mask_f)
    stacked = [jnp.stack([layer_grads[lay][item] for lay in range(LAYERS)]) for item in range(7)]
    results = tuple(stacked) + (layer_grads[0][7],)
    return (
        state,
        input_grad,
        results[7],
        results[0],
        results[1],
        results[2],
        results[3],
        results[4],
        results[5],
        results[6],
    )


def generic_solution(mesh):
    placed = (
        P(("dp", "fsdp"), None),
        P(("dp", "fsdp")),
        P(("dp", "fsdp"), None),
        P("fsdp"),
        P(None, "fsdp", None),
        P(None, "fsdp", None),
        P(None, "fsdp", None),
        P(None, "fsdp", None),
        P(None, None, "fsdp"),
        P(None, None, "fsdp"),
        P(None, "fsdp"),
    )
    return jax.shard_map(
        local,
        mesh=mesh,
        in_specs=placed,
        out_specs=(
            P(("dp", "fsdp"), None),
            P(("dp", "fsdp"), None),
            P("fsdp"),
            P(None, "fsdp", None),
            P(None, "fsdp", None),
            P(None, "fsdp", None),
            P(None, "fsdp", None),
            P(None, None, "fsdp"),
            P(None, None, "fsdp"),
            P(None, "fsdp"),
        ),
        check_vma=False,
    )
```

```python
import functools

import jax
import jax.numpy as jnp
from jax import lax
from jax.experimental import pallas as pl
from jax.experimental.pallas import tpu as pltpu
from jax.sharding import PartitionSpec as P
MESH = pl.DeviceIdType.MESH


class Pos:
    def __init__(s):
        s.dp = lax.axis_index("dp"); s.fs = lax.axis_index("fsdp")
        s.x = s.dp // 2; s.c = lax.rem(s.dp, 2)
        s.z = s.fs // 2; s.y = lax.rem(s.fs, 2)
        s.dev_c = (s.dp + 1 - 2 * s.c, s.fs)
        s.dev_x = (lax.rem(s.dp + 2, 4), s.fs)
        s.dev_y = (s.dp, s.fs + 1 - 2 * s.y)
        s.edge = (s.z == 0) | (s.z == 3)
        s.mid = (s.z == 1) | (s.z == 2)
    def dev_f(s, d):
        return (s.dp, lax.rem(s.fs + d, 8))
    def dev_at(s, z):
        return (s.dp, 2 * z + s.y)
    def up(s, d):
        return lax.rem(s.z + d, 4)
    def far(s):
        return jnp.where(s.edge, 3 - s.z, 6 - 3 * s.z)


def when(cond, f):
    if cond is None:
        f()
    else:
        pl.when(cond)(f)


class Move:
    def __init__(s, src, dst, ss, rs, dev, sends=None, takes=None):
        s.copy = pltpu.make_async_remote_copy(src_ref=src, dst_ref=dst, send_sem=ss, recv_sem=rs, device_id=dev, device_id_type=MESH)
        s.sends, s.takes = sends, takes
    def start(s):
        when(s.sends, s.copy.start)
    def sent(s):
        when(s.sends, s.copy.wait_send)
    def got(s):
        when(s.takes, s.copy.wait_recv)
    def wait(s):
        s.sent(); s.got()


def barrier(p):
    bar = pltpu.get_barrier_semaphore()
    devs = [p.dev_c, p.dev_x] + [p.dev_f(d) for d in range(1, 8)]
    for d in devs:
        pl.semaphore_signal(bar, inc=1, device_id=d, device_id_type=MESH)
    pl.semaphore_wait(bar, len(devs))


class Op:
    def __init__(s, start, finish, traffic, deps=(), cost=0.1, rank=0, after=0.0):
        s.start, s.finish, s.traffic, s.cost, s.rank, s.after = start, finish, traffic, cost, rank, after
        s.deps = [d for d in deps if d is not None]
        s.begun = s.ended = False
        s.ready = None


class Plan:
    RATE = dict(x=45e3, y=45e3, m=45e3, e=45e3, g=45e3, c=600e3)
    LATENCY = 2.2
    BACKLOG = 4
    SCALE = 1.1
    def __init__(s):
        s.ops, s.steps = [], []
        s.free = {k: 0.0 for k in s.RATE}
    def op(s, *a, **k):
        s.ops.append(Op(*a, **k))
        return s.ops[-1]
    def step(s, fn, cost, needs=(), opens=()):
        s.steps.append((fn, cost * s.SCALE, [n for n in needs if n is not None], list(opens)))
    def mark(s):
        m = Op(None, None, {}); m.begun = True
        return m
    def run(s):
        now, k, waiting, flying = 0.0, 0, list(s.ops), []
        def launch(force=False):
            nonlocal waiting
            rest = []
            for o in sorted(waiting, key=lambda o: o.rank):
                ok = all(d.ended for d in o.deps) and (force or o.after <= now)
                if ok and (force or all(s.free[r] - now < s.BACKLOG for r in o.traffic)):
                    force = False
                    o.start()
                    end = now
                    for r, v in o.traffic.items():
                        s.free[r] = max(s.free[r], now) + v / s.RATE[r]
                        end = max(end, s.free[r])
                    o.ready = end + s.LATENCY
                    flying.append(o)
                else:
                    rest.append(o)
            waiting = rest
        launch()
        while k < len(s.steps) or flying or waiting:
            flying.sort(key=lambda o: o.ready)
            can = k < len(s.steps) and all(n.ended for n in s.steps[k][2])
            if flying and (flying[0].ready <= now or not can):
                o = flying.pop(0)
                now = max(now, o.ready) + o.cost
                o.finish(); o.ended = True
            elif can:
                fn, cost, needs, opens = s.steps[k]; k += 1
                fn(); now += cost
                for m in opens: m.ended = True
            launch(not flying)
        return now


class Gather:
    PACE = 0
    def __init__(s, p, units, ssem, rsem, lead=3):
        s.p, s.units, s.ss, s.rs, s.lead = p, units, ssem, rsem, lead
        s.n = len(units)
    def move(s, u, i, block, dev, sends=None, takes=None):
        return Move(block, block, s.ss.at[u, i], s.rs.at[u, i], dev, sends, takes)
    def geo(s, u):
        w, kind = s.units[u]
        p, R = s.p, w.shape[2] // 2
        yfirst = kind in (1, 3)
        rc = pl.ds(pl.multiple_of(p.c * R, 16), R)
        wide = pl.ds(pl.multiple_of(p.x * 256, 256), 512) if kind < 2 else slice(None)
        mine = pl.ds(pl.multiple_of(p.x * 512, 256), 256)
        return w, yfirst, rc, wide, mine
    def near(s, u):
        w, yfirst, rc, wide, mine = s.geo(u); p = s.p
        ys = slice(None) if yfirst else p.y
        b = w.at[p.z, ys, rc, wide]
        return [s.move(u, 0, b, p.dev_at(p.up(1)), p.z < 3, p.z > 0), s.move(u, 1, b, p.dev_at(p.up(2))),
            s.move(u, 2, b, p.dev_at(p.up(3)), p.z > 0, p.z < 3)]
    def relay(s, u):
        w, yfirst, rc, wide, mine = s.geo(u); p = s.p
        ys = slice(None) if yfirst else p.y
        return [s.move(u, 3, w.at[p.far(), ys, rc, wide], p.dev_at(jnp.where(p.edge, p.z, 3 * p.z - 3)), p.mid, p.edge)]
    def over_y(s, u):
        w, yfirst, rc, wide, mine = s.geo(u); p = s.p
        if yfirst:
            return [s.move(u, 4, w.at[p.z, p.y, rc, wide], p.dev_y)]
        return [s.move(u, 4, w.at[:, p.y, rc, wide], p.dev_y, p.mid, p.mid),
            s.move(u, 4, w.at[pl.ds(p.z // 3, 3), p.y, rc, wide], p.dev_y, p.edge, p.edge)]
    def over_y_far(s, u):
        w, yfirst, rc, wide, mine = s.geo(u); p = s.p
        return [s.move(u, 5, w.at[p.far(), p.y, rc, wide], p.dev_y, p.edge, p.edge)]
    def over_x(s, u):
        w, yfirst, rc, wide, mine = s.geo(u); p = s.p
        return [s.move(u, 6, w.at[:, 1 - p.y, rc, mine], p.dev_x)]
    def over_x_own(s, u):
        w, yfirst, rc, wide, mine = s.geo(u); p = s.p
        return [s.move(u, 6 + d, w.at[p.up(d), p.y, rc, mine], p.dev_x) for d in (1, 2, 3)]
    def over_c(s, u):
        w, yfirst, rc, wide, mine = s.geo(u); p = s.p
        return [s.move(u, 10, w.at[:, :, rc, :], p.dev_c)]
    def plan(s, P, gate=None):
        def moves(f):
            def start():
                for m in f(): m.start()
            def finish():
                for m in f(): m.wait()
            return start, finish
        firsts, lasts, pace = [], [], 0.0
        for u in range(s.n):
            w, kind = s.units[u]
            R, b = w.shape[2] // 2, 2 * 256
            piece = R * b * (2 if kind < 2 else 3)
            k = dict(rank=u)
            first = [gate, firsts[u - s.lead] if u >= s.lead else None]
            f = lambda g, u=u: moves(lambda: g(u))
            if kind in (1, 3):
                y = P.op(*f(s.over_y), dict(y=piece), first, after=pace, **k)
                near = P.op(*f(s.near), dict(m=6 * piece, e=4 * piece, g=4 * piece), [y], **k)
                here = [P.op(*f(s.relay), dict(g=2 * piece), [near], **k)]
                if kind == 1:
                    here = [P.op(*f(lambda u: s.over_x(u) + s.over_x_own(u)), dict(x=7 * R * b), here, **k)]
                firsts.append(y)
            else:
                near = P.op(*f(s.near), dict(m=3 * piece, e=2 * piece, g=2 * piece), first, after=pace, **k)
                rel = P.op(*f(s.relay), dict(g=piece), [near], **k)
                ya = P.op(*f(s.over_y), dict(y=3.5 * piece), [near], **k)
                yb = P.op(*f(s.over_y_far), dict(y=0.5 * piece), [rel], **k)
                here = [ya, yb]
                if kind == 0:
                    xo = P.op(*f(s.over_x_own), dict(x=3 * R * b), [rel], **k)
                    here = [P.op(*f(s.over_x), dict(x=4 * R * b), here, **k), xo]
                firsts.append(near)
            c = P.op(*f(s.over_c), dict(c=24 * R * b), here, **k)
            lasts.append(c)
            pace += s.PACE * R / 48
        return lasts


class Reduce:
    def __init__(s, p, units, bufs, ssem, rsem):
        s.p, s.units, s.b, s.ss, s.rs = p, units, bufs, ssem, rsem
        s.n = len(units)
        s.kz = dict(enumerate(("z0", "z1", "z2")))
    def geo(s, u):
        w, fin, out = s.units[u]
        R = w.shape[2] // 2; p = s.p
        rc = pl.ds(pl.multiple_of(p.c * R, 16), R)
        ro = pl.ds(pl.multiple_of((1 - p.c) * R, 16), R)
        xc = pl.ds(pl.multiple_of(p.x * 384, 128), 384)
        xo = pl.ds(pl.multiple_of((1 - p.x) * 384, 128), 384)
        return w, fin, out, R, rc, ro, xc, xo
    def kind(s, u):
        return KINDS[u % len(KINDS)]
    def before(s, u, kinds):
        return [v for v in range(u) if s.kind(v) in kinds]
    def slot(s, u):
        kind = s.kind(u)
        return kind, len(s.before(u, (kind,))) % (RING if kind == 2 else RING // 2), len(s.before(u, (0, 1))) % RING
    def move(s, u, i, src, dst, dev, sends=None, takes=None):
        k = u % s.ss.shape[0]
        return Move(src, dst, s.ss.at[k, i], s.rs.at[k, i], dev, sends, takes)
    def core(s, u):
        w, fin, out, R, rc, ro, xc, xo = s.geo(u)
        return [s.move(u, 0, w.at[:, :, ro, :], s.b["c"].at[u % CRING, :, :, pl.ds(0, R), :], s.p.dev_c)]
    def add_core(s, u):
        w, fin, out, R, rc, ro, xc, xo = s.geo(u); c = s.b["c"].at[u % CRING]
        def body(i, _):
            a, b = i // 2, lax.rem(i, 2)
            w[a, b, rc, :] = w[a, b, rc, :] + c[a, b, pl.ds(0, R), :]
            return 0
        lax.fori_loop(0, 8, body, 0)
    def first(s, u):
        w, fin, out, R, rc, ro, xc, xo = s.geo(u); p = s.p
        kind, k, k2 = s.slot(u)
        if kind == 2:
            return [s.move(u, 1, w.at[:, 1 - p.y, rc, :], s.b["h1y"].at[k, :, pl.ds(0, R), :], p.dev_y)]
        return [s.move(u, 1, w.at[:, :, rc, xo], s.b["h1x"].at[k2, :, :, pl.ds(0, R), :], p.dev_x)]
    def add_first(s, u):
        w, fin, out, R, rc, ro, xc, xo = s.geo(u); p = s.p
        kind, k, k2 = s.slot(u)
        if kind == 2:
            h = s.b["h1y"].at[k]
            def body(a, _):
                w[a, p.y, rc, :] = w[a, p.y, rc, :] + h[a, pl.ds(0, R), :]
                return 0
            lax.fori_loop(0, 4, body, 0)
        else:
            h = s.b["h1x"].at[k2]
            def body(i, _):
                a, b = i // 2, lax.rem(i, 2)
                w[a, b, rc, xc] = w[a, b, rc, xc] + h[a, b, pl.ds(0, R), :]
                return 0
            lax.fori_loop(0, 8, body, 0)
    def second_y(s, u):
        w, fin, out, R, rc, ro, xc, xo = s.geo(u); p = s.p
        kind, k, k2 = s.slot(u)
        return [s.move(u, 2, w.at[:, 1 - p.y, rc, xc], s.b["h2y"].at[k, :, pl.ds(0, R), :], p.dev_y)]
    def add_second_y(s, u):
        w, fin, out, R, rc, ro, xc, xo = s.geo(u); p = s.p
        kind, k, k2 = s.slot(u)
        h = s.b["h2y"].at[k]
        def body(a, _):
            w[a, p.y, rc, xc] = w[a, p.y, rc, xc] + h[a, pl.ds(0, R), :]
            return 0
        lax.fori_loop(0, 4, body, 0)
    def zblock(s, u, z):
        w, fin, out, R, rc, ro, xc, xo = s.geo(u); p = s.p
        kind, k, k2 = s.slot(u)
        if kind == 1:
            return w.at[z, :, rc, xc]
        return w.at[z, p.y, rc, xc if kind == 0 else slice(None)]
    def zslot(s, u, d):
        kind, k, k2 = s.slot(u); R = s.geo(u)[3]
        b = s.b[s.kz[kind]]
        return b.at[k, d, :, pl.ds(0, R), :] if kind == 1 else b.at[k, d, pl.ds(0, R), :]
    def near(s, u):
        p = s.p
        one = [s.move(u, 2 + d, s.zblock(u, p.up(d)), s.zslot(u, d - 1), p.dev_at(p.up(d)), *((p.z < 3, p.z > 0) if d == 1 else (p.z > 0, p.z < 3))) for d in (1, 3)]
        return [s.far(u)] + one + [s.two(u, p.edge, p.mid)]
    def far(s, u):
        p = s.p
        return s.move(u, 6, s.zblock(u, p.far()), s.zslot(u, 3), p.dev_at(1 + p.z // 3), p.edge, p.mid)
    def two(s, u, sends, takes):
        p = s.p
        return s.move(u, 4, s.zblock(u, p.up(2)), s.zslot(u, 1), p.dev_at(p.up(2)), sends, takes)
    def far_add(s, u):
        m = s.far(u); m.got(); m.sent()
        def add():
            b, h = s.zblock(u, s.p.far()), s.zslot(u, 3)
            b[...] = b[...] + h[...]
        pl.when(s.p.mid)(add)
    def z_sum(s, u):
        f = lambda r: r[...].astype(jnp.float32)
        v = f(s.zblock(u, s.p.z))
        for d in range(3): v = v + f(s.zslot(u, d))
        return v.astype(jnp.bfloat16)
    def last_y(s, u):
        w, fin, out, R, rc, ro, xc, xo = s.geo(u); p = s.p
        kind, k, k2 = s.slot(u)
        return [s.move(u, 7, w.at[p.z, 1 - p.y, rc, xc], s.b["h3y"].at[k, pl.ds(0, R), :], p.dev_y)]
    def last_x(s, u):
        w, fin, out, R, rc, ro, xc, xo = s.geo(u); p = s.p
        kind, k, k2 = s.slot(u)
        return [s.move(u, 7, w.at[p.z, p.y, rc, :], s.b["h3x"].at[k, pl.ds(0, R), :], p.dev_x)]
    def share_x(s, u):
        w, fin, out, R, rc, ro, xc, xo = s.geo(u)
        return [s.move(u, 8, fin.at[rc, xc], fin.at[rc, xc], s.p.dev_x)]
    def share_c(s, u):
        w, fin, out, R, rc, ro, xc, xo = s.geo(u)
        return [s.move(u, 9, fin.at[rc, :], fin.at[rc, :], s.p.dev_c)]
    def out_copy(s, u):
        return pltpu.make_async_copy(s.units[u][1], s.units[u][2], s.b["osem"].at[u])
    def plan(s, P, marks, hold, gate=None):
        def run(ms):
            for m in ms: m.start()
        def wait(ms):
            for m in ms: m.wait()
        core, first, second, zs, last, share, end = [], [], [], [], [], [], []
        def back(ops, u, kinds, ring):
            same = s.before(u, kinds)
            return ops[same[-ring // 2]] if len(same) >= ring // 2 else None
        for u in range(s.n):
            w, fin, out, R, rc, ro, xc, xo = s.geo(u); p = s.p
            kind, k, k2 = s.slot(u)
            full = R * 768 * 2
            zb = full if kind != 0 else full // 2
            mine = (kind,) if kind == 2 else (0, 1)
            def f_core(u=u): wait(s.core(u)); s.add_core(u)
            def f_first(u=u): wait(s.first(u)); s.add_first(u)
            def f_second(u=u): wait(s.second_y(u)); s.add_second_y(u)
            def b_near(u=u): run(s.near(u)[1:])
            def f_near(u=u): wait(s.near(u)[1:])
            def b_rel(u=u): s.two(u, s.p.mid, s.p.edge).start()
            def f_z(u=u, w=w, fin=fin, kind=kind, rc=rc, xc=xc):
                s.two(u, s.p.mid, s.p.edge).wait()
                if kind == 0:
                    fin[rc, xc] = s.z_sum(u)
                else:
                    b = s.zblock(u, s.p.z); b[...] = s.z_sum(u)
            def f_last(u=u, w=w, fin=fin, kind=kind, rc=rc, xc=xc, R=R, k=k):
                p = s.p
                if kind == 1:
                    wait(s.last_y(u))
                    fin[rc, xc] = w[p.z, p.y, rc, xc] + s.b["h3y"][k, pl.ds(0, R), :]
                else:
                    wait(s.last_x(u))
                    fin[rc, :] = w[p.z, p.y, rc, :] + s.b["h3x"][k, pl.ds(0, R), :]
            def f_end(u=u): wait(s.share_c(u)); s.out_copy(u).start()
            c = P.op(lambda u=u: run(s.core(u)), f_core, dict(c=8 * full), [marks[u], gate, core[u - CRING // 2] if u >= CRING // 2 else None] + [end[v] for v in hold[u]], cost=0.3, rank=100 + u)
            core.append(c)
            f = P.op(lambda u=u: run(s.first(u)), f_first, dict(y=4 * full) if kind == 2 else dict(x=4 * full), [c, back(first, u, mine, RING)], cost=0.25, rank=100 + u)
            first.append(f)
            prev = f
            if kind == 0:
                prev = P.op(lambda u=u: run(s.second_y(u)), f_second, dict(y=2 * full), [f, back(second, u, (0,), RING // 2)], cost=0.15, rank=100 + u)
            second.append(prev)
            ring = back(zs, u, (kind,), RING if kind == 2 else RING // 2)
            far = P.op(lambda u=u: s.far(u).start(), lambda u=u: s.far_add(u), dict(e=zb), [prev, ring], rank=100 + u)
            near = P.op(b_near, f_near, dict(m=2 * zb, e=2 * zb, g=zb), [prev, ring], rank=100 + u)
            z = P.op(b_rel, f_z, dict(m=zb, g=zb), [far, near], cost=0.15, rank=100 + u)
            zs.append(z)
            prev = z
            if kind != 0:
                prev = P.op((lambda u=u: run(s.last_y(u))) if kind == 1 else (lambda u=u: run(s.last_x(u))), f_last,
                    dict(y=full // 2) if kind == 1 else dict(x=full), [z, back(last, u, (kind,), RING if kind == 2 else RING // 2)], rank=100 + u)
            last.append(prev)
            if kind != 2:
                prev = P.op(lambda u=u: run(s.share_x(u)), lambda u=u: wait(s.share_x(u)), dict(x=full // 2), [prev, back(share, u, (0, 1), RING)], rank=100 + u)
            share.append(prev)
            end.append(P.op(lambda u=u: run(s.share_c(u)), f_end, dict(c=full), [prev, back(end, u, (kind,), RING if kind == 2 else RING // 2)], rank=100 + u))
        return end
    def finish(s):
        for u in range(s.n): s.out_copy(u).wait()
    def clear(s):
        def zero(d):
            def f():
                for q in s.kz.values():
                    b = s.b[q]
                    for k in range(b.shape[0]):
                        b[k, d] = jnp.zeros(b.shape[2:], b.dtype)
            return f
        pl.when(s.p.z == 0)(zero(0))
        pl.when(s.p.z == 3)(zero(2))


CRING, RING = 4, 4
KINDS = (2, 0, 2, 2, 2, 1, 0, 1, 2, 0, 2, 1, 2, 0, 2, 1, 2, 0, 2, 1, 2, 0, 2, 1, 2, 0, 2, 1, 1, 0, 2, 2, 2, 2)


def reduce_scratch(n, R):
    b = jnp.bfloat16; V = pltpu.VMEM; lag = RING
    half = lag // 2
    return dict(c=V((CRING, 4, 2, R, 768), b), h1x=V((lag, 4, 2, R, 384), b), h1y=V((lag, 4, R, 768), b),
        h2y=V((half, 4, R, 384), b), z0=V((half, 4, R, 384), b), z1=V((half, 4, 2, R, 384), b), z2=V((lag, 4, R, 768), b),
        h3y=V((half, R, 384), b), h3x=V((lag, R, 768), b), osem=pltpu.SemaphoreType.DMA((n,)))
NA, ND = 8, 3
ROUTES = ((0, 0, 0, 0, 0, 0, 0, 0, 0, 0, 0), (0, 1, 0, 0, 0, 0, 0, 2, 1, 2, 3))
def gather_units(wa, wd, layer):
    return [(wa.at[layer, k] if k < NA else wd.at[layer, k - NA], ROUTES[layer][k]) for k in range(NA + ND)]

def load_shards(p, attn_in, attn_out, fc_in, fc_out, wa, wd, sem):
    out = []
    i = 0
    for l in range(2):
        for k in range(NA):
            if k < 3: src = attn_in.at[l, :, pl.ds(768 * k, 768)]
            elif k == 3: src = attn_out.at[l]
            else: src = fc_in.at[l, :, pl.ds(768 * (k - 4), 768)]
            out.append(pltpu.make_async_copy(src, wa.at[l, k, p.z, p.y], sem.at[i])); i += 1
        for k in range(ND):
            out.append(pltpu.make_async_copy(fc_out.at[l, pl.ds(128 * k, 128)], wd.at[l, k, p.z, p.y], sem.at[i])); i += 1
    return out
ORDER = [("D", 0), ("D", 1), ("D", 2), ("A", 4), ("A", 5), ("A", 6), ("A", 7), ("A", 3), ("A", 0), ("A", 1), ("A", 2)]


F32, BF = jnp.float32, jnp.bfloat16
NN = (((1,), (0,)), ((), ()))
NT = (((1,), (1,)), ((), ()))
TN = (((0,), (0,)), ((), ()))
def mm(a, b, dims=NN):
    return lax.dot_general(a, b, dims, preferred_element_type=F32)

ROWS, WIDTH, PAIRS = 512, 768, 6
def r_gain(l, i): return 2 * l + i
def r_bias(l, i): return 4 + 6 * l + i
R_EMBED = 16
def r_fcb(l, k): return 24 + 4 * l + k

def row(ref, r):
    return ref[pl.ds(r, 1), :]

def rows_loop(step, body):
    def run(i, c):
        body(pl.ds(pl.multiple_of(i * step, step), step))
        return c
    lax.fori_loop(0, ROWS // step, run, 0)

def gelu_parts(z):
    a = jnp.abs(z)
    t = 1.0 / (1.0 + (0.3275911 * 0.7071067811865476) * a)
    e = jnp.exp(-0.5 * (z * z))
    poly = t * (0.254829592 + t * (-0.284496736 + t * (1.421413741 + t * (-1.453152027 + t * 1.061405429))))
    tail = 0.5 * poly * e
    cdf = jnp.where(z < 0, tail, 1.0 - tail)
    return z * cdf, cdf + z * (0.3989422804014327 * e)

class Net:
    def __init__(s, r):
        s.__dict__.update(r)
    def w(s, l, k):
        return s.wa.at[l, k]
    def wtile(s, l, k, cols):
        v = s.wa[l, k, :, :, :, cols]
        return v.reshape(WIDTH, v.shape[-1])
    def norm(s, l, i, xh, h):
        at = pl.ds(2 * l + i, 1)
        def body(q):
            v = s.x[q, :]
            c = v - jnp.mean(v, axis=-1, keepdims=True)
            r = lax.rsqrt(jnp.mean(c * c, axis=-1, keepdims=True) + 1e-6)
            n = c * r
            xh[q, :] = n.astype(BF)
            s.rs[q, at] = r
            h[q, :] = (n * row(s.V, r_gain(l, i)) + row(s.V, r_bias(l, 4 if i else 0))).astype(BF)
        for b in range(2): body(pl.ds(256 * b, 256))
    def norm_back(s, l, i, d, xh, out):
        at = pl.ds(2 * l + i, 1)
        total = lambda v: jnp.sum(v, axis=0, keepdims=True)
        sg = sb = so = 0.0
        for b in range(2):
            q = pl.ds(256 * b, 256)
            dv, n = d[q, :], xh[q, :].astype(F32)
            dn = dv * row(s.V, r_gain(l, i))
            m1 = jnp.mean(dn, axis=-1, keepdims=True)
            m2 = jnp.mean(dn * n, axis=-1, keepdims=True)
            e = s.x[q, :] + s.rs[q, at] * (dn - m1 - n * m2)
            s.x[q, :] = e
            sg, sb = sg + total(dv * n), sb + total(dv)
            if out is not None:
                eb = e.astype(BF)
                out[q, :] = eb
                so = so + total(eb.astype(F32))
        s.S[pl.ds(r_gain(l, i), 1), :] = sg
        s.S[pl.ds(r_bias(l, 4 if i else 0), 1), :] = sb
        return so
    def unit(s, l, k):
        return s.wa[l, k].reshape(WIDTH, WIDTH)
    def project(s, l, k):
        v = mm(s.h[...], s.unit(l, k))
        if k != 1:
            v = v + row(s.V, r_bias(l, 1 if k == 0 else 2))
        s.t[k] = v.astype(BF)
    def masks(s):
        lane = lax.broadcasted_iota(jnp.int32, (1, 128), 1)
        return [(lane < 64).astype(F32).astype(BF), (lane >= 64).astype(F32).astype(BF)]
    def attend(s, l, p0, p1):
        ms = s.masks()
        def body(p, c):
            n = pl.ds(pl.multiple_of(p * 128, 128), 128)
            kk = s.t[1, :, n]
            vt = s.t[2, :, n].T
            qs = s.t[0, :, n] * 0.125
            outs = []
            for i in range(2):
                st = mm(kk, qs * ms[i], NT)
                top = jnp.max(st, axis=0, keepdims=True)
                e = jnp.exp(st - top)
                total = jnp.sum(e, axis=0, keepdims=True)
                s.lse[l, pl.ds(2 * p + i, 1), :] = top + jnp.log(total)
                outs.append(mm(vt[64 * i:64 * i + 64], e.astype(BF)) * (1.0 / total))
            s.o[:, n] = jnp.concatenate(outs, axis=0).T.astype(BF)
            return c
        lax.fori_loop(p0, p1, body, 0)
    def attend_back(s, l, p0, p1):
        ms = s.masks()
        def body(p, c):
            n = pl.ds(pl.multiple_of(p * 128, 128), 128)
            kk, vv = s.t[1, :, n], s.t[2, :, n]
            kt = kk.T
            qs = s.t[0, :, n] * 0.125
            do = s.o[:, n]
            qt, dt = qs.T, do.T
            dv, dk, dq = [], [], []
            for i in range(2):
                at = slice(64 * i, 64 * i + 64)
                pt = jnp.exp(mm(kk, qs * ms[i], NT) - s.lse[l, pl.ds(2 * p + i, 1), :])
                pd = pt * mm(vv, do * ms[i], NT)
                dv.append(mm(dt[at], pt.astype(BF), NT))
                ds = (pd - pt * jnp.sum(pd, axis=0, keepdims=True)).astype(BF)
                dk.append(mm(qt[at], ds, NT))
                dq.append(mm(kt[at], ds) * 0.125)
            for j, d in enumerate((dq, dk, dv)):
                s.t[j, :, n] = jnp.concatenate(d, axis=0).T.astype(BF)
            return c
        lax.fori_loop(p0, p1, body, 0)
    def attn_out(s, l):
        s.x[...] = s.x[...] + (mm(s.o[...], s.unit(l, 3)) + row(s.V, r_bias(l, 3)))
    def mlp_in(s, l, k):
        s.acc[...] = mm(s.h2[...], s.unit(l, 4 + k)) + row(s.V, r_fcb(l, k))
        for f in range(2):
            for j in range(3):
                a, d = gelu_parts(s.acc[:, pl.ds(384 * f + 128 * j, 128)])
                s.g[j, :, pl.ds((2 * k + f) * 128, 128)] = a.astype(BF)
                s.gp[j, :, pl.ds((2 * k + f) * 128, 128)] = d.astype(BF)
    def mlp_out(s, l, j, to):
        v = mm(s.g[j], s.wd[l, j].reshape(1024, WIDTH))
        if j == 0:
            v = v + row(s.V, r_bias(l, 5))
        to[...] = s.x[...] + v
    def start_back(s, l, make):
        if make:
            s.du[...] = s.x[...].astype(BF)
        s.col_sum(s.du, r_bias(l, 5))
    def mlp_out_back(s, l, j):
        def body(i, c):
            n = pl.ds(pl.multiple_of(i * 512, 512), 512)
            w = s.wd[l, j, pl.ds(2 * i, 2)].reshape(512, WIDTH)
            dz = (mm(s.du[...], w, NT) * s.gp[j, :, n].astype(F32)).astype(BF)
            s.gp[j, :, n] = dz
            s.bz[pl.ds(3 * l + j, 1), n] = jnp.sum(dz.astype(F32), axis=0, keepdims=True)
            return c
        lax.fori_loop(0, 2, body, 0)
    def mlp_out_grad(s, l, j, to):
        for i in range(2):
            to[pl.ds(2 * i, 2)] = mm(s.g[j, :, pl.ds(512 * i, 512)], s.du[...], TN).astype(BF).reshape(2, 2, 128, WIDTH)
    def hidden_bias(s):
        for l in range(2):
            for j in range(3):
                for f in range(8):
                    s.S[pl.ds(r_fcb(l, f // 2), 1), pl.ds(384 * (f % 2) + 128 * j, 128)] = s.bz[pl.ds(3 * l + j, 1), pl.ds(128 * f, 128)]
    def dz_tile(s, k, q):
        parts = []
        for f in range(2):
            for j in range(3):
                parts.append(s.gp[j, q, pl.ds((2 * k + f) * 128, 128)])
        return jnp.concatenate(parts, axis=1)
    def back_mm(s, l, k, get, first):
        v = mm(get(slice(None)), s.unit(l, k), NT)
        s.acc[...] = v if first else s.acc[...] + v
    def grad_a(s, to, get, lhs):
        to[...] = mm(lhs[...], get(slice(None)), TN).astype(BF).reshape(4, 2, 96, WIDTH)
    def attn_out_back(s, l):
        do = mm(s.du[...], s.unit(l, 3), NT).astype(BF)
        s.grad_a(s.w(l, 3), lambda q: s.du[q, :], s.o)
        s.o[...] = do
    def col_sum(s, ref, r):
        s.S[pl.ds(r, 1), :] = jnp.sum(ref[...].astype(F32), axis=0, keepdims=True)

def net_scratch():
    V = pltpu.VMEM
    return dict(x=V((512, 768), F32), acc=V((512, 768), F32), h=V((512, 768), BF), t=V((3, 512, 768), BF), lse=V((2, 16, 512), F32),
        o=V((512, 768), BF), h2=V((512, 768), BF), g=V((3, 512, 1024), BF), gp=V((3, 512, 1024), BF), xh1=V((512, 768), BF), xh2=V((512, 768), BF),
        rs=V((512, 128), F32), du=V((512, 768), BF),
        bz=V((8, 1024), F32), V=V((32, 768), F32), S=V((32, 768), F32))
SPILL = ["h", "t", "o", "h2", "g", "gp", "xh1", "xh2"]


SMALL = (32, 768)
VMEM_LIMIT = 63 * 1024 * 1024
EARLY = {21: 32, 0: 32, 20: 64, 2: 32}
LEAD = 30
CUTS = {(0, 'A', 1): [32, 32, 32], (0, 'A', 2): [32, 64], (0, 'A', 7): [64, 32]}
SOON = 2
DCUT = [64, 64]
SEG, SEGB = 3, 2


def gather_list(wa, wd):
    units, first = [], []
    for l in range(2):
        for w, kind in gather_units(wa, wd, l):
            h = EARLY.get(len(first), w.shape[2])
            units += [(w.at[:, :, pl.ds(a, h), :], kind) for a in range(0, w.shape[2], h)]
            first.append(len(units) - 1)
    return units, first


def reduce_list():
    out = []
    for l in (1, 0):
        for k, q in ORDER:
            H = 128 if k == "D" else 96
            hs = CUTS.get((l, k, q), DCUT if k == "D" else [H])
            a = 0
            for h in hs:
                out.append((l, k, q, a, h)); a += h
    return out


def steps(P, n, unit, marks, sent, do):
    P.step(do.embed, 1.5, [do.params])
    for l in range(2):
        P.step(lambda l=l: (do.reuse(l, "xh1", "h"), n.norm(l, 0, n.xh1, n.h), do.keep(l, "xh1")), 0.5)
        for k in range(3):
            P.step(lambda l=l, k=k: (do.reuse(l, *(["t"] if k == 0 else [])), n.project(l, k)), 1.0, [unit(l, k)])
        for a in range(0, 6, SEG):
            P.step(lambda l=l, a=a: (do.keep(l, *(["h", "t"] if a == 0 else [])), do.reuse(l, *(["o"] if a == 0 else [])), n.attend(l, a, a + SEG)), 1.25 * SEG)
        P.step(lambda l=l: (do.keep(l, "o"), n.attn_out(l)), 1.0, [unit(l, 3)])
        P.step(lambda l=l: (do.reuse(l, "xh2", "h2"), n.norm(l, 1, n.xh2, n.h2), do.keep(l, "xh2")), 0.5)
        for k in range(4):
            P.step(lambda l=l, k=k: (do.reuse(l, *(["g", "gp"] if k == 0 else [])), n.mlp_in(l, k)), 1.4, [unit(l, 4 + k)])
        if l == 1:
            P.step(lambda: n.start_back(1, False), 0.2)
            for j in range(SOON):
                P.step(lambda j=j: n.mlp_out_grad(1, j, n.wg.at[j]), 1.1, (), marks(1, "D", j))
        for j in range(3):
            P.step(lambda l=l, j=j: (do.keep(l, *(["h2", "gp"] if j == 0 else [])), n.mlp_out(l, j, n.acc if (l == 1 and j == 2) else n.x)), 1.2, [unit(l, 8 + j)])
        P.step(lambda l=l: do.keep(l, "g"), 0.0)
    P.step(do.turn, 0.8)
    for l in (1, 0):
        if l == 0:
            P.step(lambda: n.start_back(0, True), 0.3)
        for j in range(3):
            late = l == 0 or j >= SOON
            P.step(lambda l=l, j=j, late=late: (do.need(l, *(["gp", "g"] if j == 0 else [])), n.mlp_out_back(l, j),
                late and n.mlp_out_grad(l, j, n.wd.at[l, j])), 2.4 if late else 1.4, (), marks(l, "D", j) if late else ())
        P.step(lambda l=l: (do.done(l, "g"), do.need(l, "h2")), 0.0)
        for k in range(4):
            get = lambda q, k=k: n.dz_tile(k, q)
            P.step(lambda l=l, k=k, get=get: (n.back_mm(l, 4 + k, get, k == 0), n.grad_a(n.w(l, 4 + k), get, n.h2)), 1.6, (), marks(l, "A", 4 + k))
        P.step(lambda l=l: (do.done(l, "gp", "h2"), do.need(l, "xh2"), do.mid_norm(l), do.done(l, "xh2"), do.need(l, "o")), 1.0)
        P.step(lambda l=l: n.attn_out_back(l), 1.6, (), marks(l, "A", 3))
        P.step(lambda l=l: do.need(l, "t"), 0.0)
        for a in range(0, 6, SEGB):
            P.step(lambda l=l, a=a: n.attend_back(l, a, a + SEGB), 1.85 * SEGB)
        P.step(lambda l=l: (do.done(l, "o"), do.need(l, "h"), n.col_sum(n.t.at[0], r_bias(l, 1)), n.col_sum(n.t.at[2], r_bias(l, 2))), 0.3)
        for k in range(3):
            get = lambda q, k=k: n.t[k, q, :]
            if l == 1:
                P.step(lambda l=l, k=k, get=get: (n.back_mm(l, k, get, k == 0), n.grad_a(n.w(l, k), get, n.h)), 1.6, (), marks(l, "A", k))
            else:
                P.step(lambda k=k, get=get: n.grad_a(n.w(1, 4 + k), get, n.h), 1.0, sent(1, "A", 4 + k), marks(0, "A", k))
        for k in range(3 if l == 0 else 0):
            P.step(lambda k=k: n.back_mm(0, k, lambda q: n.t[k, q, :], k == 0), 1.0)
        P.step(lambda l=l: (do.done(l, "t", "h"), do.need(l, "xh1"), n.norm_back(l, 0, n.acc, n.xh1, None), do.done(l, "xh1")), 1.0)
    P.step(do.last, 1.0, (), [do.sums])


class Smalls:
    def __init__(s, p, net, b):
        s.p, s.net, s.b = p, net, b
    def pack(s, gains, biases, embed, fcb):
        k = s.b["own"]
        k[...] = jnp.zeros((32, 128), F32)
        for l in range(2):
            k[2 * l:2 * l + 2, 0:96] = gains[l].astype(F32)
            k[4 + 6 * l:10 + 6 * l, 0:96] = biases[l].astype(F32)
            for i in range(3):
                k[24 + 3 * l + i:25 + 3 * l + i, :] = fcb[l:l + 1, 128 * i:128 * i + 128].astype(F32)
        k[16:17, 0:96] = embed[...].astype(F32)
        s.b["sm"][s.p.fs] = k[...].astype(BF)
    def fetch(s, d):
        b, p = s.b, s.p
        return remote(b["sm"].at[p.fs], b["sm"].at[p.fs], b["ss"].at[d - 1], b["rs"].at[d - 1], p.dev_f(d))
    def start(s):
        for d in range(1, 8):
            s.fetch(d).start()
    def build(s):
        for d in range(1, 8):
            s.fetch(d).wait()
        V = s.net.V
        i = lax.broadcasted_iota(jnp.int32, (128, 768), 0)
        c = lax.broadcasted_iota(jnp.int32, (128, 768), 1)
        total = jnp.zeros((24, 768), F32)
        for f in range(8):
            blk = s.b["sm"][f]
            pick = jnp.where((c - 96 * f == i) & (i < 96), 1.0, 0.0).astype(BF)
            total = total + mm(blk, pick)[0:24]
        V[0:24, :] = total
        for f in range(8):
            blk = s.b["sm"][f].astype(F32)
            for l in range(2):
                for j in range(3):
                    at = 384 * (f % 2) + 128 * j
                    V[r_fcb(l, f // 2):r_fcb(l, f // 2) + 1, at:at + 128] = blk[24 + 3 * l + j:25 + 3 * l + j]
    def hop(s, h):
        b, p, S = s.b, s.p, s.net.S
        if h < 3:
            return [remote(S, b["sr"].at[h], b["ss"].at[7 + h], b["rs"].at[7 + h], (p.dev_c, p.dev_x, p.dev_y)[h])]
        return [remote(S, b["sr"].at[2 + d], b["ss"].at[9 + d], b["rs"].at[9 + d], p.dev_at(p.up(d))) for d in (1, 2, 3)]
    def send(s, h):
        for q in s.hop(h): q.start()
    def add(s, h):
        for q in s.hop(h): q.wait()
        t = s.net.S[...]
        for i in ([h] if h < 3 else [3, 4, 5]):
            t = t + s.b["sr"][i]
        s.net.S[...] = t
    def plan(s, P, begin):
        prev = begin
        for h, r in enumerate("cxym"):
            prev = P.op(lambda h=h: s.send(h), lambda h=h: s.add(h), {r: 98304 * (4 if r == "m" else 1)}, [prev], rank=-1)
        return prev
    def own(s):
        k, S, f = s.b["own"], s.net.S, s.p.fs
        k[...] = jnp.zeros((32, 128), F32)
        v = jnp.zeros((24, 96), F32)
        for i in range(8):
            v = jnp.where(f == i, S[0:24, 96 * i:96 * i + 96], v)
        k[0:24, 0:96] = v
        for l in range(2):
            w = jnp.zeros((1, 384), F32)
            for i in range(8):
                w = jnp.where(f == i, S[r_fcb(l, i // 2):r_fcb(l, i // 2) + 1, 384 * (i % 2):384 * (i % 2) + 384], w)
            for j in range(3):
                k[24 + 3 * l + j:25 + 3 * l + j, :] = w[:, 128 * j:128 * j + 128]


def remote(src, dst, ss, rs, dev):
    return pltpu.make_async_remote_copy(src_ref=src, dst_ref=dst, send_sem=ss, recv_sem=rs, device_id=dev, device_id_type=MESH)


def smalls_scratch():
    return dict(sm=pltpu.VMEM((8, 32, 128), BF), own=pltpu.VMEM((32, 128), F32), sr=pltpu.VMEM((6, 32, 768), F32),
        ss=pltpu.SemaphoreType.DMA((13,)), rs=pltpu.SemaphoreType.DMA((13,)))


class Work:
    pass


def whole_kernel(tok, cot, msk, gains, biases, embed, fcb, ai, ao, fi, fo, act, ig, so, o_ai, o_ao, o_fi, o_fo, *rest):
    spill = dict(zip(SPILL, rest[:8]))
    sc, wa, wd, wg, fa, fd, rbufs, sbufs, lsem, ssem, iosem, gss, grs, rss, rrs = rest[8:]
    p = Pos()
    n = Net(dict(sc, wa=wa, wd=wd, wg=wg))
    sm = Smalls(p, n, sbufs)
    tok_in = pltpu.make_async_copy(tok, n.o, iosem.at[0])
    cot_in = pltpu.make_async_copy(cot, n.du, iosem.at[1])
    loads = load_shards(p, ai, ao, fi, fo, wa, wd, lsem)
    for c in loads: c.start()
    tok_in.start(); cot_in.start()
    red = []
    for l, k, q, a, h in reduce_list():
        if (l, k) == (0, "A") and q < 3: w = wa.at[1, 4 + q]
        elif (l, k) == (1, "D") and q < SOON: w = wg.at[q]
        else: w = (wd if k == "D" else wa).at[l, q]
        b = q if k == "A" else 8 + q
        if l == 1: f = (fd if k == "D" else fa).at[q, pl.ds(a, h)]
        else: f = wg.at[b // 8, b % 8 // 2, b % 2, pl.ds(a, h)]
        if k == "D": o = o_fo.at[l, pl.ds(128 * q + a, h)]
        elif q == 3: o = o_ao.at[l, pl.ds(a, h)]
        elif q < 3: o = o_ai.at[l, pl.ds(a, h), pl.ds(768 * q, 768)]
        else: o = o_fi.at[l, pl.ds(a, h), pl.ds(768 * (q - 4), 768)]
        red.append((w.at[:, :, pl.ds(a, h), :], f, o))
    r = Reduce(p, red, rbufs, rss, rrs)
    r.clear()
    sm.pack(gains, biases, embed, fcb)
    mt = msk[...].astype(F32).T
    for j in range(4):
        n.rs[128 * j:128 * j + 128, 4:5] = mt[:, j:j + 1]
    for c in loads: c.wait()
    barrier(p)
    units, part = gather_list(wa, wd)
    g = Gather(p, units, gss, grs, LEAD)
    P = Plan()
    out_of = lambda nm: pltpu.make_async_copy(sc[nm], spill[nm], ssem.at[SPILL.index(nm)])
    back_to = lambda nm: pltpu.make_async_copy(spill[nm], sc[nm], ssem.at[SPILL.index(nm)])
    act_out = pltpu.make_async_copy(n.acc, act, iosem.at[0])
    ig_out = pltpu.make_async_copy(n.acc, ig, iosem.at[1])

    class Do(Work):
        params = P.op(sm.start, sm.build, dict(y=40e3), (), cost=1.0, rank=-1)
        sums = P.mark()
        @staticmethod
        def reuse(l, *nms):
            for m in nms if l == 1 else (): out_of(m).wait()
        @staticmethod
        def keep(l, *nms):
            for m in nms if l == 0 else (): out_of(m).start()
        @staticmethod
        def need(l, *nms):
            for m in nms if l == 0 else (): back_to(m).wait()
        @staticmethod
        def done(l, *nms):
            for m in nms if l == 1 else (): back_to(m).start()
        @staticmethod
        def embed():
            tok_in.wait(); cot_in.wait()
            n.S[...] = jnp.zeros(SMALL, F32)
            def body(q):
                m = n.rs[q, 4:5]
                n.x[q, :] = n.o[q, :].astype(F32) * (1.0 - m) + m * row(n.V, R_EMBED)
            rows_loop(64, body)
        @staticmethod
        def turn():
            act_out.start()
            def body(q):
                n.x[q, :] = n.du[q, :].astype(F32)
            rows_loop(64, body)
            act_out.wait()
        @staticmethod
        def mid_norm(l):
            n.S[pl.ds(r_bias(l, 3), 1), :] = n.norm_back(l, 1, n.acc, n.xh2, n.du)
        @staticmethod
        def last():
            n.hidden_bias()
            def body(j, c):
                q = pl.ds(pl.multiple_of(j * 64, 64), 64)
                m, e = n.rs[q, 4:5], n.x[q, :]
                n.acc[q, :] = e * (1.0 - m)
                return c + jnp.sum(e * m, axis=0, keepdims=True)
            n.S[pl.ds(R_EMBED, 1), :] = lax.fori_loop(0, ROWS // 64, body, jnp.zeros((1, WIDTH), F32))
            ig_out.start()

    make_plan(P, n, g, part, r, sm, Do)
    P.run()
    sm.own()
    s_out = pltpu.make_async_copy(sbufs["own"], so, iosem.at[2])
    s_out.start()
    r.finish()
    ig_out.wait()
    s_out.wait()


def make_plan(P, n, g, part, r, sm, do):
    lasts = g.plan(P)
    marks = {}
    order = []
    for l, k, q, a, h in reduce_list():
        m = P.mark()
        marks.setdefault((l, k, q), []).append(m)
        order.append(m)
    lst = reduce_list()
    early = [u for u, v in enumerate(lst) if v[:2] == (1, "D") and v[2] < SOON]
    ends = r.plan(P, order, [early if v[0] == 0 else () for v in lst])
    gone = {}
    for (l, k, q, a, h), e in zip(reduce_list(), ends):
        gone.setdefault((l, k, q), []).append(e)
    sm.plan(P, do.sums)
    steps(P, n, lambda l, k: lasts[part[11 * l + k]], lambda l, k, q: marks[(l, k, q)], lambda l, k, q: gone[(l, k, q)], do)


def whole(tok, cot, msk, gains, biases, embed, fcb, ai, ao, fi, fo):
    net = net_scratch()
    any_, vm = pl.BlockSpec(memory_space=pl.ANY), pl.BlockSpec(memory_space=pltpu.VMEM)
    sa, sd = (2, 8, 4, 2, 96, 768), (2, 3, 4, 2, 128, 768)
    fa, fd = (8, 96, 768), (3, 128, 768)
    shapes = [((512, 768), F32), ((512, 768), F32), ((32, 128), F32), (ai.shape, BF), (ao.shape, BF), (fi.shape, BF), (fo.shape, BF)]
    shapes += [(net[k].shape, net[k].dtype) for k in SPILL]
    dma = pltpu.SemaphoreType.DMA
    parts, red = 22 + sum((96 if u % 11 < 8 else 128) // h - 1 for u, h in EARLY.items()), reduce_list()
    R = max(v[4] for v in red) // 2
    return pl.pallas_call(
        whole_kernel,
        out_shape=[jax.ShapeDtypeStruct(*v) for v in shapes],
        in_specs=[any_, any_, vm, vm, vm, vm, vm] + [any_] * 4,
        out_specs=[any_] * len(shapes),
        scratch_shapes=[
            net, pltpu.VMEM(sa, BF), pltpu.VMEM(sd, BF), pltpu.VMEM((SOON,) + sd[2:], BF), pltpu.VMEM(fa, BF), pltpu.VMEM(fd, BF),
            reduce_scratch(len(red), R), smalls_scratch(), dma((22,)), dma((8,)), dma((3,)),
            dma((parts, 11)), dma((parts, 11)), dma((len(red), 10)), dma((len(red), 10)),
        ],
        compiler_params=pltpu.CompilerParams(collective_id=0, has_side_effects=True, vmem_limit_bytes=VMEM_LIMIT),
    )(tok, cot, msk, gains, biases, embed, fcb, ai, ao, fi, fo)[:7]


def results_kernel(act_i, ig_i, own, g0, g1, g2, g3, act, ig, embed, o0, o1, o2, o3, gains, biases, fcb, narrow, full, rows, isem, osem):
    grads, outs = (g0, g1, g2, g3), (o0, o1, o2, o3)
    loads = [pltpu.make_async_copy(g, b, isem.at[i]) for i, (g, b) in enumerate(zip(grads, narrow))]
    stores = [pltpu.make_async_copy(b, o, osem.at[i]) for i, (b, o) in enumerate(zip(full, outs))]
    loads += [pltpu.make_async_copy(v, rows.at[i], isem.at[4 + i]) for i, v in enumerate((act_i, ig_i))]
    stores += [pltpu.make_async_copy(rows.at[i], v, osem.at[4 + i]) for i, v in enumerate((act, ig))]
    for c in loads:
        c.start()
    for l in range(2):
        gains[l] = own[2 * l:2 * l + 2, 0:96]
        biases[l] = own[4 + 6 * l:10 + 6 * l, 0:96]
        for i in range(3):
            fcb[l:l + 1, 128 * i:128 * i + 128] = own[24 + 3 * l + i:25 + 3 * l + i, :]
    embed[...] = own[16:17, 0:96]
    for i in range(4):
        loads[i].wait()
        full[i][...] = narrow[i][...].astype(F32)
        stores[i].start()
    for i in (4, 5):
        loads[i].wait()
        stores[i].start()
    for c in stores:
        c.wait()


def results(act, ig, own, *grads):
    any_, vm = pl.BlockSpec(memory_space=pl.ANY), pl.BlockSpec(memory_space=pltpu.VMEM)
    f = lambda *s: jax.ShapeDtypeStruct(s, F32)
    return pl.pallas_call(
        results_kernel,
        out_shape=[f(*act.shape), f(*ig.shape), f(1, 96)] + [f(*g.shape) for g in grads] + [f(2, 2, 96), f(2, 6, 96), f(2, 384)],
        in_specs=[any_, any_, vm] + [any_] * 4,
        out_specs=[any_, any_, vm] + [any_] * 4 + [vm] * 3,
        scratch_shapes=[
            [pltpu.VMEM(g.shape, BF) for g in grads], [pltpu.VMEM(g.shape, F32) for g in grads],
            pltpu.VMEM((2,) + act.shape, F32), pltpu.SemaphoreType.DMA((6,)), pltpu.SemaphoreType.DMA((6,)),
        ],
        compiler_params=pltpu.CompilerParams(vmem_limit_bytes=VMEM_LIMIT),
    )(act, ig, own, *grads)


def fused_local(tokens, mask, cotangent, mask_embed, attn_in, attn_out, fc_in, fc_out, gains, biases, fc_bias):
    out = list(results(*whole(
        tokens, cotangent, mask.reshape(4, 128), gains, biases, mask_embed.reshape(1, 96), fc_bias, attn_in, attn_out, fc_in, fc_out)))
    out[2] = out[2].reshape(96)
    return tuple(out)


def solution(mesh):
    if dict(mesh.shape) != {"dp": 4, "fsdp": 8}:
        return generic_solution(mesh)
    rows = P(("dp", "fsdp"), None)
    mat = P(None, "fsdp", None)
    vec = P(None, None, "fsdp")
    return jax.shard_map(
        fused_local, mesh=mesh,
        in_specs=(rows, P(("dp", "fsdp")), rows, P("fsdp"), mat, mat, mat, mat, vec, vec, P(None, "fsdp")),
        out_specs=(rows, rows, P("fsdp"), mat, mat, mat, mat, vec, vec, P(None, "fsdp")),
        check_vma=False)


HEADS = 12
SEQ = 512
LAYERS = 2


eps = 1e-06


def norm_rows(values, gain, bias):
    center = values - jnp.mean(values, axis=-1, keepdims=True)
    spread = jnp.mean(center * center, axis=-1, keepdims=True)
    return center * lax.rsqrt(spread + eps) * gain + bias


def gelu_exact(values):
    return jax.nn.gelu(values, approximate=False)


def split_heads(values, clips):
    width = values.shape[1]
    return values.reshape(clips, SEQ, HEADS, width // HEADS)


def attend(pack):
    query, key_rows, value = pack
    scale = query.shape[-1] ** (-0.5)
    scores = jnp.einsum("qhd,khd->hqk", query, key_rows, preferred_element_type=jnp.float32) * scale
    top = jnp.max(scores, axis=-1, keepdims=True)
    expo = jnp.exp(scores - top)
    total = jnp.sum(expo, axis=-1, keepdims=True)
    probs = (expo / total).astype(jnp.bfloat16)
    mixed = jnp.einsum("hqk,khd->qhd", probs, value, preferred_element_type=jnp.float32)
    return (mixed, top + jnp.log(total))


def attend_back(pack):
    query, key_rows, value, logsum, d_mixed = pack
    scale = query.shape[-1] ** (-0.5)
    scores = jnp.einsum("qhd,khd->hqk", query, key_rows, preferred_element_type=jnp.float32) * scale
    probs = jnp.exp(scores - logsum)
    d_probs = jnp.einsum("qhd,khd->hqk", d_mixed, value, preferred_element_type=jnp.float32)
    d_value = jnp.einsum(
        "hqk,qhd->khd", probs.astype(jnp.bfloat16), d_mixed, preferred_element_type=jnp.float32
    )
    d_scores = probs * (d_probs - jnp.sum(probs * d_probs, axis=-1, keepdims=True))
    d_scaled = d_scores.astype(jnp.bfloat16) * scale
    d_query = jnp.einsum("hqk,khd->qhd", d_scaled, key_rows, preferred_element_type=jnp.float32)
    d_key = jnp.einsum("hqk,qhd->khd", d_scaled, query, preferred_element_type=jnp.float32)
    return (d_query, d_key, d_value)


def layer_forward(state, weights):
    w_qkv, w_out, w_in, w_down, gain, bias, fcb = weights
    rows, width = state.shape
    clips = rows // SEQ
    normed = norm_rows(state, gain[0].astype(jnp.float32), bias[0].astype(jnp.float32)).astype(
        jnp.bfloat16
    )
    qkv_bias = jnp.concatenate([bias[1], jnp.zeros_like(bias[1]), bias[2]]).astype(jnp.float32)
    joined = (jnp.dot(normed, w_qkv, preferred_element_type=jnp.float32) + qkv_bias).astype(
        jnp.bfloat16
    )
    query = split_heads(joined[:, :width], clips)
    key_rows = split_heads(joined[:, width : 2 * width], clips)
    value = split_heads(joined[:, 2 * width :], clips)
    mixed, logsum = lax.map(attend, (query, key_rows, value))
    mixed = mixed.reshape(rows, width).astype(jnp.bfloat16)
    middle = (
        state
        + jnp.dot(mixed, w_out, preferred_element_type=jnp.float32)
        + bias[3].astype(jnp.float32)
    )
    normed_two = norm_rows(middle, gain[1].astype(jnp.float32), bias[4].astype(jnp.float32)).astype(
        jnp.bfloat16
    )
    hidden = jnp.dot(normed_two, w_in, preferred_element_type=jnp.float32) + fcb.astype(jnp.float32)
    activated = gelu_exact(hidden).astype(jnp.bfloat16)
    return (normed, query, key_rows, value, logsum, mixed, middle, normed_two, hidden, activated)


def layer_finish(saved, weights):
    middle = saved[6]
    activated = saved[9]
    return (
        middle
        + jnp.dot(activated, weights[3], preferred_element_type=jnp.float32)
        + weights[5][5].astype(jnp.float32)
    )


def layer_backward(state, weights, grad):
    w_qkv, w_out, w_in, w_down, gain, bias, fcb = weights
    rows, width = state.shape
    clips = rows // SEQ
    normed, query, key_rows, value, logsum, mixed, middle, normed_two, hidden, activated = (
        layer_forward(state, weights)
    )
    d_up = grad.astype(jnp.bfloat16)
    g_down = jnp.einsum("tf,td->fd", activated, d_up, preferred_element_type=jnp.float32)
    d_two = jnp.sum(d_up.astype(jnp.float32), axis=0)
    d_act = jnp.einsum("td,fd->tf", d_up, w_down, preferred_element_type=jnp.float32)
    d_hidden = jax.vjp(gelu_exact, hidden)[1](d_act)[0].astype(jnp.bfloat16)
    g_in = jnp.einsum("td,tf->df", normed_two, d_hidden, preferred_element_type=jnp.float32)
    d_one = jnp.sum(d_hidden.astype(jnp.float32), axis=0)
    d_normed_two = jnp.einsum("tf,df->td", d_hidden, w_in, preferred_element_type=jnp.float32)
    back_two = jax.vjp(norm_rows, middle, gain[1].astype(jnp.float32), bias[4].astype(jnp.float32))[
        1
    ]
    d_middle, d_gain_two, d_bias_two = back_two(d_normed_two)
    d_middle = grad + d_middle
    d_branch = d_middle.astype(jnp.bfloat16)
    g_out = jnp.einsum("td,te->de", mixed, d_branch, preferred_element_type=jnp.float32)
    d_outb = jnp.sum(d_branch.astype(jnp.float32), axis=0)
    d_mixed = jnp.einsum("te,de->td", d_branch, w_out, preferred_element_type=jnp.float32).astype(
        jnp.bfloat16
    )
    d_query, d_key, d_value = lax.map(
        attend_back, (query, key_rows, value, logsum, split_heads(d_mixed, clips))
    )
    d_joined = jnp.concatenate(
        [d_query.reshape(rows, width), d_key.reshape(rows, width), d_value.reshape(rows, width)],
        axis=1,
    ).astype(jnp.bfloat16)
    g_qkv = jnp.einsum("td,te->de", normed, d_joined, preferred_element_type=jnp.float32)
    d_sums = jnp.sum(d_joined.astype(jnp.float32), axis=0)
    d_normed = jnp.einsum("te,de->td", d_joined, w_qkv, preferred_element_type=jnp.float32)
    back_one = jax.vjp(norm_rows, state, gain[0].astype(jnp.float32), bias[0].astype(jnp.float32))[
        1
    ]
    d_state, d_gain_one, d_bias_one = back_one(d_normed)
    gain_terms = jnp.stack([d_gain_one, d_gain_two])
    bias_terms = jnp.stack(
        [d_bias_one, d_sums[:width], d_sums[2 * width :], d_outb, d_bias_two, d_two]
    )
    return (d_middle + d_state, (g_qkv, g_out, g_in, g_down, gain_terms, bias_terms, d_one))


def local(
    tokens, mask, cotangent, mask_embed, attn_in, attn_out, fc_in, fc_out, gains, biases, fc_bias
):
    mask_f = mask.astype(jnp.float32)[:, None]
    state = tokens.astype(jnp.float32)
    stored = []
    kept = []
    for layer in range(LAYERS):
        fetched = (
            lax.all_gather(attn_in[layer], "fsdp", axis=0, tiled=True),
            lax.all_gather(attn_out[layer], "fsdp", axis=0, tiled=True),
            lax.all_gather(fc_in[layer], "fsdp", axis=0, tiled=True),
            lax.all_gather(fc_out[layer], "fsdp", axis=0, tiled=True),
            lax.all_gather(gains[layer], "fsdp", axis=1, tiled=True),
            lax.all_gather(biases[layer], "fsdp", axis=1, tiled=True),
            lax.all_gather(fc_bias[layer], "fsdp", axis=0, tiled=True),
            lax.all_gather(mask_embed, "fsdp", axis=0, tiled=True),
        )
        if layer == 0:
            state = state * (1.0 - mask_f) + mask_f * fetched[7].astype(jnp.float32)
        stored.append(state)
        weights = tuple(fetched[:7])
        kept.append(weights)
        state = layer_finish(layer_forward(state, weights), weights)
    grad = cotangent.astype(jnp.float32)
    layer_grads = [None] * LAYERS
    for layer in reversed(range(LAYERS)):
        weights = tuple(
            (
                lax.all_gather(attn_in[layer], "fsdp", axis=0, tiled=True),
                lax.all_gather(attn_out[layer], "fsdp", axis=0, tiled=True),
                lax.all_gather(fc_in[layer], "fsdp", axis=0, tiled=True),
                lax.all_gather(fc_out[layer], "fsdp", axis=0, tiled=True),
                lax.all_gather(gains[layer], "fsdp", axis=1, tiled=True),
                lax.all_gather(biases[layer], "fsdp", axis=1, tiled=True),
                lax.all_gather(fc_bias[layer], "fsdp", axis=0, tiled=True),
            )
        )
        grad, terms = layer_backward(stored[layer], weights, grad)
        if layer == 0:
            mask_term = jnp.sum(grad * mask_f, axis=0)
        else:
            mask_term = jnp.zeros((grad.shape[1],), jnp.float32)
        shares = (
            lax.psum_scatter(terms[0], "fsdp", scatter_dimension=0, tiled=True),
            lax.psum_scatter(terms[1], "fsdp", scatter_dimension=0, tiled=True),
            lax.psum_scatter(terms[2], "fsdp", scatter_dimension=0, tiled=True),
            lax.psum_scatter(terms[3], "fsdp", scatter_dimension=0, tiled=True),
            lax.psum_scatter(terms[4], "fsdp", scatter_dimension=1, tiled=True),
            lax.psum_scatter(terms[5], "fsdp", scatter_dimension=1, tiled=True),
            lax.psum_scatter(terms[6], "fsdp", scatter_dimension=0, tiled=True),
            lax.psum_scatter(mask_term, "fsdp", scatter_dimension=0, tiled=True),
        )
        slices = (
            lax.psum_scatter(
                shares[0].astype(jnp.bfloat16), "dp", scatter_dimension=1, tiled=True
            ).astype(jnp.float32),
            lax.psum_scatter(
                shares[1].astype(jnp.bfloat16), "dp", scatter_dimension=1, tiled=True
            ).astype(jnp.float32),
            lax.psum_scatter(
                shares[2].astype(jnp.bfloat16), "dp", scatter_dimension=1, tiled=True
            ).astype(jnp.float32),
            lax.psum_scatter(
                shares[3].astype(jnp.bfloat16), "dp", scatter_dimension=1, tiled=True
            ).astype(jnp.float32),
        )
        matrices = (
            lax.all_gather(slices[0].astype(jnp.bfloat16), "dp", axis=1, tiled=True).astype(
                jnp.float32
            ),
            lax.all_gather(slices[1].astype(jnp.bfloat16), "dp", axis=1, tiled=True).astype(
                jnp.float32
            ),
            lax.all_gather(slices[2].astype(jnp.bfloat16), "dp", axis=1, tiled=True).astype(
                jnp.float32
            ),
            lax.all_gather(slices[3].astype(jnp.bfloat16), "dp", axis=1, tiled=True).astype(
                jnp.float32
            ),
        )
        smalls = lax.psum((shares[4], shares[5], shares[6], shares[7]), "dp")
        layer_grads[layer] = (
            matrices[0],
            matrices[1],
            matrices[2],
            matrices[3],
            smalls[0],
            smalls[1],
            smalls[2],
            smalls[3],
        )
    input_grad = grad * (1.0 - mask_f)
    stacked = [jnp.stack([layer_grads[lay][item] for lay in range(LAYERS)]) for item in range(7)]
    results = tuple(stacked) + (layer_grads[0][7],)
    return (
        state,
        input_grad,
        results[7],
        results[0],
        results[1],
        results[2],
        results[3],
        results[4],
        results[5],
        results[6],
    )


def generic_solution(mesh):
    placed = (
        P(("dp", "fsdp"), None),
        P(("dp", "fsdp")),
        P(("dp", "fsdp"), None),
        P("fsdp"),
        P(None, "fsdp", None),
        P(None, "fsdp", None),
        P(None, "fsdp", None),
        P(None, "fsdp", None),
        P(None, None, "fsdp"),
        P(None, None, "fsdp"),
        P(None, "fsdp"),
    )
    return jax.shard_map(
        local,
        mesh=mesh,
        in_specs=placed,
        out_specs=(
            P(("dp", "fsdp"), None),
            P(("dp", "fsdp"), None),
            P("fsdp"),
            P(None, "fsdp", None),
            P(None, "fsdp", None),
            P(None, "fsdp", None),
            P(None, "fsdp", None),
            P(None, None, "fsdp"),
            P(None, None, "fsdp"),
            P(None, "fsdp"),
        ),
        check_vma=False,
    )
```

```python
import functools

import jax
import jax.numpy as jnp
from jax import lax
from jax.experimental import pallas as pl
from jax.experimental.pallas import tpu as pltpu
from jax.sharding import PartitionSpec as P
MESH = pl.DeviceIdType.MESH


class Pos:
    def __init__(s):
        s.dp = lax.axis_index("dp"); s.fs = lax.axis_index("fsdp")
        s.x = s.dp // 2; s.c = lax.rem(s.dp, 2)
        s.z = s.fs // 2; s.y = lax.rem(s.fs, 2)
        s.dev_c = (s.dp + 1 - 2 * s.c, s.fs)
        s.dev_x = (lax.rem(s.dp + 2, 4), s.fs)
        s.dev_y = (s.dp, s.fs + 1 - 2 * s.y)
        s.edge = (s.z == 0) | (s.z == 3)
        s.mid = (s.z == 1) | (s.z == 2)
    def dev_f(s, d):
        return (s.dp, lax.rem(s.fs + d, 8))
    def dev_at(s, z):
        return (s.dp, 2 * z + s.y)
    def up(s, d):
        return lax.rem(s.z + d, 4)
    def far(s):
        return jnp.where(s.edge, 3 - s.z, 6 - 3 * s.z)


def when(cond, f):
    if cond is None:
        f()
    else:
        pl.when(cond)(f)


class Move:
    def __init__(s, src, dst, ss, rs, dev, sends=None, takes=None):
        s.copy = pltpu.make_async_remote_copy(src_ref=src, dst_ref=dst, send_sem=ss, recv_sem=rs, device_id=dev, device_id_type=MESH)
        s.sends, s.takes = sends, takes
    def start(s):
        when(s.sends, s.copy.start)
    def sent(s):
        when(s.sends, s.copy.wait_send)
    def got(s):
        when(s.takes, s.copy.wait_recv)
    def wait(s):
        s.sent(); s.got()


def greet(p):
    bar = pltpu.get_barrier_semaphore()
    devs = [p.dev_c, p.dev_x] + [p.dev_f(d) for d in range(1, 8)]
    for d in devs:
        pl.semaphore_signal(bar, inc=1, device_id=d, device_id_type=MESH)
    return lambda: pl.semaphore_wait(bar, len(devs))


class Op:
    def __init__(s, start, finish, traffic, deps=(), cost=0.1, rank=0, after=0.0):
        s.start, s.finish, s.traffic, s.cost, s.rank, s.after = start, finish, traffic, cost, rank, after
        s.deps = [d for d in deps if d is not None]
        s.begun = s.ended = False
        s.ready = None


class Plan:
    RATE = dict(x=45e3, y=45e3, m=45e3, e=45e3, g=45e3, c=600e3)
    LATENCY = 2.2
    BACKLOG = 4
    SCALE = 1.1
    def __init__(s):
        s.ops, s.steps = [], []
        s.free = {k: 0.0 for k in s.RATE}
    def op(s, *a, **k):
        s.ops.append(Op(*a, **k))
        return s.ops[-1]
    def step(s, fn, cost, needs=(), opens=()):
        s.steps.append((fn, cost * s.SCALE, [n for n in needs if n is not None], list(opens)))
    def mark(s):
        m = Op(None, None, {}); m.begun = True
        return m
    def run(s):
        now, k, waiting, flying = 0.0, 0, list(s.ops), []
        def launch(force=False):
            nonlocal waiting
            rest = []
            for o in sorted(waiting, key=lambda o: o.rank):
                ok = all(d.ended for d in o.deps) and (force or o.after <= now)
                if ok and (force or all(s.free[r] - now < s.BACKLOG for r in o.traffic)):
                    force = False
                    o.start()
                    end = now
                    for r, v in o.traffic.items():
                        s.free[r] = max(s.free[r], now) + v / s.RATE[r]
                        end = max(end, s.free[r])
                    o.ready = end + s.LATENCY
                    flying.append(o)
                else:
                    rest.append(o)
            waiting = rest
        launch()
        while k < len(s.steps) or flying or waiting:
            flying.sort(key=lambda o: o.ready)
            can = k < len(s.steps) and all(n.ended for n in s.steps[k][2])
            if flying and (flying[0].ready <= now or not can):
                o = flying.pop(0)
                now = max(now, o.ready) + o.cost
                o.finish(); o.ended = True
            elif can:
                fn, cost, needs, opens = s.steps[k]; k += 1
                fn(); now += cost
                for m in opens: m.ended = True
            launch(not flying)
        return now


class Gather:
    PACE = 0
    def __init__(s, p, units, ssem, rsem, lead=3):
        s.p, s.units, s.ss, s.rs, s.lead = p, units, ssem, rsem, lead
        s.n = len(units)
    def move(s, u, i, block, dev, sends=None, takes=None):
        return Move(block, block, s.ss.at[u, i], s.rs.at[u, i], dev, sends, takes)
    def geo(s, u):
        w, kind, load = s.units[u]
        p, R = s.p, w.shape[2] // 2
        yfirst = kind in (1, 3)
        rc = pl.ds(pl.multiple_of(p.c * R, 16), R)
        wide = pl.ds(pl.multiple_of(p.x * 256, 256), 512) if kind < 2 else slice(None)
        mine = pl.ds(pl.multiple_of(p.x * 512, 256), 256)
        return w, yfirst, rc, wide, mine
    def near(s, u):
        w, yfirst, rc, wide, mine = s.geo(u); p = s.p
        ys = slice(None) if yfirst else p.y
        b = w.at[p.z, ys, rc, wide]
        return [s.move(u, 0, b, p.dev_at(p.up(1)), p.z < 3, p.z > 0), s.move(u, 1, b, p.dev_at(p.up(2))),
            s.move(u, 2, b, p.dev_at(p.up(3)), p.z > 0, p.z < 3)]
    def relay(s, u):
        w, yfirst, rc, wide, mine = s.geo(u); p = s.p
        ys = slice(None) if yfirst else p.y
        return [s.move(u, 3, w.at[p.far(), ys, rc, wide], p.dev_at(jnp.where(p.edge, p.z, 3 * p.z - 3)), p.mid, p.edge)]
    def over_y(s, u):
        w, yfirst, rc, wide, mine = s.geo(u); p = s.p
        if yfirst:
            return [s.move(u, 4, w.at[p.z, p.y, rc, wide], p.dev_y)]
        return [s.move(u, 4, w.at[:, p.y, rc, wide], p.dev_y, p.mid, p.mid),
            s.move(u, 4, w.at[pl.ds(p.z // 3, 3), p.y, rc, wide], p.dev_y, p.edge, p.edge)]
    def over_y_far(s, u):
        w, yfirst, rc, wide, mine = s.geo(u); p = s.p
        return [s.move(u, 5, w.at[p.far(), p.y, rc, wide], p.dev_y, p.edge, p.edge)]
    def over_x(s, u):
        w, yfirst, rc, wide, mine = s.geo(u); p = s.p
        return [s.move(u, 6, w.at[:, 1 - p.y, rc, mine], p.dev_x)]
    def over_x_own(s, u):
        w, yfirst, rc, wide, mine = s.geo(u); p = s.p
        return [s.move(u, 6 + d, w.at[p.up(d), p.y, rc, mine], p.dev_x) for d in (1, 2, 3)]
    def over_c(s, u):
        w, yfirst, rc, wide, mine = s.geo(u); p = s.p
        return [s.move(u, 10, w.at[:, 1 - p.y, rc, :], p.dev_c)] + [s.move(u, 10 + d, w.at[p.up(d), p.y, rc, :], p.dev_c) for d in (1, 2, 3)]
    def plan(s, P, gate=None):
        def moves(f):
            def start():
                for m in f(): m.start()
            def finish():
                for m in f(): m.wait()
            return start, finish
        firsts, lasts, pace, here = [], [], 0.0, []
        for u in range(s.n):
            w, kind, load = s.units[u]
            R, b = w.shape[2] // 2, 2 * 256
            piece = R * b * (2 if kind < 2 else 3)
            k = dict(rank=u)
            first = [gate, firsts[u - s.lead] if u >= s.lead else None]
            f = lambda g, u=u: moves(lambda: g(u))
            def own(op, u=u, load=load):
                begin, finish = f(op, u)
                def start():
                    if all(load is not v for v in here):
                        here.append(load); load.wait()
                    begin()
                return start, finish
            if kind in (1, 3):
                y = P.op(*own(s.over_y), dict(y=piece), first, after=pace, **k)
                near = P.op(*f(s.near), dict(m=6 * piece, e=4 * piece, g=4 * piece), [y], **k)
                got = [P.op(*f(s.relay), dict(g=2 * piece), [near], **k)]
                if kind == 1:
                    got = [P.op(*f(lambda u: s.over_x(u) + s.over_x_own(u)), dict(x=7 * R * b), got, **k)]
                firsts.append(y)
            else:
                near = P.op(*own(s.near), dict(m=3 * piece, e=2 * piece, g=2 * piece), first, after=pace, **k)
                rel = P.op(*f(s.relay), dict(g=piece), [near], **k)
                ya = P.op(*f(s.over_y), dict(y=3.5 * piece), [near], **k)
                yb = P.op(*f(s.over_y_far), dict(y=0.5 * piece), [rel], **k)
                got = [ya, yb]
                if kind == 0:
                    xo = P.op(*f(s.over_x_own), dict(x=3 * R * b), [rel], **k)
                    got = [P.op(*f(s.over_x), dict(x=4 * R * b), got, **k), xo]
                firsts.append(near)
            c = P.op(*f(s.over_c), dict(c=21 * R * b), got, **k)
            lasts.append(c)
            pace += s.PACE * R / 48
        return lasts


class Reduce:
    def __init__(s, p, units, bufs, ssem, rsem):
        s.p, s.units, s.b, s.ss, s.rs = p, units, bufs, ssem, rsem
        s.n = len(units)
        s.kz = dict(enumerate(("z0", "z1", "z2")))
    def geo(s, u):
        w, fin, out = s.units[u]
        R = w.shape[2] // 2; p = s.p
        rc = pl.ds(pl.multiple_of(p.c * R, 16), R)
        ro = pl.ds(pl.multiple_of((1 - p.c) * R, 16), R)
        xc = pl.ds(pl.multiple_of(p.x * 384, 128), 384)
        xo = pl.ds(pl.multiple_of((1 - p.x) * 384, 128), 384)
        return w, fin, out, R, rc, ro, xc, xo
    def kind(s, u):
        return KINDS[u % len(KINDS)]
    def before(s, u, kinds):
        return [v for v in range(u) if s.kind(v) in kinds]
    def slot(s, u):
        kind = s.kind(u)
        return kind, len(s.before(u, (kind,))) % (RING if kind == 2 else RING // 2), len(s.before(u, (0, 1))) % RING
    def move(s, u, i, src, dst, dev, sends=None, takes=None):
        k = u % s.ss.shape[0]
        return Move(src, dst, s.ss.at[k, i], s.rs.at[k, i], dev, sends, takes)
    def core(s, u):
        w, fin, out, R, rc, ro, xc, xo = s.geo(u)
        return [s.move(u, 0, w.at[:, :, ro, :], s.b["c"].at[u % CRING, :, :, pl.ds(0, R), :], s.p.dev_c)]
    def add_core(s, u):
        w, fin, out, R, rc, ro, xc, xo = s.geo(u); c = s.b["c"].at[u % CRING]
        def body(i, _):
            a, b = i // 2, lax.rem(i, 2)
            w[a, b, rc, :] = w[a, b, rc, :] + c[a, b, pl.ds(0, R), :]
            return 0
        lax.fori_loop(0, 8, body, 0)
    def first(s, u):
        w, fin, out, R, rc, ro, xc, xo = s.geo(u); p = s.p
        kind, k, k2 = s.slot(u)
        if kind == 2:
            return [s.move(u, 1, w.at[:, 1 - p.y, rc, :], s.b["h1y"].at[k, :, pl.ds(0, R), :], p.dev_y)]
        return [s.move(u, 1, w.at[:, :, rc, xo], s.b["h1x"].at[k2, :, :, pl.ds(0, R), :], p.dev_x)]
    def add_first(s, u):
        w, fin, out, R, rc, ro, xc, xo = s.geo(u); p = s.p
        kind, k, k2 = s.slot(u)
        if kind == 2:
            h = s.b["h1y"].at[k]
            def body(a, _):
                w[a, p.y, rc, :] = w[a, p.y, rc, :] + h[a, pl.ds(0, R), :]
                return 0
            lax.fori_loop(0, 4, body, 0)
        else:
            h = s.b["h1x"].at[k2]
            def body(i, _):
                a, b = i // 2, lax.rem(i, 2)
                w[a, b, rc, xc] = w[a, b, rc, xc] + h[a, b, pl.ds(0, R), :]
                return 0
            lax.fori_loop(0, 8, body, 0)
    def second_y(s, u):
        w, fin, out, R, rc, ro, xc, xo = s.geo(u); p = s.p
        kind, k, k2 = s.slot(u)
        return [s.move(u, 2, w.at[:, 1 - p.y, rc, xc], s.b["h2y"].at[k, :, pl.ds(0, R), :], p.dev_y)]
    def add_second_y(s, u):
        w, fin, out, R, rc, ro, xc, xo = s.geo(u); p = s.p
        kind, k, k2 = s.slot(u)
        h = s.b["h2y"].at[k]
        def body(a, _):
            w[a, p.y, rc, xc] = w[a, p.y, rc, xc] + h[a, pl.ds(0, R), :]
            return 0
        lax.fori_loop(0, 4, body, 0)
    def zblock(s, u, z):
        w, fin, out, R, rc, ro, xc, xo = s.geo(u); p = s.p
        kind, k, k2 = s.slot(u)
        if kind == 1:
            return w.at[z, :, rc, xc]
        return w.at[z, p.y, rc, xc if kind == 0 else slice(None)]
    def zslot(s, u, d):
        kind, k, k2 = s.slot(u); R = s.geo(u)[3]
        b = s.b[s.kz[kind]]
        return b.at[k, d, :, pl.ds(0, R), :] if kind == 1 else b.at[k, d, pl.ds(0, R), :]
    def near(s, u):
        p = s.p
        one = [s.move(u, 2 + d, s.zblock(u, p.up(d)), s.zslot(u, d - 1), p.dev_at(p.up(d)), *((p.z < 3, p.z > 0) if d == 1 else (p.z > 0, p.z < 3))) for d in (1, 3)]
        return [s.far(u)] + one + [s.two(u, p.edge, p.mid)]
    def far(s, u):
        p = s.p
        return s.move(u, 6, s.zblock(u, p.far()), s.zslot(u, 3), p.dev_at(1 + p.z // 3), p.edge, p.mid)
    def two(s, u, sends, takes):
        p = s.p
        return s.move(u, 4, s.zblock(u, p.up(2)), s.zslot(u, 1), p.dev_at(p.up(2)), sends, takes)
    def far_add(s, u):
        m = s.far(u); m.got(); m.sent()
        def add():
            b, h = s.zblock(u, s.p.far()), s.zslot(u, 3)
            b[...] = b[...] + h[...]
        pl.when(s.p.mid)(add)
    def z_sum(s, u):
        f = lambda r: r[...].astype(jnp.float32)
        v = f(s.zblock(u, s.p.z))
        for d in range(3): v = v + f(s.zslot(u, d))
        return v.astype(jnp.bfloat16)
    def last_y(s, u):
        w, fin, out, R, rc, ro, xc, xo = s.geo(u); p = s.p
        kind, k, k2 = s.slot(u)
        return [s.move(u, 7, w.at[p.z, 1 - p.y, rc, xc], s.b["h3y"].at[k, pl.ds(0, R), :], p.dev_y)]
    def last_x(s, u):
        w, fin, out, R, rc, ro, xc, xo = s.geo(u); p = s.p
        kind, k, k2 = s.slot(u)
        return [s.move(u, 7, w.at[p.z, p.y, rc, :], s.b["h3x"].at[k, pl.ds(0, R), :], p.dev_x)]
    def share_x(s, u):
        w, fin, out, R, rc, ro, xc, xo = s.geo(u)
        return [s.move(u, 8, fin.at[rc, xc], fin.at[rc, xc], s.p.dev_x)]
    def share_c(s, u):
        w, fin, out, R, rc, ro, xc, xo = s.geo(u)
        return [s.move(u, 9, fin.at[rc, :], fin.at[rc, :], s.p.dev_c)]
    def out_copy(s, u):
        return pltpu.make_async_copy(s.units[u][1], s.units[u][2], s.b["osem"].at[u])
    def plan(s, P, marks, hold, gate=None):
        def run(ms):
            for m in ms: m.start()
        def wait(ms):
            for m in ms: m.wait()
        core, first, second, zs, last, share, end = [], [], [], [], [], [], []
        def back(ops, u, kinds, ring):
            same = s.before(u, kinds)
            return ops[same[-ring // 2]] if len(same) >= ring // 2 else None
        for u in range(s.n):
            w, fin, out, R, rc, ro, xc, xo = s.geo(u); p = s.p
            kind, k, k2 = s.slot(u)
            full = R * 768 * 2
            zb = full if kind != 0 else full // 2
            mine = (kind,) if kind == 2 else (0, 1)
            def f_core(u=u): wait(s.core(u)); s.add_core(u)
            def f_first(u=u): wait(s.first(u)); s.add_first(u)
            def f_second(u=u): wait(s.second_y(u)); s.add_second_y(u)
            def b_near(u=u): run(s.near(u)[1:])
            def f_near(u=u): wait(s.near(u)[1:])
            def b_rel(u=u): s.two(u, s.p.mid, s.p.edge).start()
            def f_z(u=u, w=w, fin=fin, kind=kind, rc=rc, xc=xc):
                s.two(u, s.p.mid, s.p.edge).wait()
                if kind == 0:
                    fin[rc, xc] = s.z_sum(u)
                else:
                    b = s.zblock(u, s.p.z); b[...] = s.z_sum(u)
            def f_last(u=u, w=w, fin=fin, kind=kind, rc=rc, xc=xc, R=R, k=k):
                p = s.p
                if kind == 1:
                    wait(s.last_y(u))
                    fin[rc, xc] = w[p.z, p.y, rc, xc] + s.b["h3y"][k, pl.ds(0, R), :]
                else:
                    wait(s.last_x(u))
                    fin[rc, :] = w[p.z, p.y, rc, :] + s.b["h3x"][k, pl.ds(0, R), :]
            def f_end(u=u): wait(s.share_c(u)); s.out_copy(u).start()
            c = P.op(lambda u=u: run(s.core(u)), f_core, dict(c=8 * full), [marks[u], gate, core[u - CRING // 2] if u >= CRING // 2 else None] + [end[v] for v in hold[u]], cost=0.3, rank=100 + u)
            core.append(c)
            f = P.op(lambda u=u: run(s.first(u)), f_first, dict(y=4 * full) if kind == 2 else dict(x=4 * full), [c, back(first, u, mine, RING)], cost=0.25, rank=100 + u)
            first.append(f)
            prev = f
            if kind == 0:
                prev = P.op(lambda u=u: run(s.second_y(u)), f_second, dict(y=2 * full), [f, back(second, u, (0,), RING // 2)], cost=0.15, rank=100 + u)
            second.append(prev)
            ring = back(zs, u, (kind,), RING if kind == 2 else RING // 2)
            far = P.op(lambda u=u: s.far(u).start(), lambda u=u: s.far_add(u), dict(e=zb), [prev, ring], rank=100 + u)
            near = P.op(b_near, f_near, dict(m=2 * zb, e=2 * zb, g=zb), [prev, ring], rank=100 + u)
            z = P.op(b_rel, f_z, dict(m=zb, g=zb), [far, near], cost=0.15, rank=100 + u)
            zs.append(z)
            prev = z
            if kind != 0:
                prev = P.op((lambda u=u: run(s.last_y(u))) if kind == 1 else (lambda u=u: run(s.last_x(u))), f_last,
                    dict(y=full // 2) if kind == 1 else dict(x=full), [z, back(last, u, (kind,), RING if kind == 2 else RING // 2)], rank=100 + u)
            last.append(prev)
            if kind != 2:
                prev = P.op(lambda u=u: run(s.share_x(u)), lambda u=u: wait(s.share_x(u)), dict(x=full // 2), [prev, back(share, u, (0, 1), RING)], rank=100 + u)
            share.append(prev)
            end.append(P.op(lambda u=u: run(s.share_c(u)), f_end, dict(c=full), [prev, back(end, u, (kind,), RING if kind == 2 else RING // 2)], rank=100 + u))
        return end
    def finish(s):
        for u in range(s.n): s.out_copy(u).wait()
    def clear(s):
        def zero(d):
            def f():
                for q in s.kz.values():
                    b = s.b[q]
                    for k in range(b.shape[0]):
                        b[k, d] = jnp.zeros(b.shape[2:], b.dtype)
            return f
        pl.when(s.p.z == 0)(zero(0))
        pl.when(s.p.z == 3)(zero(2))


CRING, RING = 4, 4
KINDS = (2, 0, 2, 2, 2, 1, 1, 0, 2, 0, 2, 1, 2, 0, 2, 1, 2, 0, 2, 1, 2, 0, 2, 1, 2, 0, 2, 1, 1, 2, 0, 2, 2, 2, 2, 0, 1, 2, 2, 1)


def reduce_scratch(n, R):
    b = jnp.bfloat16; V = pltpu.VMEM; lag = RING
    half = lag // 2
    return dict(c=V((CRING, 4, 2, R, 768), b), h1x=V((lag, 4, 2, R, 384), b), h1y=V((lag, 4, R, 768), b),
        h2y=V((half, 4, R, 384), b), z0=V((half, 4, R, 384), b), z1=V((half, 4, 2, R, 384), b), z2=V((lag, 4, R, 768), b),
        h3y=V((half, R, 384), b), h3x=V((lag, R, 768), b), osem=pltpu.SemaphoreType.DMA((n,)))
NA, ND = 8, 3
ROUTES = ((0, 0, 0, 0, 0, 0, 0, 0, 0, 0, 0),
    (0, 1, 0, 0, 0, 0, 0, 2, 1, 2, 3))
def gather_units(wa, wd, layer):
    return [(wa.at[layer, k] if k < NA else wd.at[layer, k - NA], ROUTES[layer][k]) for k in range(NA + ND)]

def load_shards(p, attn_in, attn_out, fc_in, fc_out, wa, wd, sem):
    out = []
    i = 0
    for l in range(2):
        for k in range(NA):
            if k < 3: src = attn_in.at[l, :, pl.ds(768 * k, 768)]
            elif k == 3: src = attn_out.at[l]
            else: src = fc_in.at[l, :, pl.ds(768 * (k - 4), 768)]
            out.append(pltpu.make_async_copy(src, wa.at[l, k, p.z, p.y], sem.at[i])); i += 1
        for k in range(ND):
            out.append(pltpu.make_async_copy(fc_out.at[l, pl.ds(128 * k, 128)], wd.at[l, k, p.z, p.y], sem.at[i])); i += 1
    return out
ORDER = {1: [("D", 0), ("D", 1), ("A", 4), ("A", 5), ("D", 2), ("A", 6), ("A", 7), ("A", 3), ("A", 0), ("A", 1), ("A", 2)],
    0: [("D", 0), ("D", 1), ("D", 2), ("A", 4), ("A", 5), ("A", 6), ("A", 7), ("A", 3), ("A", 0), ("A", 1), ("A", 2)]}


F32, BF = jnp.float32, jnp.bfloat16
NN = (((1,), (0,)), ((), ()))
NT = (((1,), (1,)), ((), ()))
TN = (((0,), (0,)), ((), ()))
def mm(a, b, dims=NN):
    return lax.dot_general(a, b, dims, preferred_element_type=F32)

ROWS, WIDTH, PAIRS = 512, 768, 6
def r_gain(l, i): return 2 * l + i
def r_bias(l, i): return 4 + 6 * l + i
R_EMBED = 16
def r_fcb(l, k): return 24 + 4 * l + k

def row(ref, r):
    return ref[pl.ds(r, 1), :]

def rows_loop(step, body):
    def run(i, c):
        body(pl.ds(pl.multiple_of(i * step, step), step))
        return c
    lax.fori_loop(0, ROWS // step, run, 0)

def gelu_parts(z):
    a = jnp.abs(z)
    t = 1.0 / (1.0 + (0.3275911 * 0.7071067811865476) * a)
    e = jnp.exp(-0.5 * (z * z))
    poly = t * (0.254829592 + t * (-0.284496736 + t * (1.421413741 + t * (-1.453152027 + t * 1.061405429))))
    tail = 0.5 * poly * e
    cdf = jnp.where(z < 0, tail, 1.0 - tail)
    return z * cdf, cdf + z * (0.3989422804014327 * e)

class Net:
    def __init__(s, r):
        s.__dict__.update(r)
    def w(s, l, k):
        return s.wa.at[l, k]
    def wtile(s, l, k, cols):
        v = s.wa[l, k, :, :, :, cols]
        return v.reshape(WIDTH, v.shape[-1])
    def norm(s, l, i, xh, h):
        at = pl.ds(2 * l + i, 1)
        def body(q):
            v = s.x[q, :]
            c = v - jnp.mean(v, axis=-1, keepdims=True)
            r = lax.rsqrt(jnp.mean(c * c, axis=-1, keepdims=True) + 1e-6)
            n = c * r
            xh[q, :] = n.astype(BF)
            s.rs[q, at] = r
            h[q, :] = (n * row(s.V, r_gain(l, i)) + row(s.V, r_bias(l, 4 if i else 0))).astype(BF)
        for b in range(2): body(pl.ds(256 * b, 256))
    def norm_back(s, l, i, d, xh, out):
        at = pl.ds(2 * l + i, 1)
        total = lambda v: jnp.sum(v, axis=0, keepdims=True)
        sg = sb = so = 0.0
        for b in range(2):
            q = pl.ds(256 * b, 256)
            dv, n = d[q, :], xh[q, :].astype(F32)
            dn = dv * row(s.V, r_gain(l, i))
            m1 = jnp.mean(dn, axis=-1, keepdims=True)
            m2 = jnp.mean(dn * n, axis=-1, keepdims=True)
            e = s.x[q, :] + s.rs[q, at] * (dn - m1 - n * m2)
            s.x[q, :] = e
            sg, sb = sg + total(dv * n), sb + total(dv)
            if out is not None:
                eb = e.astype(BF)
                out[q, :] = eb
                so = so + total(eb.astype(F32))
        s.S[pl.ds(r_gain(l, i), 1), :] = sg
        s.S[pl.ds(r_bias(l, 4 if i else 0), 1), :] = sb
        return so
    def unit(s, l, k):
        return s.wa[l, k].reshape(WIDTH, WIDTH)
    def project(s, l, k):
        v = mm(s.h[...], s.unit(l, k))
        if k != 1:
            v = v + row(s.V, r_bias(l, 1 if k == 0 else 2))
        s.t[k] = v.astype(BF)
    def masks(s):
        lane = lax.broadcasted_iota(jnp.int32, (1, 128), 1)
        return [(lane < 64).astype(F32).astype(BF), (lane >= 64).astype(F32).astype(BF)]
    def attend(s, l, p0, p1):
        ms = s.masks()
        def body(p, c):
            n = pl.ds(pl.multiple_of(p * 128, 128), 128)
            kk = s.t[1, :, n]
            vt = s.t[2, :, n].T
            qs = s.t[0, :, n] * 0.125
            outs = []
            for i in range(2):
                st = mm(kk, qs * ms[i], NT)
                top = jnp.max(st, axis=0, keepdims=True)
                e = jnp.exp(st - top)
                total = jnp.sum(e, axis=0, keepdims=True)
                s.lse[l, pl.ds(2 * p + i, 1), :] = top + jnp.log(total)
                outs.append(mm(vt[64 * i:64 * i + 64], e.astype(BF)) * (1.0 / total))
            s.o[:, n] = jnp.concatenate(outs, axis=0).T.astype(BF)
            return c
        lax.fori_loop(p0, p1, body, 0)
    def attend_back(s, l, p0, p1):
        ms = s.masks()
        def body(p, c):
            n = pl.ds(pl.multiple_of(p * 128, 128), 128)
            kk, vv = s.t[1, :, n], s.t[2, :, n]
            kt = kk.T
            qs = s.t[0, :, n] * 0.125
            do = s.o[:, n]
            qt, dt = qs.T, do.T
            dv, dk, dq = [], [], []
            for i in range(2):
                at = slice(64 * i, 64 * i + 64)
                pt = jnp.exp(mm(kk, qs * ms[i], NT) - s.lse[l, pl.ds(2 * p + i, 1), :])
                pd = pt * mm(vv, do * ms[i], NT)
                dv.append(mm(dt[at], pt.astype(BF), NT))
                ds = (pd - pt * jnp.sum(pd, axis=0, keepdims=True)).astype(BF)
                dk.append(mm(qt[at], ds, NT))
                dq.append(mm(kt[at], ds) * 0.125)
            for j, d in enumerate((dq, dk, dv)):
                s.t[j, :, n] = jnp.concatenate(d, axis=0).T.astype(BF)
            return c
        lax.fori_loop(p0, p1, body, 0)
    def attn_out(s, l):
        s.x[...] = s.x[...] + (mm(s.o[...], s.unit(l, 3)) + row(s.V, r_bias(l, 3)))
    def mlp_in(s, l, k):
        s.acc[...] = mm(s.h2[...], s.unit(l, 4 + k)) + row(s.V, r_fcb(l, k))
        for f in range(2):
            for j in range(3):
                a, d = gelu_parts(s.acc[:, pl.ds(384 * f + 128 * j, 128)])
                s.g[j, :, pl.ds((2 * k + f) * 128, 128)] = a.astype(BF)
                s.gp[j, :, pl.ds((2 * k + f) * 128, 128)] = d.astype(BF)
    def mlp_out(s, l, j):
        v = mm(s.g[j], s.wd[l, j].reshape(1024, WIDTH))
        if j == 0:
            v = v + row(s.V, r_bias(l, 5))
        s.x[...] = s.x[...] + v
    def start_back(s, l, make):
        if make:
            s.du[...] = s.x[...].astype(BF)
        s.col_sum(s.du, r_bias(l, 5))
    def mlp_out_back(s, l, j):
        def body(i, c):
            n = pl.ds(pl.multiple_of(i * 512, 512), 512)
            w = s.wd[l, j, pl.ds(2 * i, 2)].reshape(512, WIDTH)
            dz = (mm(s.du[...], w, NT) * s.gp[j, :, n].astype(F32)).astype(BF)
            s.gp[j, :, n] = dz
            s.bz[pl.ds(3 * l + j, 1), n] = jnp.sum(dz.astype(F32), axis=0, keepdims=True)
            return c
        lax.fori_loop(0, 2, body, 0)
    def mlp_out_grad(s, l, j, to):
        for i in range(2):
            to[pl.ds(2 * i, 2)] = mm(s.g[j, :, pl.ds(512 * i, 512)], s.du[...], TN).astype(BF).reshape(2, 2, 128, WIDTH)
    def hidden_bias(s):
        for l in range(2):
            for j in range(3):
                for f in range(8):
                    s.S[pl.ds(r_fcb(l, f // 2), 1), pl.ds(384 * (f % 2) + 128 * j, 128)] = s.bz[pl.ds(3 * l + j, 1), pl.ds(128 * f, 128)]
    def dz_tile(s, k, q):
        parts = []
        for f in range(2):
            for j in range(3):
                parts.append(s.gp[j, q, pl.ds((2 * k + f) * 128, 128)])
        return jnp.concatenate(parts, axis=1)
    def back_mm(s, l, k, get, first):
        v = mm(get(slice(None)), s.unit(l, k), NT)
        s.acc[...] = v if first else s.acc[...] + v
    def grad_a(s, to, get, lhs):
        to[...] = mm(lhs[...], get(slice(None)), TN).astype(BF).reshape(4, 2, 96, WIDTH)
    def attn_out_back(s, l):
        do = mm(s.du[...], s.unit(l, 3), NT).astype(BF)
        s.grad_a(s.w(l, 3), lambda q: s.du[q, :], s.o)
        s.o[...] = do
    def col_sum(s, ref, r):
        s.S[pl.ds(r, 1), :] = jnp.sum(ref[...].astype(F32), axis=0, keepdims=True)

def net_scratch():
    V = pltpu.VMEM
    return dict(x=V((512, 768), F32), acc=V((512, 768), F32), h=V((512, 768), BF), t=V((3, 512, 768), BF), lse=V((2, 16, 512), F32),
        o=V((512, 768), BF), h2=V((512, 768), BF), g=V((3, 512, 1024), BF), gp=V((3, 512, 1024), BF), xh1=V((512, 768), BF), xh2=V((512, 768), BF),
        rs=V((512, 128), F32), du=V((512, 768), BF),
        bz=V((8, 1024), F32), V=V((32, 768), F32), S=V((32, 768), F32))
SPILL = ["h", "t", "o", "h2", "g", "gp", "xh1", "xh2"]


SMALL = (32, 768)
VMEM_LIMIT = 63 * 1024 * 1024
EARLY = {21: 32, 0: 32, 2: 32}
LEAD = 30
CUTS = {(0, 'A', 2): [64, 32], (1, 'A', 0): [32, 64], (0, 'A', 3): [64, 32], (0, 'A', 6): [32, 64], (0, 'A', 0): [64, 32]}
SOON = 2
DCUT = [64, 64]
SEG, SEGB = 3, 2


def gather_list(wa, wd, loads):
    units, first = [], []
    for l in range(2):
        for w, kind in gather_units(wa, wd, l):
            h = EARLY.get(len(first), w.shape[2])
            units += [(w.at[:, :, pl.ds(a, h), :], kind, loads[len(first)]) for a in range(0, w.shape[2], h)]
            first.append(len(units) - 1)
    return units, first


def reduce_list():
    out = []
    for l in (1, 0):
        for k, q in ORDER[l]:
            H = 128 if k == "D" else 96
            hs = CUTS.get((l, k, q), DCUT if k == "D" else [H])
            a = 0
            for h in hs:
                out.append((l, k, q, a, h)); a += h
    return out


def steps(P, n, unit, marks, sent, do):
    P.step(do.embed, 1.5, [do.params])
    for l in range(2):
        P.step(lambda l=l: (do.reuse(l, "xh1", "h"), n.norm(l, 0, n.xh1, n.h), do.keep(l, "xh1")), 0.5)
        for k in range(3):
            P.step(lambda l=l, k=k: (do.reuse(l, *(["t"] if k == 0 else [])), n.project(l, k)), 1.0, [unit(l, k)])
        for a in range(0, 6, SEG):
            P.step(lambda l=l, a=a: (do.keep(l, *(["h", "t"] if a == 0 else [])), do.reuse(l, *(["o"] if a == 0 else [])), n.attend(l, a, a + SEG)), 1.25 * SEG)
        P.step(lambda l=l: (do.keep(l, "o"), n.attn_out(l)), 1.0, [unit(l, 3)])
        P.step(lambda l=l: (do.reuse(l, "xh2", "h2"), n.norm(l, 1, n.xh2, n.h2), do.keep(l, "xh2")), 0.5)
        for k in range(4):
            P.step(lambda l=l, k=k: (do.reuse(l, *(["g", "gp"] if k == 0 else [])), n.mlp_in(l, k)), 1.4, [unit(l, 4 + k)])
        if l == 1:
            P.step(lambda: n.start_back(1, False), 0.2)
            for j in range(SOON):
                P.step(lambda j=j: n.mlp_out_grad(1, j, n.wg.at[j]), 1.1, (), marks(1, "D", j))
        for j in range(3):
            if l == 1:
                P.step(lambda j=j: n.mlp_out_back(1, j), 1.4, [unit(1, 8 + j)])
            if l == 0 or j < 2:
                P.step(lambda l=l, j=j: (do.keep(l, *(["h2", "gp"] if j == 0 else [])), n.mlp_out(l, j)), 1.2, [unit(l, 8 + j)])
        P.step(lambda l=l: do.keep(l, "g"), 0.0)
    for l in (1, 0):
        if l == 0:
            P.step(lambda: n.start_back(0, True), 0.3)
        for j in range(3):
            if l == 0:
                P.step(lambda j=j: (do.need(0, *(["gp", "g"] if j == 0 else [])), n.mlp_out_back(0, j), n.mlp_out_grad(0, j, n.wd.at[0, j])), 2.4, (), marks(0, "D", j))
        if l == 0:
            P.step(lambda: do.need(0, "h2"), 0.0)
        for k in range(4):
            get = lambda q, k=k: n.dz_tile(k, q)
            P.step(lambda l=l, k=k, get=get: (n.back_mm(l, 4 + k, get, k == 0), n.grad_a(n.w(l, 4 + k), get, n.h2)), 1.6, (), marks(l, "A", 4 + k))
            if l == 1 and k == 1:
                P.step(lambda: (n.mlp_out(1, 2), do.send()), 1.2)
                P.step(lambda: (n.mlp_out_grad(1, 2, n.wd.at[1, 2]), do.done(1, "g")), 1.1, (), marks(1, "D", 2))
        if l == 1:
            P.step(do.turn, 0.8)
        P.step(lambda l=l: (do.done(l, "gp", "h2"), do.need(l, "xh2"), do.mid_norm(l), do.done(l, "xh2"), do.need(l, "o")), 1.0)
        P.step(lambda l=l: n.attn_out_back(l), 1.6, (), marks(l, "A", 3))
        P.step(lambda l=l: do.need(l, "t"), 0.0)
        for a in range(0, 6, SEGB):
            P.step(lambda l=l, a=a: n.attend_back(l, a, a + SEGB), 1.85 * SEGB)
        P.step(lambda l=l: (do.done(l, "o"), do.need(l, "h"), n.col_sum(n.t.at[0], r_bias(l, 1)), n.col_sum(n.t.at[2], r_bias(l, 2))), 0.3)
        for k in range(3):
            get = lambda q, k=k: n.t[k, q, :]
            if l == 1:
                P.step(lambda l=l, k=k, get=get: (n.back_mm(l, k, get, k == 0), n.grad_a(n.w(l, k), get, n.h)), 1.6, (), marks(l, "A", k))
            else:
                P.step(lambda k=k, get=get: n.grad_a(n.w(1, 4 + k), get, n.h), 1.0, sent(1, "A", 4 + k), marks(0, "A", k))
        for k in range(3 if l == 0 else 0):
            P.step(lambda k=k: n.back_mm(0, k, lambda q: n.t[k, q, :], k == 0), 1.0)
        P.step(lambda l=l: (do.done(l, "t", "h"), do.need(l, "xh1"), n.norm_back(l, 0, n.acc, n.xh1, None), do.done(l, "xh1")), 1.0)
    P.step(do.last, 1.0, (), [do.sums])


class Smalls:
    def __init__(s, p, net, b):
        s.p, s.net, s.b = p, net, b
    def pack(s, gains, biases, embed, fcb):
        k = s.b["own"]
        k[...] = jnp.zeros((32, 128), F32)
        for l in range(2):
            k[2 * l:2 * l + 2, 0:96] = gains[l].astype(F32)
            for i in range(6):
                k[4 + 6 * l + i:5 + 6 * l + i, 0:96] = biases[i, l:l + 1, :].astype(F32)
            for i in range(3):
                k[24 + 3 * l + i:25 + 3 * l + i, :] = fcb[l:l + 1, 128 * i:128 * i + 128].astype(F32)
        k[16:17, 0:96] = embed[...].astype(F32)
        s.b["sm"][s.p.fs] = k[...].astype(BF)
    def fetch(s, d):
        b, p = s.b, s.p
        return remote(b["sm"].at[p.fs], b["sm"].at[p.fs], b["ss"].at[d - 1], b["rs"].at[d - 1], p.dev_f(d))
    def start(s):
        for d in range(1, 8):
            s.fetch(d).start()
    def build(s):
        for d in range(1, 8):
            s.fetch(d).wait()
        V = s.net.V
        i = lax.broadcasted_iota(jnp.int32, (128, 768), 0)
        c = lax.broadcasted_iota(jnp.int32, (128, 768), 1)
        total = jnp.zeros((24, 768), F32)
        for f in range(8):
            blk = s.b["sm"][f]
            pick = jnp.where((c - 96 * f == i) & (i < 96), 1.0, 0.0).astype(BF)
            total = total + mm(blk, pick)[0:24]
        V[0:24, :] = total
        for f in range(8):
            blk = s.b["sm"][f].astype(F32)
            for l in range(2):
                for j in range(3):
                    at = 384 * (f % 2) + 128 * j
                    V[r_fcb(l, f // 2):r_fcb(l, f // 2) + 1, at:at + 128] = blk[24 + 3 * l + j:25 + 3 * l + j]
    def hop(s, h):
        b, p, S = s.b, s.p, s.net.S
        if h < 3:
            return [remote(S, b["sr"].at[h], b["ss"].at[7 + h], b["rs"].at[7 + h], (p.dev_c, p.dev_x, p.dev_y)[h])]
        return [remote(S, b["sr"].at[2 + d], b["ss"].at[9 + d], b["rs"].at[9 + d], p.dev_at(p.up(d))) for d in (1, 2, 3)]
    def send(s, h):
        for q in s.hop(h): q.start()
    def add(s, h):
        for q in s.hop(h): q.wait()
        t = s.net.S[...]
        for i in ([h] if h < 3 else [3, 4, 5]):
            t = t + s.b["sr"][i]
        s.net.S[...] = t
    def plan(s, P, begin):
        prev = begin
        for h, r in enumerate("cxym"):
            prev = P.op(lambda h=h: s.send(h), lambda h=h: s.add(h), {r: 98304 * (4 if r == "m" else 1)}, [prev], rank=-1)
        return prev
    def own(s):
        k, S, f = s.b["own"], s.net.S, s.p.fs
        k[...] = jnp.zeros((32, 128), F32)
        v = jnp.zeros((24, 96), F32)
        for i in range(8):
            v = jnp.where(f == i, S[0:24, 96 * i:96 * i + 96], v)
        k[0:24, 0:96] = v
        for l in range(2):
            w = jnp.zeros((1, 384), F32)
            for i in range(8):
                w = jnp.where(f == i, S[r_fcb(l, i // 2):r_fcb(l, i // 2) + 1, 384 * (i % 2):384 * (i % 2) + 384], w)
            for j in range(3):
                k[24 + 3 * l + j:25 + 3 * l + j, :] = w[:, 128 * j:128 * j + 128]


def remote(src, dst, ss, rs, dev):
    return pltpu.make_async_remote_copy(src_ref=src, dst_ref=dst, send_sem=ss, recv_sem=rs, device_id=dev, device_id_type=MESH)


def smalls_scratch():
    return dict(sm=pltpu.VMEM((8, 32, 128), BF), own=pltpu.VMEM((32, 128), F32), sr=pltpu.VMEM((6, 32, 768), F32),
        ss=pltpu.SemaphoreType.DMA((13,)), rs=pltpu.SemaphoreType.DMA((13,)))


class Work:
    pass


def whole_kernel(tok, cot, msk, gains, biases, embed, fcb, ai, ao, fi, fo, act, ig, so, o_ai, o_ao, o_fi, o_fo, *rest):
    spill = dict(zip(SPILL, rest[:8]))
    sc, wa, wd, wg, fa, fd, rbufs, sbufs, lsem, ssem, iosem, gss, grs, rss, rrs = rest[8:]
    p = Pos()
    met = greet(p)
    n = Net(dict(sc, wa=wa, wd=wd, wg=wg))
    sm = Smalls(p, n, sbufs)
    tok_in = pltpu.make_async_copy(tok, n.o, iosem.at[0])
    cot_in = pltpu.make_async_copy(cot, n.du, iosem.at[1])
    loads = load_shards(p, ai, ao, fi, fo, wa, wd, lsem)
    for c in loads: c.start()
    tok_in.start(); cot_in.start()
    red = []
    for l, k, q, a, h in reduce_list():
        if (l, k) == (0, "A") and q < 3: w = wa.at[1, 4 + q]
        elif (l, k) == (1, "D") and q < SOON: w = wg.at[q]
        else: w = (wd if k == "D" else wa).at[l, q]
        b = q if k == "A" else 8 + q
        if l == 1: f = (fd if k == "D" else fa).at[q, pl.ds(a, h)]
        else: f = wg.at[b // 8, b % 8 // 2, b % 2, pl.ds(a, h)]
        if k == "D": o = o_fo.at[l, pl.ds(128 * q + a, h)]
        elif q == 3: o = o_ao.at[l, pl.ds(a, h)]
        elif q < 3: o = o_ai.at[l, pl.ds(a, h), pl.ds(768 * q, 768)]
        else: o = o_fi.at[l, pl.ds(a, h), pl.ds(768 * (q - 4), 768)]
        red.append((w.at[:, :, pl.ds(a, h), :], f, o))
    r = Reduce(p, red, rbufs, rss, rrs)
    r.clear()
    sm.pack(gains, biases, embed, fcb)
    mt = msk[...].astype(F32).T
    for j in range(4):
        n.rs[128 * j:128 * j + 128, 4:5] = mt[:, j:j + 1]
    met()
    units, part = gather_list(wa, wd, loads)
    g = Gather(p, units, gss, grs, LEAD)
    P = Plan()
    out_of = lambda nm: pltpu.make_async_copy(sc[nm], spill[nm], ssem.at[SPILL.index(nm)])
    back_to = lambda nm: pltpu.make_async_copy(spill[nm], sc[nm], ssem.at[SPILL.index(nm)])
    act_out = pltpu.make_async_copy(n.x, act, iosem.at[0])
    ig_out = pltpu.make_async_copy(n.acc, ig, iosem.at[1])

    class Do(Work):
        params = P.op(sm.start, sm.build, dict(y=40e3), (), cost=1.0, rank=-1)
        sums = P.mark()
        @staticmethod
        def reuse(l, *nms):
            for m in nms if l == 1 else (): out_of(m).wait()
        @staticmethod
        def keep(l, *nms):
            for m in nms if l == 0 else (): out_of(m).start()
        @staticmethod
        def need(l, *nms):
            for m in nms if l == 0 else (): back_to(m).wait()
        @staticmethod
        def done(l, *nms):
            for m in nms if l == 1 else (): back_to(m).start()
        @staticmethod
        def embed():
            tok_in.wait(); cot_in.wait()
            n.S[...] = jnp.zeros(SMALL, F32)
            def body(q):
                m = n.rs[q, 4:5]
                n.x[q, :] = n.o[q, :].astype(F32) * (1.0 - m) + m * row(n.V, R_EMBED)
            rows_loop(64, body)
        @staticmethod
        def send():
            act_out.start()
        @staticmethod
        def turn():
            act_out.wait()
            n.x[...] = n.du[...].astype(F32)
        @staticmethod
        def mid_norm(l):
            n.S[pl.ds(r_bias(l, 3), 1), :] = n.norm_back(l, 1, n.acc, n.xh2, n.du)
        @staticmethod
        def last():
            n.hidden_bias()
            def body(j, c):
                q = pl.ds(pl.multiple_of(j * 64, 64), 64)
                m, e = n.rs[q, 4:5], n.x[q, :]
                n.acc[q, :] = e * (1.0 - m)
                return c + jnp.sum(e * m, axis=0, keepdims=True)
            n.S[pl.ds(R_EMBED, 1), :] = lax.fori_loop(0, ROWS // 64, body, jnp.zeros((1, WIDTH), F32))
            ig_out.start()

    make_plan(P, n, g, part, r, sm, Do)
    P.run()
    sm.own()
    s_out = pltpu.make_async_copy(sbufs["own"], so, iosem.at[2])
    s_out.start()
    r.finish()
    ig_out.wait()
    s_out.wait()


def make_plan(P, n, g, part, r, sm, do):
    lasts = g.plan(P)
    marks = {}
    order = []
    for l, k, q, a, h in reduce_list():
        m = P.mark()
        marks.setdefault((l, k, q), []).append(m)
        order.append(m)
    lst = reduce_list()
    early = [u for u, v in enumerate(lst) if v[:2] == (1, "D") and v[2] < SOON]
    ends = r.plan(P, order, [early if v[0] == 0 else () for v in lst])
    gone = {}
    for (l, k, q, a, h), e in zip(reduce_list(), ends):
        gone.setdefault((l, k, q), []).append(e)
    sm.plan(P, do.sums)
    steps(P, n, lambda l, k: lasts[part[11 * l + k]], lambda l, k, q: marks[(l, k, q)], lambda l, k, q: gone[(l, k, q)], do)


def whole(tok, cot, msk, gains, biases, embed, fcb, ai, ao, fi, fo):
    net = net_scratch()
    any_, vm = pl.BlockSpec(memory_space=pl.ANY), pl.BlockSpec(memory_space=pltpu.VMEM)
    sa, sd = (2, 8, 4, 2, 96, 768), (2, 3, 4, 2, 128, 768)
    fa, fd = (8, 96, 768), (3, 128, 768)
    shapes = [((512, 768), F32), ((512, 768), F32), ((32, 128), F32), (ai.shape, BF), (ao.shape, BF), (fi.shape, BF), (fo.shape, BF)]
    shapes += [(net[k].shape, net[k].dtype) for k in SPILL]
    dma = pltpu.SemaphoreType.DMA
    parts, red = 22 + sum((96 if u % 11 < 8 else 128) // h - 1 for u, h in EARLY.items()), reduce_list()
    R = max(v[4] for v in red) // 2
    return pl.pallas_call(
        whole_kernel,
        out_shape=[jax.ShapeDtypeStruct(*v) for v in shapes],
        in_specs=[any_, any_, vm, vm, vm, vm, vm] + [any_] * 4,
        out_specs=[any_] * len(shapes),
        scratch_shapes=[
            net, pltpu.VMEM(sa, BF), pltpu.VMEM(sd, BF), pltpu.VMEM((SOON,) + sd[2:], BF), pltpu.VMEM(fa, BF), pltpu.VMEM(fd, BF),
            reduce_scratch(len(red), R), smalls_scratch(), dma((22,)), dma((8,)), dma((3,)),
            dma((parts, 14)), dma((parts, 14)), dma((len(red), 10)), dma((len(red), 10)),
        ],
        compiler_params=pltpu.CompilerParams(collective_id=0, has_side_effects=True, vmem_limit_bytes=VMEM_LIMIT),
    )(tok, cot, msk, gains, biases, embed, fcb, ai, ao, fi, fo)[:7]


def results_kernel(act_i, ig_i, own, g0, g1, g2, g3, act, ig, embed, o0, o1, o2, o3, gains, biases, fcb, narrow, full, rows, isem, osem):
    grads, outs = (g0, g1, g2, g3), (o0, o1, o2, o3)
    loads = [pltpu.make_async_copy(g, b, isem.at[i]) for i, (g, b) in enumerate(zip(grads, narrow))]
    stores = [pltpu.make_async_copy(b, o, osem.at[i]) for i, (b, o) in enumerate(zip(full, outs))]
    loads += [pltpu.make_async_copy(v, rows.at[i], isem.at[4 + i]) for i, v in enumerate((act_i, ig_i))]
    stores += [pltpu.make_async_copy(rows.at[i], v, osem.at[4 + i]) for i, v in enumerate((act, ig))]
    for c in loads:
        c.start()
    for l in range(2):
        gains[l] = own[2 * l:2 * l + 2, 0:96]
        for i in range(6):
            biases[i, l:l + 1, :] = own[4 + 6 * l + i:5 + 6 * l + i, 0:96]
        for i in range(3):
            fcb[l:l + 1, 128 * i:128 * i + 128] = own[24 + 3 * l + i:25 + 3 * l + i, :]
    embed[...] = own[16:17, 0:96]
    for i in (0, 4, 2, 5, 3, 1):
        loads[i].wait()
        if i < 4:
            full[i][...] = narrow[i][...].astype(F32)
        stores[i].start()
    for c in stores:
        c.wait()


def results(act, ig, own, *grads):
    any_, vm = pl.BlockSpec(memory_space=pl.ANY), pl.BlockSpec(memory_space=pltpu.VMEM)
    f = lambda *s: jax.ShapeDtypeStruct(s, F32)
    return pl.pallas_call(
        results_kernel,
        out_shape=[f(*act.shape), f(*ig.shape), f(1, 96)] + [f(*g.shape) for g in grads] + [f(2, 2, 96), f(6, 2, 96), f(2, 384)],
        in_specs=[any_, any_, vm] + [any_] * 4,
        out_specs=[any_, any_, vm] + [any_] * 4 + [vm] * 3,
        scratch_shapes=[
            [pltpu.VMEM(g.shape, BF) for g in grads], [pltpu.VMEM(g.shape, F32) for g in grads],
            pltpu.VMEM((2,) + act.shape, F32), pltpu.SemaphoreType.DMA((6,)), pltpu.SemaphoreType.DMA((6,)),
        ],
        compiler_params=pltpu.CompilerParams(vmem_limit_bytes=VMEM_LIMIT),
    )(act, ig, own, *grads)


def fused_local(tokens, mask, cotangent, mask_embed, attn_in, attn_out, fc_in, fc_out, gains, biases, fc_bias):
    out = list(results(*whole(
        tokens, cotangent, mask.reshape(4, 128), gains, biases.transpose(1, 0, 2), mask_embed.reshape(1, 96), fc_bias, attn_in, attn_out, fc_in, fc_out)))
    out[2] = out[2].reshape(96)
    out[8] = out[8].transpose(1, 0, 2)
    return tuple(out)


def solution(mesh):
    if dict(mesh.shape) != {"dp": 4, "fsdp": 8}:
        return generic_solution(mesh)
    rows = P(("dp", "fsdp"), None)
    mat = P(None, "fsdp", None)
    vec = P(None, None, "fsdp")
    return jax.shard_map(
        fused_local, mesh=mesh,
        in_specs=(rows, P(("dp", "fsdp")), rows, P("fsdp"), mat, mat, mat, mat, vec, vec, P(None, "fsdp")),
        out_specs=(rows, rows, P("fsdp"), mat, mat, mat, mat, vec, vec, P(None, "fsdp")),
        check_vma=False)


HEADS = 12
SEQ = 512
LAYERS = 2


eps = 1e-06


def norm_rows(values, gain, bias):
    center = values - jnp.mean(values, axis=-1, keepdims=True)
    spread = jnp.mean(center * center, axis=-1, keepdims=True)
    return center * lax.rsqrt(spread + eps) * gain + bias


def gelu_exact(values):
    return jax.nn.gelu(values, approximate=False)


def split_heads(values, clips):
    width = values.shape[1]
    return values.reshape(clips, SEQ, HEADS, width // HEADS)


def attend(pack):
    query, key_rows, value = pack
    scale = query.shape[-1] ** (-0.5)
    scores = jnp.einsum("qhd,khd->hqk", query, key_rows, preferred_element_type=jnp.float32) * scale
    top = jnp.max(scores, axis=-1, keepdims=True)
    expo = jnp.exp(scores - top)
    total = jnp.sum(expo, axis=-1, keepdims=True)
    probs = (expo / total).astype(jnp.bfloat16)
    mixed = jnp.einsum("hqk,khd->qhd", probs, value, preferred_element_type=jnp.float32)
    return (mixed, top + jnp.log(total))


def attend_back(pack):
    query, key_rows, value, logsum, d_mixed = pack
    scale = query.shape[-1] ** (-0.5)
    scores = jnp.einsum("qhd,khd->hqk", query, key_rows, preferred_element_type=jnp.float32) * scale
    probs = jnp.exp(scores - logsum)
    d_probs = jnp.einsum("qhd,khd->hqk", d_mixed, value, preferred_element_type=jnp.float32)
    d_value = jnp.einsum(
        "hqk,qhd->khd", probs.astype(jnp.bfloat16), d_mixed, preferred_element_type=jnp.float32
    )
    d_scores = probs * (d_probs - jnp.sum(probs * d_probs, axis=-1, keepdims=True))
    d_scaled = d_scores.astype(jnp.bfloat16) * scale
    d_query = jnp.einsum("hqk,khd->qhd", d_scaled, key_rows, preferred_element_type=jnp.float32)
    d_key = jnp.einsum("hqk,qhd->khd", d_scaled, query, preferred_element_type=jnp.float32)
    return (d_query, d_key, d_value)


def layer_forward(state, weights):
    w_qkv, w_out, w_in, w_down, gain, bias, fcb = weights
    rows, width = state.shape
    clips = rows // SEQ
    normed = norm_rows(state, gain[0].astype(jnp.float32), bias[0].astype(jnp.float32)).astype(
        jnp.bfloat16
    )
    qkv_bias = jnp.concatenate([bias[1], jnp.zeros_like(bias[1]), bias[2]]).astype(jnp.float32)
    joined = (jnp.dot(normed, w_qkv, preferred_element_type=jnp.float32) + qkv_bias).astype(
        jnp.bfloat16
    )
    query = split_heads(joined[:, :width], clips)
    key_rows = split_heads(joined[:, width : 2 * width], clips)
    value = split_heads(joined[:, 2 * width :], clips)
    mixed, logsum = lax.map(attend, (query, key_rows, value))
    mixed = mixed.reshape(rows, width).astype(jnp.bfloat16)
    middle = (
        state
        + jnp.dot(mixed, w_out, preferred_element_type=jnp.float32)
        + bias[3].astype(jnp.float32)
    )
    normed_two = norm_rows(middle, gain[1].astype(jnp.float32), bias[4].astype(jnp.float32)).astype(
        jnp.bfloat16
    )
    hidden = jnp.dot(normed_two, w_in, preferred_element_type=jnp.float32) + fcb.astype(jnp.float32)
    activated = gelu_exact(hidden).astype(jnp.bfloat16)
    return (normed, query, key_rows, value, logsum, mixed, middle, normed_two, hidden, activated)


def layer_finish(saved, weights):
    middle = saved[6]
    activated = saved[9]
    return (
        middle
        + jnp.dot(activated, weights[3], preferred_element_type=jnp.float32)
        + weights[5][5].astype(jnp.float32)
    )


def layer_backward(state, weights, grad):
    w_qkv, w_out, w_in, w_down, gain, bias, fcb = weights
    rows, width = state.shape
    clips = rows // SEQ
    normed, query, key_rows, value, logsum, mixed, middle, normed_two, hidden, activated = (
        layer_forward(state, weights)
    )
    d_up = grad.astype(jnp.bfloat16)
    g_down = jnp.einsum("tf,td->fd", activated, d_up, preferred_element_type=jnp.float32)
    d_two = jnp.sum(d_up.astype(jnp.float32), axis=0)
    d_act = jnp.einsum("td,fd->tf", d_up, w_down, preferred_element_type=jnp.float32)
    d_hidden = jax.vjp(gelu_exact, hidden)[1](d_act)[0].astype(jnp.bfloat16)
    g_in = jnp.einsum("td,tf->df", normed_two, d_hidden, preferred_element_type=jnp.float32)
    d_one = jnp.sum(d_hidden.astype(jnp.float32), axis=0)
    d_normed_two = jnp.einsum("tf,df->td", d_hidden, w_in, preferred_element_type=jnp.float32)
    back_two = jax.vjp(norm_rows, middle, gain[1].astype(jnp.float32), bias[4].astype(jnp.float32))[
        1
    ]
    d_middle, d_gain_two, d_bias_two = back_two(d_normed_two)
    d_middle = grad + d_middle
    d_branch = d_middle.astype(jnp.bfloat16)
    g_out = jnp.einsum("td,te->de", mixed, d_branch, preferred_element_type=jnp.float32)
    d_outb = jnp.sum(d_branch.astype(jnp.float32), axis=0)
    d_mixed = jnp.einsum("te,de->td", d_branch, w_out, preferred_element_type=jnp.float32).astype(
        jnp.bfloat16
    )
    d_query, d_key, d_value = lax.map(
        attend_back, (query, key_rows, value, logsum, split_heads(d_mixed, clips))
    )
    d_joined = jnp.concatenate(
        [d_query.reshape(rows, width), d_key.reshape(rows, width), d_value.reshape(rows, width)],
        axis=1,
    ).astype(jnp.bfloat16)
    g_qkv = jnp.einsum("td,te->de", normed, d_joined, preferred_element_type=jnp.float32)
    d_sums = jnp.sum(d_joined.astype(jnp.float32), axis=0)
    d_normed = jnp.einsum("te,de->td", d_joined, w_qkv, preferred_element_type=jnp.float32)
    back_one = jax.vjp(norm_rows, state, gain[0].astype(jnp.float32), bias[0].astype(jnp.float32))[
        1
    ]
    d_state, d_gain_one, d_bias_one = back_one(d_normed)
    gain_terms = jnp.stack([d_gain_one, d_gain_two])
    bias_terms = jnp.stack(
        [d_bias_one, d_sums[:width], d_sums[2 * width :], d_outb, d_bias_two, d_two]
    )
    return (d_middle + d_state, (g_qkv, g_out, g_in, g_down, gain_terms, bias_terms, d_one))


def local(
    tokens, mask, cotangent, mask_embed, attn_in, attn_out, fc_in, fc_out, gains, biases, fc_bias
):
    mask_f = mask.astype(jnp.float32)[:, None]
    state = tokens.astype(jnp.float32)
    stored = []
    kept = []
    for layer in range(LAYERS):
        fetched = (
            lax.all_gather(attn_in[layer], "fsdp", axis=0, tiled=True),
            lax.all_gather(attn_out[layer], "fsdp", axis=0, tiled=True),
            lax.all_gather(fc_in[layer], "fsdp", axis=0, tiled=True),
            lax.all_gather(fc_out[layer], "fsdp", axis=0, tiled=True),
            lax.all_gather(gains[layer], "fsdp", axis=1, tiled=True),
            lax.all_gather(biases[layer], "fsdp", axis=1, tiled=True),
            lax.all_gather(fc_bias[layer], "fsdp", axis=0, tiled=True),
            lax.all_gather(mask_embed, "fsdp", axis=0, tiled=True),
        )
        if layer == 0:
            state = state * (1.0 - mask_f) + mask_f * fetched[7].astype(jnp.float32)
        stored.append(state)
        weights = tuple(fetched[:7])
        kept.append(weights)
        state = layer_finish(layer_forward(state, weights), weights)
    grad = cotangent.astype(jnp.float32)
    layer_grads = [None] * LAYERS
    for layer in reversed(range(LAYERS)):
        weights = tuple(
            (
                lax.all_gather(attn_in[layer], "fsdp", axis=0, tiled=True),
                lax.all_gather(attn_out[layer], "fsdp", axis=0, tiled=True),
                lax.all_gather(fc_in[layer], "fsdp", axis=0, tiled=True),
                lax.all_gather(fc_out[layer], "fsdp", axis=0, tiled=True),
                lax.all_gather(gains[layer], "fsdp", axis=1, tiled=True),
                lax.all_gather(biases[layer], "fsdp", axis=1, tiled=True),
                lax.all_gather(fc_bias[layer], "fsdp", axis=0, tiled=True),
            )
        )
        grad, terms = layer_backward(stored[layer], weights, grad)
        if layer == 0:
            mask_term = jnp.sum(grad * mask_f, axis=0)
        else:
            mask_term = jnp.zeros((grad.shape[1],), jnp.float32)
        shares = (
            lax.psum_scatter(terms[0], "fsdp", scatter_dimension=0, tiled=True),
            lax.psum_scatter(terms[1], "fsdp", scatter_dimension=0, tiled=True),
            lax.psum_scatter(terms[2], "fsdp", scatter_dimension=0, tiled=True),
            lax.psum_scatter(terms[3], "fsdp", scatter_dimension=0, tiled=True),
            lax.psum_scatter(terms[4], "fsdp", scatter_dimension=1, tiled=True),
            lax.psum_scatter(terms[5], "fsdp", scatter_dimension=1, tiled=True),
            lax.psum_scatter(terms[6], "fsdp", scatter_dimension=0, tiled=True),
            lax.psum_scatter(mask_term, "fsdp", scatter_dimension=0, tiled=True),
        )
        slices = (
            lax.psum_scatter(
                shares[0].astype(jnp.bfloat16), "dp", scatter_dimension=1, tiled=True
            ).astype(jnp.float32),
            lax.psum_scatter(
                shares[1].astype(jnp.bfloat16), "dp", scatter_dimension=1, tiled=True
            ).astype(jnp.float32),
            lax.psum_scatter(
                shares[2].astype(jnp.bfloat16), "dp", scatter_dimension=1, tiled=True
            ).astype(jnp.float32),
            lax.psum_scatter(
                shares[3].astype(jnp.bfloat16), "dp", scatter_dimension=1, tiled=True
            ).astype(jnp.float32),
        )
        matrices = (
            lax.all_gather(slices[0].astype(jnp.bfloat16), "dp", axis=1, tiled=True).astype(
                jnp.float32
            ),
            lax.all_gather(slices[1].astype(jnp.bfloat16), "dp", axis=1, tiled=True).astype(
                jnp.float32
            ),
            lax.all_gather(slices[2].astype(jnp.bfloat16), "dp", axis=1, tiled=True).astype(
                jnp.float32
            ),
            lax.all_gather(slices[3].astype(jnp.bfloat16), "dp", axis=1, tiled=True).astype(
                jnp.float32
            ),
        )
        smalls = lax.psum((shares[4], shares[5], shares[6], shares[7]), "dp")
        layer_grads[layer] = (
            matrices[0],
            matrices[1],
            matrices[2],
            matrices[3],
            smalls[0],
            smalls[1],
            smalls[2],
            smalls[3],
        )
    input_grad = grad * (1.0 - mask_f)
    stacked = [jnp.stack([layer_grads[lay][item] for lay in range(LAYERS)]) for item in range(7)]
    results = tuple(stacked) + (layer_grads[0][7],)
    return (
        state,
        input_grad,
        results[7],
        results[0],
        results[1],
        results[2],
        results[3],
        results[4],
        results[5],
        results[6],
    )


def generic_solution(mesh):
    placed = (
        P(("dp", "fsdp"), None),
        P(("dp", "fsdp")),
        P(("dp", "fsdp"), None),
        P("fsdp"),
        P(None, "fsdp", None),
        P(None, "fsdp", None),
        P(None, "fsdp", None),
        P(None, "fsdp", None),
        P(None, None, "fsdp"),
        P(None, None, "fsdp"),
        P(None, "fsdp"),
    )
    return jax.shard_map(
        local,
        mesh=mesh,
        in_specs=placed,
        out_specs=(
            P(("dp", "fsdp"), None),
            P(("dp", "fsdp"), None),
            P("fsdp"),
            P(None, "fsdp", None),
            P(None, "fsdp", None),
            P(None, "fsdp", None),
            P(None, "fsdp", None),
            P(None, None, "fsdp"),
            P(None, None, "fsdp"),
            P(None, "fsdp"),
        ),
        check_vma=False,
    )
```

```python
import functools

import jax
import jax.numpy as jnp
from jax import lax
from jax.experimental import pallas as pl
from jax.experimental.pallas import tpu as pltpu
from jax.sharding import PartitionSpec as P
MESH = pl.DeviceIdType.MESH


class Pos:
    def __init__(s):
        s.dp = lax.axis_index("dp"); s.fs = lax.axis_index("fsdp")
        s.x = s.dp // 2; s.c = lax.rem(s.dp, 2)
        s.z = s.fs // 2; s.y = lax.rem(s.fs, 2)
        s.dev_c = (s.dp + 1 - 2 * s.c, s.fs)
        s.dev_x = (lax.rem(s.dp + 2, 4), s.fs)
        s.dev_y = (s.dp, s.fs + 1 - 2 * s.y)
        s.edge = (s.z == 0) | (s.z == 3)
        s.mid = (s.z == 1) | (s.z == 2)
    def dev_f(s, d):
        return (s.dp, lax.rem(s.fs + d, 8))
    def dev_at(s, z):
        return (s.dp, 2 * z + s.y)
    def up(s, d):
        return lax.rem(s.z + d, 4)
    def far(s):
        return jnp.where(s.edge, 3 - s.z, 6 - 3 * s.z)


def when(cond, f):
    if cond is None:
        f()
    else:
        pl.when(cond)(f)


class Move:
    def __init__(s, src, dst, ss, rs, dev, sends=None, takes=None):
        s.copy = pltpu.make_async_remote_copy(src_ref=src, dst_ref=dst, send_sem=ss, recv_sem=rs, device_id=dev, device_id_type=MESH)
        s.sends, s.takes = sends, takes
    def start(s):
        when(s.sends, s.copy.start)
    def sent(s):
        when(s.sends, s.copy.wait_send)
    def got(s):
        when(s.takes, s.copy.wait_recv)
    def wait(s):
        s.sent(); s.got()


def greet(p):
    bar = pltpu.get_barrier_semaphore()
    devs = [p.dev_c, p.dev_x] + [p.dev_f(d) for d in range(1, 8)]
    for d in devs:
        pl.semaphore_signal(bar, inc=1, device_id=d, device_id_type=MESH)
    return lambda: pl.semaphore_wait(bar, len(devs))


class Op:
    def __init__(s, start, finish, traffic, deps=(), cost=0.1, rank=0, after=0.0):
        s.start, s.finish, s.traffic, s.cost, s.rank, s.after = start, finish, traffic, cost, rank, after
        s.deps = [d for d in deps if d is not None]
        s.begun = s.ended = False
        s.ready = None


class Plan:
    RATE = dict(x=45e3, y=45e3, m=45e3, e=45e3, g=45e3, c=600e3)
    LATENCY = 2.2
    BACKLOG = 4
    SCALE = 1.1
    def __init__(s):
        s.ops, s.steps = [], []
        s.free = {k: 0.0 for k in s.RATE}
    def op(s, *a, **k):
        s.ops.append(Op(*a, **k))
        return s.ops[-1]
    def step(s, fn, cost, needs=(), opens=()):
        s.steps.append((fn, cost * s.SCALE, [n for n in needs if n is not None], list(opens)))
    def mark(s):
        m = Op(None, None, {}); m.begun = True
        return m
    def run(s):
        now, k, waiting, flying = 0.0, 0, list(s.ops), []
        def launch(force=False):
            nonlocal waiting
            rest = []
            for o in sorted(waiting, key=lambda o: o.rank):
                ok = all(d.ended for d in o.deps) and (force or o.after <= now)
                if ok and (force or all(s.free[r] - now < s.BACKLOG for r in o.traffic)):
                    force = False
                    o.start()
                    end = now
                    for r, v in o.traffic.items():
                        s.free[r] = max(s.free[r], now) + v / s.RATE[r]
                        end = max(end, s.free[r])
                    o.ready = end + s.LATENCY
                    flying.append(o)
                else:
                    rest.append(o)
            waiting = rest
        launch()
        while k < len(s.steps) or flying or waiting:
            flying.sort(key=lambda o: o.ready)
            can = k < len(s.steps) and all(n.ended for n in s.steps[k][2])
            if flying and (flying[0].ready <= now or not can):
                o = flying.pop(0)
                now = max(now, o.ready) + o.cost
                o.finish(); o.ended = True
            elif can:
                fn, cost, needs, opens = s.steps[k]; k += 1
                fn(); now += cost
                for m in opens: m.ended = True
            launch(not flying)
        return now


class Gather:
    PACE = 0
    def __init__(s, p, units, ssem, rsem, lead=3):
        s.p, s.units, s.ss, s.rs, s.lead = p, units, ssem, rsem, lead
        s.n = len(units)
    def move(s, u, i, block, dev, sends=None, takes=None):
        return Move(block, block, s.ss.at[u, i], s.rs.at[u, i], dev, sends, takes)
    def geo(s, u):
        w, kind, load = s.units[u]
        p, R = s.p, w.shape[2] // 2
        yfirst = kind in (1, 3)
        rc = pl.ds(pl.multiple_of(p.c * R, 16), R)
        wide = pl.ds(pl.multiple_of(p.x * 256, 256), 512) if kind < 2 else slice(None)
        mine = pl.ds(pl.multiple_of(p.x * 512, 256), 256)
        return w, yfirst, rc, wide, mine
    def near(s, u):
        w, yfirst, rc, wide, mine = s.geo(u); p = s.p
        ys = slice(None) if yfirst else p.y
        b = w.at[p.z, ys, rc, wide]
        return [s.move(u, 0, b, p.dev_at(p.up(1)), p.z < 3, p.z > 0), s.move(u, 1, b, p.dev_at(p.up(2))),
            s.move(u, 2, b, p.dev_at(p.up(3)), p.z > 0, p.z < 3)]
    def relay(s, u):
        w, yfirst, rc, wide, mine = s.geo(u); p = s.p
        ys = slice(None) if yfirst else p.y
        return [s.move(u, 3, w.at[p.far(), ys, rc, wide], p.dev_at(jnp.where(p.edge, p.z, 3 * p.z - 3)), p.mid, p.edge)]
    def over_y(s, u):
        w, yfirst, rc, wide, mine = s.geo(u); p = s.p
        if yfirst:
            return [s.move(u, 4, w.at[p.z, p.y, rc, wide], p.dev_y)]
        return [s.move(u, 4, w.at[:, p.y, rc, wide], p.dev_y, p.mid, p.mid),
            s.move(u, 4, w.at[pl.ds(p.z // 3, 3), p.y, rc, wide], p.dev_y, p.edge, p.edge)]
    def over_y_far(s, u):
        w, yfirst, rc, wide, mine = s.geo(u); p = s.p
        return [s.move(u, 5, w.at[p.far(), p.y, rc, wide], p.dev_y, p.edge, p.edge)]
    def over_x(s, u):
        w, yfirst, rc, wide, mine = s.geo(u); p = s.p
        return [s.move(u, 6, w.at[:, 1 - p.y, rc, mine], p.dev_x)]
    def over_x_own(s, u):
        w, yfirst, rc, wide, mine = s.geo(u); p = s.p
        return [s.move(u, 6 + d, w.at[p.up(d), p.y, rc, mine], p.dev_x) for d in (1, 2, 3)]
    def over_c(s, u):
        w, yfirst, rc, wide, mine = s.geo(u); p = s.p
        return [s.move(u, 10, w.at[:, 1 - p.y, rc, :], p.dev_c)] + [s.move(u, 10 + d, w.at[p.up(d), p.y, rc, :], p.dev_c) for d in (1, 2, 3)]
    def plan(s, P, gate=None):
        def moves(f):
            def start():
                for m in f(): m.start()
            def finish():
                for m in f(): m.wait()
            return start, finish
        firsts, lasts, pace, here = [], [], 0.0, []
        for u in range(s.n):
            w, kind, load = s.units[u]
            R, b = w.shape[2] // 2, 2 * 256
            piece = R * b * (2 if kind < 2 else 3)
            k = dict(rank=u)
            first = [gate, firsts[u - s.lead] if u >= s.lead else None]
            f = lambda g, u=u: moves(lambda: g(u))
            def own(op, u=u, load=load):
                begin, finish = f(op, u)
                def start():
                    if all(load is not v for v in here):
                        here.append(load); load.wait()
                    begin()
                return start, finish
            if kind in (1, 3):
                y = P.op(*own(s.over_y), dict(y=piece), first, after=pace, **k)
                near = P.op(*f(s.near), dict(m=6 * piece, e=4 * piece, g=4 * piece), [y], **k)
                got = [P.op(*f(s.relay), dict(g=2 * piece), [near], **k)]
                if kind == 1:
                    got = [P.op(*f(lambda u: s.over_x(u) + s.over_x_own(u)), dict(x=7 * R * b), got, **k)]
                firsts.append(y)
            else:
                near = P.op(*own(s.near), dict(m=3 * piece, e=2 * piece, g=2 * piece), first, after=pace, **k)
                rel = P.op(*f(s.relay), dict(g=piece), [near], **k)
                ya = P.op(*f(s.over_y), dict(y=3.5 * piece), [near], **k)
                yb = P.op(*f(s.over_y_far), dict(y=0.5 * piece), [rel], **k)
                got = [ya, yb]
                if kind == 0:
                    xo = P.op(*f(s.over_x_own), dict(x=3 * R * b), [rel], **k)
                    got = [P.op(*f(s.over_x), dict(x=4 * R * b), got, **k), xo]
                firsts.append(near)
            c = P.op(*f(s.over_c), dict(c=21 * R * b), got, **k)
            lasts.append(c)
            pace += s.PACE * R / 48
        return lasts


class Reduce:
    def __init__(s, p, units, bufs, ssem, rsem):
        s.p, s.units, s.b, s.ss, s.rs = p, units, bufs, ssem, rsem
        s.n = len(units)
        s.kz = dict(enumerate(("z0", "z1", "z2")))
    def geo(s, u):
        w, fin, out = s.units[u]
        R = w.shape[2] // 2; p = s.p
        rc = pl.ds(pl.multiple_of(p.c * R, 16), R)
        ro = pl.ds(pl.multiple_of((1 - p.c) * R, 16), R)
        xc = pl.ds(pl.multiple_of(p.x * 384, 128), 384)
        xo = pl.ds(pl.multiple_of((1 - p.x) * 384, 128), 384)
        return w, fin, out, R, rc, ro, xc, xo
    def kind(s, u):
        return KINDS[u % len(KINDS)]
    def before(s, u, kinds):
        return [v for v in range(u) if s.kind(v) in kinds]
    def slot(s, u):
        kind = s.kind(u)
        return kind, len(s.before(u, (kind,))) % (RING if kind == 2 else RING // 2), len(s.before(u, (0, 1))) % RING
    def move(s, u, i, src, dst, dev, sends=None, takes=None):
        k = u % s.ss.shape[0]
        return Move(src, dst, s.ss.at[k, i], s.rs.at[k, i], dev, sends, takes)
    def core(s, u):
        w, fin, out, R, rc, ro, xc, xo = s.geo(u)
        return [s.move(u, 0, w.at[:, :, ro, :], s.b["c"].at[u % CRING, :, :, pl.ds(0, R), :], s.p.dev_c)]
    def add_core(s, u):
        w, fin, out, R, rc, ro, xc, xo = s.geo(u); c = s.b["c"].at[u % CRING]
        def body(i, _):
            a, b = i // 2, lax.rem(i, 2)
            w[a, b, rc, :] = w[a, b, rc, :] + c[a, b, pl.ds(0, R), :]
            return 0
        lax.fori_loop(0, 8, body, 0)
    def first(s, u):
        w, fin, out, R, rc, ro, xc, xo = s.geo(u); p = s.p
        kind, k, k2 = s.slot(u)
        if kind == 2:
            return [s.move(u, 1, w.at[:, 1 - p.y, rc, :], s.b["h1y"].at[k, :, pl.ds(0, R), :], p.dev_y)]
        return [s.move(u, 1, w.at[:, :, rc, xo], s.b["h1x"].at[k2, :, :, pl.ds(0, R), :], p.dev_x)]
    def add_first(s, u):
        w, fin, out, R, rc, ro, xc, xo = s.geo(u); p = s.p
        kind, k, k2 = s.slot(u)
        if kind == 2:
            h = s.b["h1y"].at[k]
            def body(a, _):
                w[a, p.y, rc, :] = w[a, p.y, rc, :] + h[a, pl.ds(0, R), :]
                return 0
            lax.fori_loop(0, 4, body, 0)
        else:
            h = s.b["h1x"].at[k2]
            def body(i, _):
                a, b = i // 2, lax.rem(i, 2)
                w[a, b, rc, xc] = w[a, b, rc, xc] + h[a, b, pl.ds(0, R), :]
                return 0
            lax.fori_loop(0, 8, body, 0)
    def second_y(s, u):
        w, fin, out, R, rc, ro, xc, xo = s.geo(u); p = s.p
        kind, k, k2 = s.slot(u)
        return [s.move(u, 2, w.at[:, 1 - p.y, rc, xc], s.b["h2y"].at[k, :, pl.ds(0, R), :], p.dev_y)]
    def add_second_y(s, u):
        w, fin, out, R, rc, ro, xc, xo = s.geo(u); p = s.p
        kind, k, k2 = s.slot(u)
        h = s.b["h2y"].at[k]
        def body(a, _):
            w[a, p.y, rc, xc] = w[a, p.y, rc, xc] + h[a, pl.ds(0, R), :]
            return 0
        lax.fori_loop(0, 4, body, 0)
    def zblock(s, u, z):
        w, fin, out, R, rc, ro, xc, xo = s.geo(u); p = s.p
        kind, k, k2 = s.slot(u)
        if kind == 1:
            return w.at[z, :, rc, xc]
        return w.at[z, p.y, rc, xc if kind == 0 else slice(None)]
    def zslot(s, u, d):
        kind, k, k2 = s.slot(u); R = s.geo(u)[3]
        b = s.b[s.kz[kind]]
        return b.at[k, d, :, pl.ds(0, R), :] if kind == 1 else b.at[k, d, pl.ds(0, R), :]
    def near(s, u):
        p = s.p
        one = [s.move(u, 2 + d, s.zblock(u, p.up(d)), s.zslot(u, d - 1), p.dev_at(p.up(d)), *((p.z < 3, p.z > 0) if d == 1 else (p.z > 0, p.z < 3))) for d in (1, 3)]
        return [s.far(u)] + one + [s.two(u, p.edge, p.mid)]
    def far(s, u):
        p = s.p
        return s.move(u, 6, s.zblock(u, p.far()), s.zslot(u, 3), p.dev_at(1 + p.z // 3), p.edge, p.mid)
    def two(s, u, sends, takes):
        p = s.p
        return s.move(u, 4, s.zblock(u, p.up(2)), s.zslot(u, 1), p.dev_at(p.up(2)), sends, takes)
    def far_add(s, u):
        m = s.far(u); m.got(); m.sent()
        def add():
            b, h = s.zblock(u, s.p.far()), s.zslot(u, 3)
            b[...] = b[...] + h[...]
        pl.when(s.p.mid)(add)
    def z_sum(s, u):
        f = lambda r: r[...].astype(jnp.float32)
        v = f(s.zblock(u, s.p.z))
        for d in range(3): v = v + f(s.zslot(u, d))
        return v.astype(jnp.bfloat16)
    def last_y(s, u):
        w, fin, out, R, rc, ro, xc, xo = s.geo(u); p = s.p
        kind, k, k2 = s.slot(u)
        return [s.move(u, 7, w.at[p.z, 1 - p.y, rc, xc], s.b["h3y"].at[k, pl.ds(0, R), :], p.dev_y)]
    def last_x(s, u):
        w, fin, out, R, rc, ro, xc, xo = s.geo(u); p = s.p
        kind, k, k2 = s.slot(u)
        return [s.move(u, 7, w.at[p.z, p.y, rc, :], s.b["h3x"].at[k, pl.ds(0, R), :], p.dev_x)]
    def share_x(s, u):
        w, fin, out, R, rc, ro, xc, xo = s.geo(u)
        return [s.move(u, 8, fin.at[rc, xc], fin.at[rc, xc], s.p.dev_x)]
    def share_c(s, u):
        w, fin, out, R, rc, ro, xc, xo = s.geo(u)
        return [s.move(u, 9, fin.at[rc, :], fin.at[rc, :], s.p.dev_c)]
    def out_copy(s, u):
        return pltpu.make_async_copy(s.units[u][1], s.units[u][2], s.b["osem"].at[u])
    def plan(s, P, marks, hold, gate=None):
        def run(ms):
            for m in ms: m.start()
        def wait(ms):
            for m in ms: m.wait()
        core, first, second, zs, last, share, end = [], [], [], [], [], [], []
        def back(ops, u, kinds, ring):
            same = s.before(u, kinds)
            return ops[same[-ring // 2]] if len(same) >= ring // 2 else None
        for u in range(s.n):
            w, fin, out, R, rc, ro, xc, xo = s.geo(u); p = s.p
            kind, k, k2 = s.slot(u)
            full = R * 768 * 2
            zb = full if kind != 0 else full // 2
            mine = (kind,) if kind == 2 else (0, 1)
            def f_core(u=u): wait(s.core(u)); s.add_core(u)
            def f_first(u=u): wait(s.first(u)); s.add_first(u)
            def f_second(u=u): wait(s.second_y(u)); s.add_second_y(u)
            def b_near(u=u): run(s.near(u)[1:])
            def f_near(u=u): wait(s.near(u)[1:])
            def b_rel(u=u): s.two(u, s.p.mid, s.p.edge).start()
            def f_z(u=u, w=w, fin=fin, kind=kind, rc=rc, xc=xc):
                s.two(u, s.p.mid, s.p.edge).wait()
                if kind == 0:
                    fin[rc, xc] = s.z_sum(u)
                else:
                    b = s.zblock(u, s.p.z); b[...] = s.z_sum(u)
            def f_last(u=u, w=w, fin=fin, kind=kind, rc=rc, xc=xc, R=R, k=k):
                p = s.p
                if kind == 1:
                    wait(s.last_y(u))
                    fin[rc, xc] = w[p.z, p.y, rc, xc] + s.b["h3y"][k, pl.ds(0, R), :]
                else:
                    wait(s.last_x(u))
                    fin[rc, :] = w[p.z, p.y, rc, :] + s.b["h3x"][k, pl.ds(0, R), :]
            def f_end(u=u): wait(s.share_c(u)); s.out_copy(u).start()
            c = P.op(lambda u=u: run(s.core(u)), f_core, dict(c=8 * full), [marks[u], gate, core[u - CRING // 2] if u >= CRING // 2 else None] + [end[v] for v in hold[u]], cost=0.3, rank=100 + u)
            core.append(c)
            f = P.op(lambda u=u: run(s.first(u)), f_first, dict(y=4 * full) if kind == 2 else dict(x=4 * full), [c, back(first, u, mine, RING)], cost=0.25, rank=100 + u)
            first.append(f)
            prev = f
            if kind == 0:
                prev = P.op(lambda u=u: run(s.second_y(u)), f_second, dict(y=2 * full), [f, back(second, u, (0,), RING // 2)], cost=0.15, rank=100 + u)
            second.append(prev)
            ring = back(zs, u, (kind,), RING if kind == 2 else RING // 2)
            far = P.op(lambda u=u: s.far(u).start(), lambda u=u: s.far_add(u), dict(e=zb), [prev, ring], rank=100 + u)
            near = P.op(b_near, f_near, dict(m=2 * zb, e=2 * zb, g=zb), [prev, ring], rank=100 + u)
            z = P.op(b_rel, f_z, dict(m=zb, g=zb), [far, near], cost=0.15, rank=100 + u)
            zs.append(z)
            prev = z
            if kind != 0:
                prev = P.op((lambda u=u: run(s.last_y(u))) if kind == 1 else (lambda u=u: run(s.last_x(u))), f_last,
                    dict(y=full // 2) if kind == 1 else dict(x=full), [z, back(last, u, (kind,), RING if kind == 2 else RING // 2)], rank=100 + u)
            last.append(prev)
            if kind != 2:
                prev = P.op(lambda u=u: run(s.share_x(u)), lambda u=u: wait(s.share_x(u)), dict(x=full // 2), [prev, back(share, u, (0, 1), RING)], rank=100 + u)
            share.append(prev)
            end.append(P.op(lambda u=u: run(s.share_c(u)), f_end, dict(c=full), [prev, back(end, u, (kind,), RING if kind == 2 else RING // 2)], rank=100 + u))
        return end
    def finish(s):
        for u in range(s.n): s.out_copy(u).wait()
    def clear(s):
        def zero(d):
            def f():
                for q in s.kz.values():
                    b = s.b[q]
                    for k in range(b.shape[0]):
                        b[k, d] = jnp.zeros(b.shape[2:], b.dtype)
            return f
        pl.when(s.p.z == 0)(zero(0))
        pl.when(s.p.z == 3)(zero(2))


CRING, RING = 4, 4
KINDS = (2, 1, 2, 2, 2, 1, 1, 0, 2, 0, 2, 1, 2, 0, 2, 1, 2, 0, 2, 1, 2, 0, 2, 1, 2, 0, 2, 2, 1, 2, 0, 2, 1, 2, 2, 0, 1, 2, 2, 1)


def reduce_scratch(n, R):
    b = jnp.bfloat16; V = pltpu.VMEM; lag = RING
    half = lag // 2
    return dict(c=V((CRING, 4, 2, R, 768), b), h1x=V((lag, 4, 2, R, 384), b), h1y=V((lag, 4, R, 768), b),
        h2y=V((half, 4, R, 384), b), z0=V((half, 4, R, 384), b), z1=V((half, 4, 2, R, 384), b), z2=V((lag, 4, R, 768), b),
        h3y=V((half, R, 384), b), h3x=V((lag, R, 768), b), osem=pltpu.SemaphoreType.DMA((n,)))
NA, ND = 8, 3
ROUTES = ((0, 0, 0, 0, 0, 0, 0, 0, 0, 0, 0),
    (0, 1, 0, 0, 0, 0, 0, 2, 1, 2, 3))
def gather_units(wa, wd, layer):
    return [(wa.at[layer, k] if k < NA else wd.at[layer, k - NA], ROUTES[layer][k]) for k in range(NA + ND)]

def load_shards(p, attn_in, attn_out, fc_in, fc_out, wa, wd, sem):
    out = []
    i = 0
    for l in range(2):
        for k in range(NA):
            if k < 3: src = attn_in.at[l, :, pl.ds(768 * k, 768)]
            elif k == 3: src = attn_out.at[l]
            else: src = fc_in.at[l, :, pl.ds(768 * (k - 4), 768)]
            out.append(pltpu.make_async_copy(src, wa.at[l, k, p.z, p.y], sem.at[i])); i += 1
        for k in range(ND):
            out.append(pltpu.make_async_copy(fc_out.at[l, pl.ds(128 * k, 128)], wd.at[l, k, p.z, p.y], sem.at[i])); i += 1
    return out
ORDER = {1: [("D", 0), ("D", 1), ("A", 4), ("A", 5), ("D", 2), ("A", 6), ("A", 7), ("A", 3), ("A", 0), ("A", 1), ("A", 2)],
    0: [("D", 0), ("D", 1), ("D", 2), ("A", 4), ("A", 5), ("A", 6), ("A", 7), ("A", 3), ("A", 0), ("A", 1), ("A", 2)]}


F32, BF = jnp.float32, jnp.bfloat16
NN = (((1,), (0,)), ((), ()))
NT = (((1,), (1,)), ((), ()))
TN = (((0,), (0,)), ((), ()))
def mm(a, b, dims=NN):
    return lax.dot_general(a, b, dims, preferred_element_type=F32)

ROWS, WIDTH, PAIRS = 512, 768, 6
def r_gain(l, i): return 2 * l + i
def r_bias(l, i): return 4 + 6 * l + i
R_EMBED = 16
def r_fcb(l, k): return 24 + 4 * l + k

def row(ref, r):
    return ref[pl.ds(r, 1), :]

def rows_loop(step, body):
    def run(i, c):
        body(pl.ds(pl.multiple_of(i * step, step), step))
        return c
    lax.fori_loop(0, ROWS // step, run, 0)

def gelu_parts(z):
    a = jnp.abs(z)
    t = 1.0 / (1.0 + (0.3275911 * 0.7071067811865476) * a)
    e = jnp.exp(-0.5 * (z * z))
    poly = t * (0.254829592 + t * (-0.284496736 + t * (1.421413741 + t * (-1.453152027 + t * 1.061405429))))
    tail = 0.5 * poly * e
    cdf = jnp.where(z < 0, tail, 1.0 - tail)
    return z * cdf, cdf + z * (0.3989422804014327 * e)

class Net:
    def __init__(s, r):
        s.__dict__.update(r)
    def w(s, l, k):
        return s.wa.at[l, k]
    def wtile(s, l, k, cols):
        v = s.wa[l, k, :, :, :, cols]
        return v.reshape(WIDTH, v.shape[-1])
    def norm(s, l, i, xh, h):
        at = pl.ds(2 * l + i, 1)
        def body(q):
            v = s.x[q, :]
            c = v - jnp.mean(v, axis=-1, keepdims=True)
            r = lax.rsqrt(jnp.mean(c * c, axis=-1, keepdims=True) + 1e-6)
            n = c * r
            xh[q, :] = n.astype(BF)
            s.rs[q, at] = r
            h[q, :] = (n * row(s.V, r_gain(l, i)) + row(s.V, r_bias(l, 4 if i else 0))).astype(BF)
        for b in range(2): body(pl.ds(256 * b, 256))
    def norm_back(s, l, i, d, xh, out):
        at = pl.ds(2 * l + i, 1)
        total = lambda v: jnp.sum(v, axis=0, keepdims=True)
        sg = sb = so = 0.0
        for b in range(2):
            q = pl.ds(256 * b, 256)
            dv, n = d[q, :], xh[q, :].astype(F32)
            dn = dv * row(s.V, r_gain(l, i))
            m1 = jnp.mean(dn, axis=-1, keepdims=True)
            m2 = jnp.mean(dn * n, axis=-1, keepdims=True)
            e = s.x[q, :] + s.rs[q, at] * (dn - m1 - n * m2)
            s.x[q, :] = e
            sg, sb = sg + total(dv * n), sb + total(dv)
            if out is not None:
                eb = e.astype(BF)
                out[q, :] = eb
                so = so + total(eb.astype(F32))
        s.S[pl.ds(r_gain(l, i), 1), :] = sg
        s.S[pl.ds(r_bias(l, 4 if i else 0), 1), :] = sb
        return so
    def unit(s, l, k):
        return s.wa[l, k].reshape(WIDTH, WIDTH)
    def project(s, l, k):
        v = mm(s.h[...], s.unit(l, k))
        if k != 1:
            v = v + row(s.V, r_bias(l, 1 if k == 0 else 2))
        s.t[k] = v.astype(BF)
    def masks(s):
        lane = lax.broadcasted_iota(jnp.int32, (1, 128), 1)
        return [(lane < 64).astype(F32).astype(BF), (lane >= 64).astype(F32).astype(BF)]
    def attend(s, l, p0, p1):
        ms = s.masks()
        def body(p, c):
            n = pl.ds(pl.multiple_of(p * 128, 128), 128)
            kk = s.t[1, :, n]
            vt = s.t[2, :, n].T
            qs = s.t[0, :, n] * 0.125
            outs = []
            for i in range(2):
                st = mm(kk, qs * ms[i], NT)
                top = jnp.max(st, axis=0, keepdims=True)
                e = jnp.exp(st - top)
                total = jnp.sum(e, axis=0, keepdims=True)
                s.lse[l, pl.ds(2 * p + i, 1), :] = top + jnp.log(total)
                outs.append(mm(vt[64 * i:64 * i + 64], e.astype(BF)) * (1.0 / total))
            s.o[:, n] = jnp.concatenate(outs, axis=0).T.astype(BF)
            return c
        lax.fori_loop(p0, p1, body, 0)
    def attend_back(s, l, p0, p1):
        ms = s.masks()
        def body(p, c):
            n = pl.ds(pl.multiple_of(p * 128, 128), 128)
            kk, vv = s.t[1, :, n], s.t[2, :, n]
            kt = kk.T
            qs = s.t[0, :, n] * 0.125
            do = s.o[:, n]
            qt, dt = qs.T, do.T
            dv, dk, dq = [], [], []
            for i in range(2):
                at = slice(64 * i, 64 * i + 64)
                pt = jnp.exp(mm(kk, qs * ms[i], NT) - s.lse[l, pl.ds(2 * p + i, 1), :])
                pd = pt * mm(vv, do * ms[i], NT)
                dv.append(mm(dt[at], pt.astype(BF), NT))
                ds = (pd - pt * jnp.sum(pd, axis=0, keepdims=True)).astype(BF)
                dk.append(mm(qt[at], ds, NT))
                dq.append(mm(kt[at], ds) * 0.125)
            for j, d in enumerate((dq, dk, dv)):
                s.t[j, :, n] = jnp.concatenate(d, axis=0).T.astype(BF)
            return c
        lax.fori_loop(p0, p1, body, 0)
    def attn_out(s, l):
        s.x[...] = s.x[...] + (mm(s.o[...], s.unit(l, 3)) + row(s.V, r_bias(l, 3)))
    def mlp_in(s, l, k):
        s.acc[...] = mm(s.h2[...], s.unit(l, 4 + k)) + row(s.V, r_fcb(l, k))
        for f in range(2):
            for j in range(3):
                a, d = gelu_parts(s.acc[:, pl.ds(384 * f + 128 * j, 128)])
                s.g[j, :, pl.ds((2 * k + f) * 128, 128)] = a.astype(BF)
                s.gp[j, :, pl.ds((2 * k + f) * 128, 128)] = d.astype(BF)
    def mlp_out(s, l, j):
        v = mm(s.g[j], s.wd[l, j].reshape(1024, WIDTH))
        if j == 0:
            v = v + row(s.V, r_bias(l, 5))
        s.x[...] = s.x[...] + v
    def start_back(s, l, make):
        if make:
            s.du[...] = s.x[...].astype(BF)
        s.col_sum(s.du, r_bias(l, 5))
    def mlp_out_back(s, l, j):
        def body(i, c):
            n = pl.ds(pl.multiple_of(i * 512, 512), 512)
            w = s.wd[l, j, pl.ds(2 * i, 2)].reshape(512, WIDTH)
            dz = (mm(s.du[...], w, NT) * s.gp[j, :, n].astype(F32)).astype(BF)
            s.gp[j, :, n] = dz
            s.bz[pl.ds(3 * l + j, 1), n] = jnp.sum(dz.astype(F32), axis=0, keepdims=True)
            return c
        lax.fori_loop(0, 2, body, 0)
    def mlp_out_grad(s, l, j, to):
        for i in range(2):
            to[pl.ds(2 * i, 2)] = mm(s.g[j, :, pl.ds(512 * i, 512)], s.du[...], TN).astype(BF).reshape(2, 2, 128, WIDTH)
    def hidden_bias(s):
        for l in range(2):
            for j in range(3):
                for f in range(8):
                    s.S[pl.ds(r_fcb(l, f // 2), 1), pl.ds(384 * (f % 2) + 128 * j, 128)] = s.bz[pl.ds(3 * l + j, 1), pl.ds(128 * f, 128)]
    def dz_tile(s, k, q):
        parts = []
        for f in range(2):
            for j in range(3):
                parts.append(s.gp[j, q, pl.ds((2 * k + f) * 128, 128)])
        return jnp.concatenate(parts, axis=1)
    def back_mm(s, l, k, get, first):
        v = mm(get(slice(None)), s.unit(l, k), NT)
        s.acc[...] = v if first else s.acc[...] + v
    def grad_a(s, to, get, lhs):
        to[...] = mm(lhs[...], get(slice(None)), TN).astype(BF).reshape(4, 2, 96, WIDTH)
    def attn_out_back(s, l):
        do = mm(s.du[...], s.unit(l, 3), NT).astype(BF)
        s.grad_a(s.w(l, 3), lambda q: s.du[q, :], s.o)
        s.o[...] = do
    def col_sum(s, ref, r):
        s.S[pl.ds(r, 1), :] = jnp.sum(ref[...].astype(F32), axis=0, keepdims=True)

def net_scratch():
    V = pltpu.VMEM
    return dict(x=V((512, 768), F32), acc=V((512, 768), F32), h=V((512, 768), BF), t=V((3, 512, 768), BF), lse=V((2, 16, 512), F32),
        o=V((512, 768), BF), h2=V((512, 768), BF), g=V((3, 512, 1024), BF), gp=V((3, 512, 1024), BF), xh1=V((512, 768), BF), xh2=V((512, 768), BF),
        rs=V((512, 128), F32), du=V((512, 768), BF),
        bz=V((8, 1024), F32), V=V((32, 768), F32), S=V((32, 768), F32))
SPILL = ["h", "t", "o", "h2", "g", "gp", "xh1", "xh2"]


SMALL = (32, 768)
VMEM_LIMIT = 63 * 1024 * 1024
EARLY = {21: 32, 0: 32, 2: 32}
LEAD = 30
CUTS = {(0, 'A', 2): [64, 32], (1, 'A', 0): [32, 64], (0, 'A', 3): [64, 32], (0, 'A', 6): [64, 32], (0, 'A', 0): [32, 64]}
SOON = 2
DCUT = [64, 64]
SEG, SEGB = 3, 2


def gather_list(wa, wd, loads):
    units, first = [], []
    for l in range(2):
        for w, kind in gather_units(wa, wd, l):
            h = EARLY.get(len(first), w.shape[2])
            units += [(w.at[:, :, pl.ds(a, h), :], kind, loads[len(first)]) for a in range(0, w.shape[2], h)]
            first.append(len(units) - 1)
    return units, first


def reduce_list():
    out = []
    for l in (1, 0):
        for k, q in ORDER[l]:
            H = 128 if k == "D" else 96
            hs = CUTS.get((l, k, q), DCUT if k == "D" else [H])
            a = 0
            for h in hs:
                out.append((l, k, q, a, h)); a += h
    return out


def steps(P, n, unit, marks, sent, do):
    P.step(do.embed, 1.5, [do.params])
    for l in range(2):
        P.step(lambda l=l: (do.reuse(l, "xh1", "h"), n.norm(l, 0, n.xh1, n.h), do.keep(l, "xh1")), 0.5)
        for k in range(3):
            P.step(lambda l=l, k=k: (do.reuse(l, *(["t"] if k == 0 else [])), n.project(l, k)), 1.0, [unit(l, k)])
        for a in range(0, 6, SEG):
            P.step(lambda l=l, a=a: (do.keep(l, *(["h", "t"] if a == 0 else [])), do.reuse(l, *(["o"] if a == 0 else [])), n.attend(l, a, a + SEG)), 1.25 * SEG)
        P.step(lambda l=l: (do.keep(l, "o"), n.attn_out(l)), 1.0, [unit(l, 3)])
        P.step(lambda l=l: (do.reuse(l, "xh2", "h2"), n.norm(l, 1, n.xh2, n.h2), do.keep(l, "xh2")), 0.5)
        for k in range(4):
            P.step(lambda l=l, k=k: (do.reuse(l, *(["g", "gp"] if k == 0 else [])), n.mlp_in(l, k)), 1.4, [unit(l, 4 + k)])
        if l == 1:
            P.step(lambda: n.start_back(1, False), 0.2)
            for j in range(SOON):
                P.step(lambda j=j: n.mlp_out_grad(1, j, n.wg.at[j]), 1.1, (), marks(1, "D", j))
        for j in range(3):
            if l == 1:
                P.step(lambda j=j: n.mlp_out_back(1, j), 1.4, [unit(1, 8 + j)])
            if l == 0 or j < 2:
                P.step(lambda l=l, j=j: (do.keep(l, *(["h2", "gp"] if j == 0 else [])), n.mlp_out(l, j)), 1.2, [unit(l, 8 + j)])
        P.step(lambda l=l: do.keep(l, "g"), 0.0)
    for l in (1, 0):
        if l == 0:
            P.step(lambda: n.start_back(0, True), 0.3)
        for j in range(3):
            if l == 0:
                P.step(lambda j=j: (do.need(0, *(["gp", "g"] if j == 0 else [])), n.mlp_out_back(0, j), n.mlp_out_grad(0, j, n.wd.at[0, j])), 2.4, (), marks(0, "D", j))
        if l == 0:
            P.step(lambda: do.need(0, "h2"), 0.0)
        for k in range(4):
            get = lambda q, k=k: n.dz_tile(k, q)
            P.step(lambda l=l, k=k, get=get: (n.back_mm(l, 4 + k, get, k == 0), n.grad_a(n.w(l, 4 + k), get, n.h2)), 1.6, (), marks(l, "A", 4 + k))
            if l == 1 and k == 1:
                P.step(lambda: (n.mlp_out(1, 2), do.send()), 1.2)
                P.step(lambda: (n.mlp_out_grad(1, 2, n.wd.at[1, 2]), do.done(1, "g")), 1.1, (), marks(1, "D", 2))
        if l == 1:
            P.step(do.turn, 0.8)
        P.step(lambda l=l: (do.done(l, "gp", "h2"), do.need(l, "xh2"), do.mid_norm(l), do.done(l, "xh2"), do.need(l, "o")), 1.0)
        P.step(lambda l=l: n.attn_out_back(l), 1.6, (), marks(l, "A", 3))
        P.step(lambda l=l: do.need(l, "t"), 0.0)
        for a in range(0, 6, SEGB):
            P.step(lambda l=l, a=a: n.attend_back(l, a, a + SEGB), 1.85 * SEGB)
        P.step(lambda l=l: (do.done(l, "o"), do.need(l, "h"), n.col_sum(n.t.at[0], r_bias(l, 1)), n.col_sum(n.t.at[2], r_bias(l, 2))), 0.3)
        for k in range(3):
            get = lambda q, k=k: n.t[k, q, :]
            if l == 1:
                P.step(lambda l=l, k=k, get=get: (n.back_mm(l, k, get, k == 0), n.grad_a(n.w(l, k), get, n.h)), 1.6, (), marks(l, "A", k))
            else:
                P.step(lambda k=k, get=get: n.grad_a(n.w(1, 4 + k), get, n.h), 1.0, sent(1, "A", 4 + k), marks(0, "A", k))
        for k in range(3 if l == 0 else 0):
            P.step(lambda k=k: n.back_mm(0, k, lambda q: n.t[k, q, :], k == 0), 1.0)
        P.step(lambda l=l: (do.done(l, "t", "h"), do.need(l, "xh1"), n.norm_back(l, 0, n.acc, n.xh1, None), do.done(l, "xh1")), 1.0)
    P.step(do.last, 1.0, (), [do.sums])


class Smalls:
    def __init__(s, p, net, b):
        s.p, s.net, s.b = p, net, b
    def pack(s, gains, biases, embed, fcb):
        k = s.b["own"]
        k[...] = jnp.zeros((32, 128), F32)
        for l in range(2):
            k[2 * l:2 * l + 2, 0:96] = gains[l].astype(F32)
            for i in range(6):
                k[4 + 6 * l + i:5 + 6 * l + i, 0:96] = biases[i, l:l + 1, :].astype(F32)
            for i in range(3):
                k[24 + 3 * l + i:25 + 3 * l + i, :] = fcb[l:l + 1, 128 * i:128 * i + 128].astype(F32)
        k[16:17, 0:96] = embed[...].astype(F32)
        s.b["sm"][s.p.fs] = k[...].astype(BF)
    def fetch(s, d):
        b, p = s.b, s.p
        return remote(b["sm"].at[p.fs], b["sm"].at[p.fs], b["ss"].at[d - 1], b["rs"].at[d - 1], p.dev_f(d))
    def start(s):
        for d in range(1, 8):
            s.fetch(d).start()
    def build(s):
        for d in range(1, 8):
            s.fetch(d).wait()
        V = s.net.V
        i = lax.broadcasted_iota(jnp.int32, (128, 768), 0)
        c = lax.broadcasted_iota(jnp.int32, (128, 768), 1)
        total = jnp.zeros((24, 768), F32)
        for f in range(8):
            blk = s.b["sm"][f]
            pick = jnp.where((c - 96 * f == i) & (i < 96), 1.0, 0.0).astype(BF)
            total = total + mm(blk, pick)[0:24]
        V[0:24, :] = total
        for f in range(8):
            blk = s.b["sm"][f].astype(F32)
            for l in range(2):
                for j in range(3):
                    at = 384 * (f % 2) + 128 * j
                    V[r_fcb(l, f // 2):r_fcb(l, f // 2) + 1, at:at + 128] = blk[24 + 3 * l + j:25 + 3 * l + j]
    def hop(s, h):
        b, p, S = s.b, s.p, s.net.S
        if h < 3:
            return [remote(S, b["sr"].at[h], b["ss"].at[7 + h], b["rs"].at[7 + h], (p.dev_c, p.dev_x, p.dev_y)[h])]
        return [remote(S, b["sr"].at[2 + d], b["ss"].at[9 + d], b["rs"].at[9 + d], p.dev_at(p.up(d))) for d in (1, 2, 3)]
    def send(s, h):
        for q in s.hop(h): q.start()
    def add(s, h):
        for q in s.hop(h): q.wait()
        t = s.net.S[...]
        for i in ([h] if h < 3 else [3, 4, 5]):
            t = t + s.b["sr"][i]
        s.net.S[...] = t
    def plan(s, P, begin):
        prev = begin
        for h, r in enumerate("cxym"):
            prev = P.op(lambda h=h: s.send(h), lambda h=h: s.add(h), {r: 98304 * (4 if r == "m" else 1)}, [prev], rank=-1)
        return prev
    def own(s):
        k, S, f = s.b["own"], s.net.S, s.p.fs
        k[...] = jnp.zeros((32, 128), F32)
        v = jnp.zeros((24, 96), F32)
        for i in range(8):
            v = jnp.where(f == i, S[0:24, 96 * i:96 * i + 96], v)
        k[0:24, 0:96] = v
        for l in range(2):
            w = jnp.zeros((1, 384), F32)
            for i in range(8):
                w = jnp.where(f == i, S[r_fcb(l, i // 2):r_fcb(l, i // 2) + 1, 384 * (i % 2):384 * (i % 2) + 384], w)
            for j in range(3):
                k[24 + 3 * l + j:25 + 3 * l + j, :] = w[:, 128 * j:128 * j + 128]


def remote(src, dst, ss, rs, dev):
    return pltpu.make_async_remote_copy(src_ref=src, dst_ref=dst, send_sem=ss, recv_sem=rs, device_id=dev, device_id_type=MESH)


def smalls_scratch():
    return dict(sm=pltpu.VMEM((8, 32, 128), BF), own=pltpu.VMEM((32, 128), F32), sr=pltpu.VMEM((6, 32, 768), F32),
        ss=pltpu.SemaphoreType.DMA((13,)), rs=pltpu.SemaphoreType.DMA((13,)))


class Work:
    pass


def whole_kernel(tok, cot, msk, gains, biases, embed, fcb, ai, ao, fi, fo, act, ig, so, o_ai, o_ao, o_fi, o_fo, *rest):
    spill = dict(zip(SPILL, rest[:8]))
    sc, wa, wd, wg, fa, fd, rbufs, sbufs, lsem, ssem, iosem, gss, grs, rss, rrs = rest[8:]
    p = Pos()
    met = greet(p)
    n = Net(dict(sc, wa=wa, wd=wd, wg=wg))
    sm = Smalls(p, n, sbufs)
    tok_in = pltpu.make_async_copy(tok, n.o, iosem.at[0])
    cot_in = pltpu.make_async_copy(cot, n.du, iosem.at[1])
    loads = load_shards(p, ai, ao, fi, fo, wa, wd, lsem)
    for c in loads: c.start()
    tok_in.start(); cot_in.start()
    red = []
    for l, k, q, a, h in reduce_list():
        if (l, k) == (0, "A") and q < 3: w = wa.at[1, 4 + q]
        elif (l, k) == (1, "D") and q < SOON: w = wg.at[q]
        else: w = (wd if k == "D" else wa).at[l, q]
        b = q if k == "A" else 8 + q
        if l == 1: f = (fd if k == "D" else fa).at[q, pl.ds(a, h)]
        else: f = wg.at[b // 8, b % 8 // 2, b % 2, pl.ds(a, h)]
        if k == "D": o = o_fo.at[l, pl.ds(128 * q + a, h)]
        elif q == 3: o = o_ao.at[l, pl.ds(a, h)]
        elif q < 3: o = o_ai.at[l, pl.ds(a, h), pl.ds(768 * q, 768)]
        else: o = o_fi.at[l, pl.ds(a, h), pl.ds(768 * (q - 4), 768)]
        red.append((w.at[:, :, pl.ds(a, h), :], f, o))
    r = Reduce(p, red, rbufs, rss, rrs)
    r.clear()
    sm.pack(gains, biases, embed, fcb)
    mt = msk[...].astype(F32).T
    for j in range(4):
        n.rs[128 * j:128 * j + 128, 4:5] = mt[:, j:j + 1]
    met()
    units, part = gather_list(wa, wd, loads)
    g = Gather(p, units, gss, grs, LEAD)
    P = Plan()
    out_of = lambda nm: pltpu.make_async_copy(sc[nm], spill[nm], ssem.at[SPILL.index(nm)])
    back_to = lambda nm: pltpu.make_async_copy(spill[nm], sc[nm], ssem.at[SPILL.index(nm)])
    act_out = pltpu.make_async_copy(n.x, act, iosem.at[0])
    ig_out = pltpu.make_async_copy(n.acc, ig, iosem.at[1])

    class Do(Work):
        params = P.op(sm.start, sm.build, dict(y=40e3), (), cost=1.0, rank=-1)
        sums = P.mark()
        @staticmethod
        def reuse(l, *nms):
            for m in nms if l == 1 else (): out_of(m).wait()
        @staticmethod
        def keep(l, *nms):
            for m in nms if l == 0 else (): out_of(m).start()
        @staticmethod
        def need(l, *nms):
            for m in nms if l == 0 else (): back_to(m).wait()
        @staticmethod
        def done(l, *nms):
            for m in nms if l == 1 else (): back_to(m).start()
        @staticmethod
        def embed():
            tok_in.wait(); cot_in.wait()
            n.S[...] = jnp.zeros(SMALL, F32)
            def body(q):
                m = n.rs[q, 4:5]
                n.x[q, :] = n.o[q, :].astype(F32) * (1.0 - m) + m * row(n.V, R_EMBED)
            rows_loop(64, body)
        @staticmethod
        def send():
            act_out.start()
        @staticmethod
        def turn():
            act_out.wait()
            n.x[...] = n.du[...].astype(F32)
        @staticmethod
        def mid_norm(l):
            n.S[pl.ds(r_bias(l, 3), 1), :] = n.norm_back(l, 1, n.acc, n.xh2, n.du)
        @staticmethod
        def last():
            n.hidden_bias()
            def body(j, c):
                q = pl.ds(pl.multiple_of(j * 64, 64), 64)
                m, e = n.rs[q, 4:5], n.x[q, :]
                n.acc[q, :] = e * (1.0 - m)
                return c + jnp.sum(e * m, axis=0, keepdims=True)
            n.S[pl.ds(R_EMBED, 1), :] = lax.fori_loop(0, ROWS // 64, body, jnp.zeros((1, WIDTH), F32))
            ig_out.start()

    make_plan(P, n, g, part, r, sm, Do)
    P.run()
    sm.own()
    s_out = pltpu.make_async_copy(sbufs["own"], so, iosem.at[2])
    s_out.start()
    r.finish()
    ig_out.wait()
    s_out.wait()


def make_plan(P, n, g, part, r, sm, do):
    lasts = g.plan(P)
    marks = {}
    order = []
    for l, k, q, a, h in reduce_list():
        m = P.mark()
        marks.setdefault((l, k, q), []).append(m)
        order.append(m)
    lst = reduce_list()
    early = [u for u, v in enumerate(lst) if v[:2] == (1, "D") and v[2] < SOON]
    ends = r.plan(P, order, [early if v[0] == 0 else () for v in lst])
    gone = {}
    for (l, k, q, a, h), e in zip(reduce_list(), ends):
        gone.setdefault((l, k, q), []).append(e)
    sm.plan(P, do.sums)
    steps(P, n, lambda l, k: lasts[part[11 * l + k]], lambda l, k, q: marks[(l, k, q)], lambda l, k, q: gone[(l, k, q)], do)


def whole(tok, cot, msk, gains, biases, embed, fcb, ai, ao, fi, fo):
    net = net_scratch()
    any_, vm = pl.BlockSpec(memory_space=pl.ANY), pl.BlockSpec(memory_space=pltpu.VMEM)
    sa, sd = (2, 8, 4, 2, 96, 768), (2, 3, 4, 2, 128, 768)
    fa, fd = (8, 96, 768), (3, 128, 768)
    shapes = [((512, 768), F32), ((512, 768), F32), ((32, 128), F32), (ai.shape, BF), (ao.shape, BF), (fi.shape, BF), (fo.shape, BF)]
    shapes += [(net[k].shape, net[k].dtype) for k in SPILL]
    dma = pltpu.SemaphoreType.DMA
    parts, red = 22 + sum((96 if u % 11 < 8 else 128) // h - 1 for u, h in EARLY.items()), reduce_list()
    R = max(v[4] for v in red) // 2
    return pl.pallas_call(
        whole_kernel,
        out_shape=[jax.ShapeDtypeStruct(*v) for v in shapes],
        in_specs=[any_, any_, vm, vm, vm, vm, vm] + [any_] * 4,
        out_specs=[any_] * len(shapes),
        scratch_shapes=[
            net, pltpu.VMEM(sa, BF), pltpu.VMEM(sd, BF), pltpu.VMEM((SOON,) + sd[2:], BF), pltpu.VMEM(fa, BF), pltpu.VMEM(fd, BF),
            reduce_scratch(len(red), R), smalls_scratch(), dma((22,)), dma((8,)), dma((3,)),
            dma((parts, 14)), dma((parts, 14)), dma((len(red), 10)), dma((len(red), 10)),
        ],
        compiler_params=pltpu.CompilerParams(collective_id=0, has_side_effects=True, vmem_limit_bytes=VMEM_LIMIT),
    )(tok, cot, msk, gains, biases, embed, fcb, ai, ao, fi, fo)[:7]


def results_kernel(act_i, ig_i, own, g0, g1, g2, g3, act, ig, embed, o0, o1, o2, o3, gains, biases, fcb, narrow, full, rows, isem, osem):
    grads, outs = (g0, g1, g2, g3), (o0, o1, o2, o3)
    loads = [pltpu.make_async_copy(g, b, isem.at[i]) for i, (g, b) in enumerate(zip(grads, narrow))]
    stores = [pltpu.make_async_copy(b, o, osem.at[i]) for i, (b, o) in enumerate(zip(full, outs))]
    loads += [pltpu.make_async_copy(v, rows.at[i], isem.at[4 + i]) for i, v in enumerate((act_i, ig_i))]
    stores += [pltpu.make_async_copy(rows.at[i], v, osem.at[4 + i]) for i, v in enumerate((act, ig))]
    for c in loads:
        c.start()
    for l in range(2):
        gains[l] = own[2 * l:2 * l + 2, 0:96]
        for i in range(6):
            biases[i, l:l + 1, :] = own[4 + 6 * l + i:5 + 6 * l + i, 0:96]
        for i in range(3):
            fcb[l:l + 1, 128 * i:128 * i + 128] = own[24 + 3 * l + i:25 + 3 * l + i, :]
    embed[...] = own[16:17, 0:96]
    for i in range(4):
        loads[i].wait()
        full[i][...] = narrow[i][...].astype(F32)
        stores[i].start()
    for i in (4, 5):
        loads[i].wait()
        stores[i].start()
    for c in stores:
        c.wait()


def results(act, ig, own, *grads):
    any_, vm = pl.BlockSpec(memory_space=pl.ANY), pl.BlockSpec(memory_space=pltpu.VMEM)
    f = lambda *s: jax.ShapeDtypeStruct(s, F32)
    return pl.pallas_call(
        results_kernel,
        out_shape=[f(*act.shape), f(*ig.shape), f(1, 96)] + [f(*g.shape) for g in grads] + [f(2, 2, 96), f(6, 2, 96), f(2, 384)],
        in_specs=[any_, any_, vm] + [any_] * 4,
        out_specs=[any_, any_, vm] + [any_] * 4 + [vm] * 3,
        scratch_shapes=[
            [pltpu.VMEM(g.shape, BF) for g in grads], [pltpu.VMEM(g.shape, F32) for g in grads],
            pltpu.VMEM((2,) + act.shape, F32), pltpu.SemaphoreType.DMA((6,)), pltpu.SemaphoreType.DMA((6,)),
        ],
        compiler_params=pltpu.CompilerParams(vmem_limit_bytes=VMEM_LIMIT),
    )(act, ig, own, *grads)


def fused_local(tokens, mask, cotangent, mask_embed, attn_in, attn_out, fc_in, fc_out, gains, biases, fc_bias):
    out = list(results(*whole(
        tokens, cotangent, mask.reshape(4, 128), gains, biases.transpose(1, 0, 2), mask_embed.reshape(1, 96), fc_bias, attn_in, attn_out, fc_in, fc_out)))
    out[2] = out[2].reshape(96)
    out[8] = out[8].transpose(1, 0, 2)
    return tuple(out)


def solution(mesh):
    if dict(mesh.shape) != {"dp": 4, "fsdp": 8}:
        return generic_solution(mesh)
    rows = P(("dp", "fsdp"), None)
    mat = P(None, "fsdp", None)
    vec = P(None, None, "fsdp")
    return jax.shard_map(
        fused_local, mesh=mesh,
        in_specs=(rows, P(("dp", "fsdp")), rows, P("fsdp"), mat, mat, mat, mat, vec, vec, P(None, "fsdp")),
        out_specs=(rows, rows, P("fsdp"), mat, mat, mat, mat, vec, vec, P(None, "fsdp")),
        check_vma=False)


HEADS = 12
SEQ = 512
LAYERS = 2


eps = 1e-06


def norm_rows(values, gain, bias):
    center = values - jnp.mean(values, axis=-1, keepdims=True)
    spread = jnp.mean(center * center, axis=-1, keepdims=True)
    return center * lax.rsqrt(spread + eps) * gain + bias


def gelu_exact(values):
    return jax.nn.gelu(values, approximate=False)


def split_heads(values, clips):
    width = values.shape[1]
    return values.reshape(clips, SEQ, HEADS, width // HEADS)


def attend(pack):
    query, key_rows, value = pack
    scale = query.shape[-1] ** (-0.5)
    scores = jnp.einsum("qhd,khd->hqk", query, key_rows, preferred_element_type=jnp.float32) * scale
    top = jnp.max(scores, axis=-1, keepdims=True)
    expo = jnp.exp(scores - top)
    total = jnp.sum(expo, axis=-1, keepdims=True)
    probs = (expo / total).astype(jnp.bfloat16)
    mixed = jnp.einsum("hqk,khd->qhd", probs, value, preferred_element_type=jnp.float32)
    return (mixed, top + jnp.log(total))


def attend_back(pack):
    query, key_rows, value, logsum, d_mixed = pack
    scale = query.shape[-1] ** (-0.5)
    scores = jnp.einsum("qhd,khd->hqk", query, key_rows, preferred_element_type=jnp.float32) * scale
    probs = jnp.exp(scores - logsum)
    d_probs = jnp.einsum("qhd,khd->hqk", d_mixed, value, preferred_element_type=jnp.float32)
    d_value = jnp.einsum(
        "hqk,qhd->khd", probs.astype(jnp.bfloat16), d_mixed, preferred_element_type=jnp.float32
    )
    d_scores = probs * (d_probs - jnp.sum(probs * d_probs, axis=-1, keepdims=True))
    d_scaled = d_scores.astype(jnp.bfloat16) * scale
    d_query = jnp.einsum("hqk,khd->qhd", d_scaled, key_rows, preferred_element_type=jnp.float32)
    d_key = jnp.einsum("hqk,qhd->khd", d_scaled, query, preferred_element_type=jnp.float32)
    return (d_query, d_key, d_value)


def layer_forward(state, weights):
    w_qkv, w_out, w_in, w_down, gain, bias, fcb = weights
    rows, width = state.shape
    clips = rows // SEQ
    normed = norm_rows(state, gain[0].astype(jnp.float32), bias[0].astype(jnp.float32)).astype(
        jnp.bfloat16
    )
    qkv_bias = jnp.concatenate([bias[1], jnp.zeros_like(bias[1]), bias[2]]).astype(jnp.float32)
    joined = (jnp.dot(normed, w_qkv, preferred_element_type=jnp.float32) + qkv_bias).astype(
        jnp.bfloat16
    )
    query = split_heads(joined[:, :width], clips)
    key_rows = split_heads(joined[:, width : 2 * width], clips)
    value = split_heads(joined[:, 2 * width :], clips)
    mixed, logsum = lax.map(attend, (query, key_rows, value))
    mixed = mixed.reshape(rows, width).astype(jnp.bfloat16)
    middle = (
        state
        + jnp.dot(mixed, w_out, preferred_element_type=jnp.float32)
        + bias[3].astype(jnp.float32)
    )
    normed_two = norm_rows(middle, gain[1].astype(jnp.float32), bias[4].astype(jnp.float32)).astype(
        jnp.bfloat16
    )
    hidden = jnp.dot(normed_two, w_in, preferred_element_type=jnp.float32) + fcb.astype(jnp.float32)
    activated = gelu_exact(hidden).astype(jnp.bfloat16)
    return (normed, query, key_rows, value, logsum, mixed, middle, normed_two, hidden, activated)


def layer_finish(saved, weights):
    middle = saved[6]
    activated = saved[9]
    return (
        middle
        + jnp.dot(activated, weights[3], preferred_element_type=jnp.float32)
        + weights[5][5].astype(jnp.float32)
    )


def layer_backward(state, weights, grad):
    w_qkv, w_out, w_in, w_down, gain, bias, fcb = weights
    rows, width = state.shape
    clips = rows // SEQ
    normed, query, key_rows, value, logsum, mixed, middle, normed_two, hidden, activated = (
        layer_forward(state, weights)
    )
    d_up = grad.astype(jnp.bfloat16)
    g_down = jnp.einsum("tf,td->fd", activated, d_up, preferred_element_type=jnp.float32)
    d_two = jnp.sum(d_up.astype(jnp.float32), axis=0)
    d_act = jnp.einsum("td,fd->tf", d_up, w_down, preferred_element_type=jnp.float32)
    d_hidden = jax.vjp(gelu_exact, hidden)[1](d_act)[0].astype(jnp.bfloat16)
    g_in = jnp.einsum("td,tf->df", normed_two, d_hidden, preferred_element_type=jnp.float32)
    d_one = jnp.sum(d_hidden.astype(jnp.float32), axis=0)
    d_normed_two = jnp.einsum("tf,df->td", d_hidden, w_in, preferred_element_type=jnp.float32)
    back_two = jax.vjp(norm_rows, middle, gain[1].astype(jnp.float32), bias[4].astype(jnp.float32))[
        1
    ]
    d_middle, d_gain_two, d_bias_two = back_two(d_normed_two)
    d_middle = grad + d_middle
    d_branch = d_middle.astype(jnp.bfloat16)
    g_out = jnp.einsum("td,te->de", mixed, d_branch, preferred_element_type=jnp.float32)
    d_outb = jnp.sum(d_branch.astype(jnp.float32), axis=0)
    d_mixed = jnp.einsum("te,de->td", d_branch, w_out, preferred_element_type=jnp.float32).astype(
        jnp.bfloat16
    )
    d_query, d_key, d_value = lax.map(
        attend_back, (query, key_rows, value, logsum, split_heads(d_mixed, clips))
    )
    d_joined = jnp.concatenate(
        [d_query.reshape(rows, width), d_key.reshape(rows, width), d_value.reshape(rows, width)],
        axis=1,
    ).astype(jnp.bfloat16)
    g_qkv = jnp.einsum("td,te->de", normed, d_joined, preferred_element_type=jnp.float32)
    d_sums = jnp.sum(d_joined.astype(jnp.float32), axis=0)
    d_normed = jnp.einsum("te,de->td", d_joined, w_qkv, preferred_element_type=jnp.float32)
    back_one = jax.vjp(norm_rows, state, gain[0].astype(jnp.float32), bias[0].astype(jnp.float32))[
        1
    ]
    d_state, d_gain_one, d_bias_one = back_one(d_normed)
    gain_terms = jnp.stack([d_gain_one, d_gain_two])
    bias_terms = jnp.stack(
        [d_bias_one, d_sums[:width], d_sums[2 * width :], d_outb, d_bias_two, d_two]
    )
    return (d_middle + d_state, (g_qkv, g_out, g_in, g_down, gain_terms, bias_terms, d_one))


def local(
    tokens, mask, cotangent, mask_embed, attn_in, attn_out, fc_in, fc_out, gains, biases, fc_bias
):
    mask_f = mask.astype(jnp.float32)[:, None]
    state = tokens.astype(jnp.float32)
    stored = []
    kept = []
    for layer in range(LAYERS):
        fetched = (
            lax.all_gather(attn_in[layer], "fsdp", axis=0, tiled=True),
            lax.all_gather(attn_out[layer], "fsdp", axis=0, tiled=True),
            lax.all_gather(fc_in[layer], "fsdp", axis=0, tiled=True),
            lax.all_gather(fc_out[layer], "fsdp", axis=0, tiled=True),
            lax.all_gather(gains[layer], "fsdp", axis=1, tiled=True),
            lax.all_gather(biases[layer], "fsdp", axis=1, tiled=True),
            lax.all_gather(fc_bias[layer], "fsdp", axis=0, tiled=True),
            lax.all_gather(mask_embed, "fsdp", axis=0, tiled=True),
        )
        if layer == 0:
            state = state * (1.0 - mask_f) + mask_f * fetched[7].astype(jnp.float32)
        stored.append(state)
        weights = tuple(fetched[:7])
        kept.append(weights)
        state = layer_finish(layer_forward(state, weights), weights)
    grad = cotangent.astype(jnp.float32)
    layer_grads = [None] * LAYERS
    for layer in reversed(range(LAYERS)):
        weights = tuple(
            (
                lax.all_gather(attn_in[layer], "fsdp", axis=0, tiled=True),
                lax.all_gather(attn_out[layer], "fsdp", axis=0, tiled=True),
                lax.all_gather(fc_in[layer], "fsdp", axis=0, tiled=True),
                lax.all_gather(fc_out[layer], "fsdp", axis=0, tiled=True),
                lax.all_gather(gains[layer], "fsdp", axis=1, tiled=True),
                lax.all_gather(biases[layer], "fsdp", axis=1, tiled=True),
                lax.all_gather(fc_bias[layer], "fsdp", axis=0, tiled=True),
            )
        )
        grad, terms = layer_backward(stored[layer], weights, grad)
        if layer == 0:
            mask_term = jnp.sum(grad * mask_f, axis=0)
        else:
            mask_term = jnp.zeros((grad.shape[1],), jnp.float32)
        shares = (
            lax.psum_scatter(terms[0], "fsdp", scatter_dimension=0, tiled=True),
            lax.psum_scatter(terms[1], "fsdp", scatter_dimension=0, tiled=True),
            lax.psum_scatter(terms[2], "fsdp", scatter_dimension=0, tiled=True),
            lax.psum_scatter(terms[3], "fsdp", scatter_dimension=0, tiled=True),
            lax.psum_scatter(terms[4], "fsdp", scatter_dimension=1, tiled=True),
            lax.psum_scatter(terms[5], "fsdp", scatter_dimension=1, tiled=True),
            lax.psum_scatter(terms[6], "fsdp", scatter_dimension=0, tiled=True),
            lax.psum_scatter(mask_term, "fsdp", scatter_dimension=0, tiled=True),
        )
        slices = (
            lax.psum_scatter(
                shares[0].astype(jnp.bfloat16), "dp", scatter_dimension=1, tiled=True
            ).astype(jnp.float32),
            lax.psum_scatter(
                shares[1].astype(jnp.bfloat16), "dp", scatter_dimension=1, tiled=True
            ).astype(jnp.float32),
            lax.psum_scatter(
                shares[2].astype(jnp.bfloat16), "dp", scatter_dimension=1, tiled=True
            ).astype(jnp.float32),
            lax.psum_scatter(
                shares[3].astype(jnp.bfloat16), "dp", scatter_dimension=1, tiled=True
            ).astype(jnp.float32),
        )
        matrices = (
            lax.all_gather(slices[0].astype(jnp.bfloat16), "dp", axis=1, tiled=True).astype(
                jnp.float32
            ),
            lax.all_gather(slices[1].astype(jnp.bfloat16), "dp", axis=1, tiled=True).astype(
                jnp.float32
            ),
            lax.all_gather(slices[2].astype(jnp.bfloat16), "dp", axis=1, tiled=True).astype(
                jnp.float32
            ),
            lax.all_gather(slices[3].astype(jnp.bfloat16), "dp", axis=1, tiled=True).astype(
                jnp.float32
            ),
        )
        smalls = lax.psum((shares[4], shares[5], shares[6], shares[7]), "dp")
        layer_grads[layer] = (
            matrices[0],
            matrices[1],
            matrices[2],
            matrices[3],
            smalls[0],
            smalls[1],
            smalls[2],
            smalls[3],
        )
    input_grad = grad * (1.0 - mask_f)
    stacked = [jnp.stack([layer_grads[lay][item] for lay in range(LAYERS)]) for item in range(7)]
    results = tuple(stacked) + (layer_grads[0][7],)
    return (
        state,
        input_grad,
        results[7],
        results[0],
        results[1],
        results[2],
        results[3],
        results[4],
        results[5],
        results[6],
    )


def generic_solution(mesh):
    placed = (
        P(("dp", "fsdp"), None),
        P(("dp", "fsdp")),
        P(("dp", "fsdp"), None),
        P("fsdp"),
        P(None, "fsdp", None),
        P(None, "fsdp", None),
        P(None, "fsdp", None),
        P(None, "fsdp", None),
        P(None, None, "fsdp"),
        P(None, None, "fsdp"),
        P(None, "fsdp"),
    )
    return jax.shard_map(
        local,
        mesh=mesh,
        in_specs=placed,
        out_specs=(
            P(("dp", "fsdp"), None),
            P(("dp", "fsdp"), None),
            P("fsdp"),
            P(None, "fsdp", None),
            P(None, "fsdp", None),
            P(None, "fsdp", None),
            P(None, "fsdp", None),
            P(None, None, "fsdp"),
            P(None, None, "fsdp"),
            P(None, "fsdp"),
        ),
        check_vma=False,
    )
```
